32 devices in a mesh: dp: 8 (over z, y), mp: 4 (over x, core).
Axes of the slice: x: 2, y: 2, z: 4, core: 2. Of those that a mesh axis runs over, the one named last changes fastest.
Arguments:
- patches: bfloat16 [16, 64, 32, 512], P('mp', 'dp'), may hold values from -6 to 6
- cotangent: float32 [16, 64, 32, 512], P('mp', 'dp'), may hold values from -40 to 40
- grid_shape: int32 [64, 2], P('dp'), may hold values from 8 to 32, as said below
- qkv_weight: float32 [512, 3, 512], P('dp', None, 'mp'), may hold values from -0.25 to 0.25
- qkv_mean: float32 [512, 3, 512], P('dp', None, 'mp'), may hold values from -0.0009765625 to 0.0009765625
- qkv_square: float32 [512, 3, 512], P('dp', None, 'mp'), may hold values from 3.142093e-10 to 1.2568372e-09
- proj_weight: float32 [512, 512], P('dp', 'mp'), may hold values from -0.25 to 0.25
- proj_mean: float32 [512, 512], P('dp', 'mp'), may hold values from -0.0009765625 to 0.0009765625
- proj_square: float32 [512, 512], P('dp', 'mp'), may hold values from 3.142093e-10 to 1.2568372e-09
- expand_weight: float32 [512, 2048], P('dp', 'mp'), may hold values from -3 to 3
- expand_mean: float32 [512, 2048], P('dp', 'mp'), may hold values from -0.0004272461 to 0.0004272461
- expand_square: float32 [512, 2048], P('dp', 'mp'), may hold values from 7.8552324e-11 to 3.142093e-10
- contract_weight: float32 [512, 2048], P('dp', 'mp'), may hold values from -0.125 to 0.125
- contract_mean: float32 [512, 2048], P('dp', 'mp'), may hold values from -0.0009765625 to 0.0009765625
- contract_square: float32 [512, 2048], P('dp', 'mp'), may hold values from 3.142093e-10 to 1.2568372e-09
- small_params: float32 [72, 512], replicated, may hold values from -4 to 7
- small_mean: float32 [72, 512], replicated, may hold values from -0.0029296875 to 0.0029296875
- small_square: float32 [72, 512], replicated, may hold values from 2.8278837e-09 to 1.1311535e-08
Outputs:
- block_out: bfloat16 [16, 64, 32, 512], P('mp', 'dp')
- patch_grad: float32 [16, 64, 32, 512], P('mp', 'dp')
- grad_norm: float32 [], replicated
- qkv_updated: float32 [512, 3, 512], P('dp', None, 'mp')
- qkv_moment: float32 [512, 3, 512], P('dp', None, 'mp')
- qkv_variance: float32 [512, 3, 512], P('dp', None, 'mp')
- proj_updated: float32 [512, 512], P('dp', 'mp')
- proj_moment: float32 [512, 512], P('dp', 'mp')
- proj_variance: float32 [512, 512], P('dp', 'mp')
- expand_updated: float32 [512, 2048], P('dp', 'mp')
- expand_moment: float32 [512, 2048], P('dp', 'mp')
- expand_variance: float32 [512, 2048], P('dp', 'mp')
- contract_updated: float32 [512, 2048], P('dp', 'mp')
- contract_moment: float32 [512, 2048], P('dp', 'mp')
- contract_variance: float32 [512, 2048], P('dp', 'mp')
- small_updated: float32 [72, 512], replicated
- small_moment: float32 [72, 512], replicated
- small_variance: float32 [72, 512], replicated
The draws below stay inside these ranges and needn't reach their ends.
Inputs may be any that keep to these rules, and one draw needn't show every extreme that they name: `grid_shape`: row i holds the height and width of image i's patch grid, placed at the canvas's top left; every aligned block of 8 images holds one image that fills the whole 16 x 32 canvas.
All inputs are finite; a program needn't handle non-finite values.
Results may differ from the reference program's by a relative error of at most 0.022.
Values may be sent and summed in bfloat16 or wider, within the bound.
No kernel may reach another device: no remote copies, remote signals or barrier semaphores. Data moves between devices by JAX's collectives and lax.ppermute only.
A program may use at most 192 MiB of HBM per device.

```python
import math
import jax
import jax.numpy as jnp
from jax import lax

D = 512
HD = 64
FF = 2048
GH = 16
GW = 32
IMG_DEV = 8
STEP = 10
IMAGES = 64
NPACK = 72


def draw_grid_shape(key, part):
    key = jax.random.fold_in(key, 11)
    key_heights, key_widths, key_full = jax.random.split(key, 3)
    heights = jax.random.randint(key_heights, (IMAGES,), GH // 2, GH + 1)
    widths = jax.random.randint(key_widths, (IMAGES,), GW // 2, GW + 1)
    block_count = IMAGES // IMG_DEV
    chosen = jax.random.randint(key_full, (block_count, 1), 0, IMG_DEV)
    filled = (jnp.arange(IMG_DEV)[None, :] == chosen).reshape(IMAGES)
    heights = jnp.where(filled, GH, heights)
    widths = jnp.where(filled, GW, widths)
    return jnp.stack([heights, widths], axis=1).astype(jnp.int32)


def draw_cotangent(key, part):
    key = jax.random.fold_in(key, 12)
    position = jnp.arange(D, dtype=jnp.float32) / D
    base = jax.random.normal(key, (GH, IMAGES, GW, D), jnp.float32)
    rising = 3.0 ** position
    return (base * rising).astype(jnp.float32)


def draw_expand_weight(key, part):
    key = jax.random.fold_in(key, 13)
    position = jnp.arange(FF, dtype=jnp.float32) / FF
    base = jax.random.normal(key, (D, FF), jnp.float32)
    rising = 3.0 ** position
    return (base * rising[None, :] * D ** (-0.5)).astype(jnp.float32)


def draw_small_params(key, part):
    key = jax.random.fold_in(key, 14)
    key_base, key_gain = jax.random.split(key)
    position = jnp.arange(D, dtype=jnp.float32) / D
    base = jax.random.normal(key_base, (NPACK, D), jnp.float32)
    rising = 3.0 ** position
    row_index = jnp.arange(NPACK)[:, None]
    gains = rising[None, :] * jax.random.uniform(key_gain, (NPACK, D), jnp.float32, 0.7, 1.3)
    scales = jnp.where(row_index < 9, 0.3, jnp.where(row_index < 58, 0.06, 0.5))
    is_gain = (row_index == 59) | (row_index == 65)
    return jnp.where(is_gain, gains, base * scales).astype(jnp.float32)


def levels(rng, extent, cuts, least, high):
    level = 1.0
    for dim, shards_of in cuts:
        steps = jax.random.uniform(jax.random.fold_in(jax.random.fold_in(rng, 6), dim), (shards_of,), jnp.float32, least / len(cuts), high / len(cuts))
        level = level * jnp.repeat(jnp.exp(steps), extent[dim] // shards_of).reshape((-1,) + (1,) * (len(extent) - 1 - dim))
    return level


def normal_values(stream_key, extent, deviation, reach, cuts=(), kind=jnp.bfloat16):
    factor_of = levels(stream_key, extent, cuts, -0.22, 0.18) if cuts else 1.0
    drawn = jax.random.normal(stream_key, extent, jnp.float32) * deviation * factor_of
    return jnp.minimum(jnp.maximum(drawn, -reach), reach).astype(kind)


def setup_inputs(seed: int = 0) -> dict:
    key_list = jax.random.split(jax.random.key(seed), 19)
    return {
        "patches": normal_values(key_list[0], (GH, IMAGES, GW, D), 1.0, 6.0, ((0, 4), (1, 8))),
        "cotangent": draw_cotangent(jax.random.fold_in(key_list[18], 71), 0),
        "grid_shape": draw_grid_shape(jax.random.fold_in(key_list[18], 71), 0),
        "qkv_weight": normal_values(key_list[3], (D, 3, D), D ** -0.5, 0.25, ((0, 8), (2, 4)), jnp.float32),
        "qkv_mean": normal_values(key_list[4], (D, 3, D), (0.11 / (4 * D * D + 2 * D * FF + NPACK * D) ** 0.5), 0.0009765625, ((0, 8), (2, 4)), jnp.float32),
        "qkv_square": jnp.clip(jnp.exp(math.log(1.2568371898780129e-09) - 1.3862944 * jax.random.uniform(key_list[5], (D, 3, D), jnp.float32) ** levels(key_list[5], (D, 3, D), ((0, 8), (2, 4)), -0.2, 0.2)), 3.142092974695032e-10, 1.2568371898780129e-09),
        "proj_weight": normal_values(key_list[6], (D, D), D ** -0.5, 0.25, ((0, 8), (1, 4)), jnp.float32),
        "proj_mean": normal_values(key_list[7], (D, D), (0.11 / (4 * D * D + 2 * D * FF + NPACK * D) ** 0.5), 0.0009765625, ((0, 8), (1, 4)), jnp.float32),
        "proj_square": jnp.clip(jnp.exp(math.log(1.2568371898780129e-09) - 1.3862944 * jax.random.uniform(key_list[8], (D, D), jnp.float32) ** levels(key_list[8], (D, D), ((0, 8), (1, 4)), -0.2, 0.2)), 3.142092974695032e-10, 1.2568371898780129e-09),
        "expand_weight": draw_expand_weight(jax.random.fold_in(key_list[18], 71), 0),
        "expand_mean": normal_values(key_list[10], (D, FF), (0.05 / (4 * D * D + 2 * D * FF + NPACK * D) ** 0.5), 0.0004272461, ((0, 8), (1, 4)), jnp.float32),
        "expand_square": jnp.clip(jnp.exp(math.log(3.142092974695032e-10) - 1.3862944 * jax.random.uniform(key_list[11], (D, FF), jnp.float32) ** levels(key_list[11], (D, FF), ((0, 8), (1, 4)), -0.2, 0.2)), 7.85523243673758e-11, 3.142092974695032e-10),
        "contract_weight": normal_values(key_list[12], (D, FF), FF ** -0.5, 0.125, ((0, 8), (1, 4)), jnp.float32),
        "contract_mean": normal_values(key_list[13], (D, FF), (0.11 / (4 * D * D + 2 * D * FF + NPACK * D) ** 0.5), 0.0009765625, ((0, 8), (1, 4)), jnp.float32),
        "contract_square": jnp.clip(jnp.exp(math.log(1.2568371898780129e-09) - 1.3862944 * jax.random.uniform(key_list[14], (D, FF), jnp.float32) ** levels(key_list[14], (D, FF), ((0, 8), (1, 4)), -0.2, 0.2)), 3.142092974695032e-10, 1.2568371898780129e-09),
        "small_params": draw_small_params(jax.random.fold_in(key_list[18], 71), 0),
        "small_mean": normal_values(key_list[16], (NPACK, D), (0.33 / (4 * D * D + 2 * D * FF + NPACK * D) ** 0.5), 0.0029296875, (), jnp.float32),
        "small_square": jnp.clip(jnp.exp(jax.random.uniform(key_list[17], (NPACK, D), jnp.float32, math.log(2.8278837049811045e-09), math.log(1.1311534819924418e-08))), 2.8278837049811045e-09, 1.1311534819924418e-08),
    }


@jax.custom_vjp
def low(v):
    return lax.optimization_barrier(v.astype(jnp.bfloat16)).astype(jnp.float32)

@jax.custom_vjp
def low_back(v):
    return v

def low_keep(v):
    return (low(v), None)

def low_pass(kept, grad):
    return (grad,)

def back_keep(v):
    return (v, None)

def back_low(kept, grad):
    return (low(grad),)
low.defvjp(low_keep, low_pass)
low_back.defvjp(back_keep, back_low)
NORM_EPS = 1e-06
CLIP_NORM = 1.0
BETA_ONE = 0.9
BETA_TWO = 0.999
ADAM_EPS = 1e-08
WEIGHT_DECAY = 0.05
RATE_FACTOR = 2.0
SMALL_RATE = 0.5
HIGHEST = lax.Precision.HIGHEST

def canvas_mask(grid_shape, first_row, row_count, col_count):
    row_index = first_row + jnp.arange(row_count, dtype=jnp.int32)
    col_index = jnp.arange(col_count, dtype=jnp.int32)
    inside_rows = row_index[:, None, None] < grid_shape[:, 0][None, :, None]
    inside_cols = col_index[None, None, :] < grid_shape[:, 1][None, :, None]
    return (inside_rows & inside_cols).astype(jnp.float32)

def window_mask(first_chan, chan_count):
    head_index = (first_chan + jnp.arange(chan_count, dtype=jnp.int32)) // HD
    radius = jnp.where(head_index < 2, 1, jnp.where(head_index < 5, 2, 3))
    tap_list = jnp.arange(49, dtype=jnp.int32)
    tap_row = jnp.abs(tap_list // 7 - 3)
    tap_col = jnp.abs(tap_list % 7 - 3)
    inside = (tap_row[:, None] <= radius[None, :]) & (tap_col[:, None] <= radius[None, :])
    return inside.astype(jnp.float32)

def depthwise(padded, kernel, reach_cells):
    tap_side = 2 * reach_cells + 1
    row_count = padded.shape[0] - 2 * reach_cells
    col_count = padded.shape[2] - 2 * reach_cells
    result = None
    for tap_index in range(tap_side * tap_side):
        tap_row = tap_index // tap_side
        tap_col = tap_index % tap_side
        term = kernel[tap_index] * padded[tap_row:tap_row + row_count, :, tap_col:tap_col + col_count, :]
        result = term if result is None else result + term
    return result

def layer_norm(values, gain_row, shift_row):
    center = values - lax.optimization_barrier(jnp.mean(values, axis=-1, keepdims=True))
    spread = lax.optimization_barrier(jnp.mean(center * center, axis=-1, keepdims=True))
    return center * lax.rsqrt(spread + NORM_EPS) * gain_row + shift_row

def block(inputs, mask, qkv_used, proj_used, expand_used, contract_used, small_used):
    row_count, image_count, col_count, channels = inputs.shape
    head_count = channels // HD
    keep = mask[..., None]
    masked_in = inputs * keep
    in_pad = jnp.pad(masked_in, ((1, 1), (0, 0), (1, 1), (0, 0)))
    first_sum = masked_in + depthwise(in_pad, small_used[0:9], 1) + small_used[58]
    normed_attn = low(layer_norm(first_sum, small_used[59], small_used[60]))
    projected = jnp.einsum('yixd,dke->yixke', normed_attn, qkv_used, precision=HIGHEST)
    query = low(low_back(projected[..., 0, :] + small_used[61]))
    key_raw = low_back(projected[..., 1, :])
    value = low(low_back(projected[..., 2, :] + small_used[62]))
    key_masked = jnp.where(keep > 0, key_raw, -1e+30)
    key_top = lax.optimization_barrier(jnp.max(key_masked, axis=(0, 2), keepdims=True))
    expo = jnp.exp(key_masked - key_top)
    probs = low(expo / lax.optimization_barrier(jnp.sum(expo, axis=(0, 2), keepdims=True)))
    split = (row_count, image_count, col_count, head_count, HD)
    key_value = low(low_back(jnp.einsum('yixha,yixhb->ihab', probs.reshape(split), value.reshape(split), precision=HIGHEST)))
    factored = HD ** (-0.5) * jnp.einsum('yixha,ihab->yixhb', query.reshape(split), key_value, precision=HIGHEST)
    value_pad = jnp.pad(value * keep, ((3, 3), (0, 0), (3, 3), (0, 0)))
    near = depthwise(value_pad, small_used[9:58] * window_mask(0, channels), 3) + small_used[63]
    attended = low(low_back(factored.reshape(query.shape) + query * near))
    attn_out = low_back(jnp.einsum('yixe,de->yixd', attended, proj_used, precision=HIGHEST) + small_used[64])
    second_sum = first_sum + attn_out
    normed_mlp = low(layer_norm(second_sum, small_used[65], small_used[66]))
    hidden_pre = low_back(jnp.einsum('yixd,df->yixf', normed_mlp, expand_used, precision=HIGHEST) + small_used[68:].reshape(-1))
    hidden_act = low(jax.nn.gelu(hidden_pre, approximate=False))
    mlp_out = low_back(jnp.einsum('yixf,df->yixd', hidden_act, contract_used, precision=HIGHEST) + small_used[67])
    return second_sum + mlp_out

def to_low(weight):
    return lax.optimization_barrier(weight.astype(jnp.bfloat16)).astype(jnp.float32)

def adamw(weight, mean, square, gradient, factor, rate, decay):
    clipped = gradient * factor
    mean_new = BETA_ONE * mean + (1.0 - BETA_ONE) * clipped
    square_new = BETA_TWO * square + (1.0 - BETA_TWO) * clipped * clipped
    mean_hat = mean_new / (1.0 - BETA_ONE ** STEP)
    square_hat = square_new / (1.0 - BETA_TWO ** STEP)
    weight_new = weight - rate * (mean_hat / (jnp.sqrt(square_hat) + ADAM_EPS) + decay * weight)
    return (weight_new, mean_new, square_new)

def reference(patches, cotangent, grid_shape, qkv_weight, qkv_mean, qkv_square, proj_weight, proj_mean, proj_square, expand_weight, expand_mean, expand_square, contract_weight, contract_mean, contract_square, small_params, small_mean, small_square):
    qkv_low = to_low(qkv_weight)
    proj_low = to_low(proj_weight)
    expand_low = to_low(expand_weight)
    contract_low = to_low(contract_weight)
    group_count = IMAGES // IMG_DEV

    def regroup(values):
        shaped = values.reshape((GH, group_count, IMG_DEV) + values.shape[2:])
        return jnp.moveaxis(shaped, 1, 0)

    def ungroup(values):
        return jnp.moveaxis(values, 0, 1).reshape((GH, IMAGES) + values.shape[3:])
    grid_groups = grid_shape.reshape(group_count, IMG_DEV, 2)
    zero_init = (jnp.zeros(qkv_weight.shape, jnp.float32), jnp.zeros(proj_weight.shape, jnp.float32), jnp.zeros(expand_weight.shape, jnp.float32), jnp.zeros(contract_weight.shape, jnp.float32), jnp.zeros(small_params.shape, jnp.float32))

    def one_group(totals, item):
        group_in, group_cot, group_grid = item
        mask = canvas_mask(group_grid, 0, GH, GW)

        def forward(inputs, qkv_used, proj_used, expand_used, contract_used, small_used):
            return block(inputs, mask, qkv_used, proj_used, expand_used, contract_used, small_used)
        outputs, pullback = jax.vjp(forward, group_in.astype(jnp.float32), qkv_low, proj_low, expand_low, contract_low, small_params)
        grads = pullback(group_cot * mask[..., None])
        totals = tuple((accum + fresh for accum, fresh in zip(totals, grads[1:])))
        return (totals, (outputs.astype(jnp.bfloat16), grads[0]))
    totals, (outputs, input_grads) = lax.scan(one_group, zero_init, (regroup(patches), regroup(cotangent), grid_groups))
    grad_qkv, grad_proj, grad_expand, grad_contract, grad_small = totals
    total_sq = jnp.sum(grad_qkv * grad_qkv) + jnp.sum(grad_proj * grad_proj) + jnp.sum(grad_expand * grad_expand) + jnp.sum(grad_contract * grad_contract) + jnp.sum(grad_small * grad_small)
    grad_norm = jnp.sqrt(total_sq)
    factor = jnp.minimum(1.0, CLIP_NORM / (grad_norm + 1e-06))
    rate_model = RATE_FACTOR * D ** (-0.5)
    rate_hidden = RATE_FACTOR * FF ** (-0.5)
    qkv_new = adamw(qkv_weight, qkv_mean, qkv_square, grad_qkv, factor, rate_model, WEIGHT_DECAY)
    proj_new = adamw(proj_weight, proj_mean, proj_square, grad_proj, factor, rate_model, WEIGHT_DECAY)
    expand_new = adamw(expand_weight, expand_mean, expand_square, grad_expand, factor, rate_model, WEIGHT_DECAY)
    contract_new = adamw(contract_weight, contract_mean, contract_square, grad_contract, factor, rate_hidden, WEIGHT_DECAY)
    small_new = adamw(small_params, small_mean, small_square, grad_small, factor, SMALL_RATE, 0.0)
    return (ungroup(outputs), ungroup(input_grads), grad_norm, qkv_new[0], qkv_new[1], qkv_new[2], proj_new[0], proj_new[1], proj_new[2], expand_new[0], expand_new[1], expand_new[2], contract_new[0], contract_new[1], contract_new[2], small_new[0], small_new[1], small_new[2])
```

```python
import functools
import math

import jax
import jax.numpy as jnp
from jax import lax
from jax.experimental import pallas as pl
from jax.experimental.pallas import tpu as pltpu
from jax.sharding import PartitionSpec as P

D = 512
HD = 64
FF = 2048
STEP = 10


NORM_EPS = 1e-06
CLIP_NORM = 1.0
BETA_ONE = 0.9
BETA_TWO = 0.999
ADAM_EPS = 1e-08
WEIGHT_DECAY = 0.05
RATE_FACTOR = 2.0
SMALL_RATE = 0.5
ROOT_HALF = 0.7071067811865476
INV_ROOT_TAU = 0.3989422804014327
HEAD_SCALE = HD ** (-0.5)

LANES = 128
SUB = 8
VMEM_LIMIT = 60 * 1024 * 1024
F32 = jnp.float32
BF16 = jnp.bfloat16


def radius_of(head):
    return 1 if head < 2 else 2 if head < 5 else 3


def log2(size):
    bits = size.bit_length() - 1
    assert 1 << bits == size
    return bits


def flip(array, axis, bit):
    size = lax.axis_size(axis)
    return lax.ppermute(array, axis, [(i, i ^ (1 << bit)) for i in range(size)])


def bit_of(axis, bit):
    return (lax.axis_index(axis) >> bit) & 1


def gathered(array, axis):
    array = array[None]
    for bit in range(log2(lax.axis_size(axis))):
        other = flip(array, axis, bit)
        upper = bit_of(axis, bit) == 1
        array = jnp.where(
            upper,
            jnp.concatenate([other, array], axis=0),
            jnp.concatenate([array, other], axis=0),
        )
    return array


def halved(array, axis, dim):
    size = lax.axis_size(axis)
    bits = log2(size)
    before, after = array.shape[:dim], array.shape[dim + 1 :]
    array = array.reshape(*before, *([2] * bits), *after)
    for bit in range(bits):
        place = dim + bits - 1 - bit
        mine = lax.dynamic_index_in_dim(array, bit_of(axis, bit), place, keepdims=False)
        theirs = lax.dynamic_index_in_dim(array, 1 - bit_of(axis, bit), place, keepdims=False)
        got = flip(theirs, axis, bit)
        array = (mine.astype(F32) + got.astype(F32)).astype(array.dtype)
    return array


def to_images(cells):
    size = lax.axis_size("mp")
    rows, images, cols, channels = cells.shape
    tiles = cells.reshape(rows, size, images // size, cols, channels).transpose(1, 0, 2, 3, 4)
    tiles = lax.all_to_all(tiles, "mp", 0, 0, tiled=True)
    return tiles.transpose(2, 0, 1, 3, 4).reshape(images // size, size * rows, cols, channels)


def to_rows(cells):
    size = lax.axis_size("mp")
    images, rows, cols, channels = cells.shape
    tiles = cells.reshape(images, size, rows // size, cols, channels).transpose(1, 0, 2, 3, 4)
    tiles = lax.all_to_all(tiles, "mp", 0, 0, tiled=True)
    return tiles.transpose(2, 0, 1, 3, 4).reshape(rows // size, size * images, cols, channels)


def dot(a, b):
    return lax.dot_general(a, b, (((1,), (0,)), ((), ())), preferred_element_type=F32)


def dot_rt(a, b):
    return lax.dot_general(a, b, (((1,), (1,)), ((), ())), preferred_element_type=F32)


def dot_lt(a, b):
    return lax.dot_general(a, b, (((0,), (0,)), ((), ())), preferred_element_type=F32)


def row_mean(values):
    return jnp.sum(values, axis=-1, keepdims=True) * (1.0 / values.shape[-1])


def norm_parts(values):
    center = values - row_mean(values)
    rstd = lax.rsqrt(row_mean(center * center) + NORM_EPS)
    return center * rstd, rstd


def norm_back(gradient, normed, rstd, gain_row):
    scaled = gradient * gain_row
    return rstd * (scaled - row_mean(scaled) - normed * row_mean(scaled * normed))


def shifted_rows(src, lead, rows, start, lanes=slice(None)):
    return [src[lead, y, pl.ds(start, SUB), lanes] for y in range(rows)]


def filtered(src, lead, rows, col, taps, radius, sign, lanes=slice(None)):
    acc = [None] * rows
    for dx in range(-radius, radius + 1):
        cells = shifted_rows(src, lead, rows, col + SUB + sign * dx, lanes)
        for dy in range(-radius, radius + 1):
            tap = taps(dy, dx)
            for y in range(rows):
                from_row = y + sign * dy
                if 0 <= from_row < rows:
                    term = tap * cells[from_row]
                    acc[y] = term if acc[y] is None else acc[y] + term
    return acc


def tap_products(src, own, images, rows, cols, dx, radius, lanes=slice(None)):
    def image(lead, acc):
        acc = list(acc)
        for col in range(0, cols, SUB):
            cells = shifted_rows(src, lead, rows, col + SUB - dx, lanes)
            mine = [own(lead, y, col) for y in range(rows)]
            for k, dy in enumerate(range(-radius, radius + 1)):
                total = acc[k]
                for y in range(rows):
                    if 0 <= y - dy < rows:
                        total = total + mine[y] * cells[y - dy]
                acc[k] = total
        return tuple(acc)

    zero = jnp.zeros((SUB, LANES), F32)
    return lax.fori_loop(0, images, image, (zero,) * (2 * radius + 1))


def loop(count, body):
    def step(i, carry):
        body(i)
        return carry

    lax.fori_loop(0, count, step, 0)


def col_keep(shape_ref, lead, cols, lanes):
    return lax.broadcasted_iota(jnp.int32, (cols, lanes), 0) < shape_ref[lead, 1]


def cell_keep(shape_ref, lead, rows, cols, lanes):
    x = lax.broadcasted_iota(jnp.int32, (rows, cols, lanes), 1)
    y = lax.broadcasted_iota(jnp.int32, (rows, cols, lanes), 0)
    kept = (x < shape_ref[lead, 1]) & (y < shape_ref[lead, 0])
    return kept.reshape(rows * cols, lanes)


def head_diagonal():
    a = lax.broadcasted_iota(jnp.int32, (LANES, LANES), 0) // HD
    b = lax.broadcasted_iota(jnp.int32, (LANES, LANES), 1) // HD
    return a == b


def by_radius(step, radii, run):
    for radius in sorted(set(radii)):
        steps = [k for k, r in enumerate(radii) if r == radius]
        hit = functools.reduce(lambda a, b: a | b, [step == k for k in steps])
        pl.when(hit)(functools.partial(run, radius))


def attention_kernel(
    dims,
    radii,
    shape_ref,
    x_ref,
    small_ref,
    part_ref,
    wq_ref,
    wp_ref,
    first_ref,
    norma_ref,
    query_ref,
    probs_ref,
    value_ref,
    near_ref,
    attended_ref,
    kv_ref,
    second_ref,
    normb_ref,
    pad_x,
    pad_v,
    near_f,
    total,
):
    images, rows, cols, channels = dims
    cells = rows * cols
    step = pl.program_id(0)
    last = pl.num_programs(0) - 1

    @pl.when(step == 0)
    def _():
        pad_x[...] = jnp.zeros_like(pad_x)
        pad_v[...] = jnp.zeros_like(pad_v)

        def mask_row(r):
            lead = r // rows
            y = r % rows
            kept = col_keep(shape_ref, lead, cols, channels) & (y < shape_ref[lead, 0])
            block = x_ref[pl.ds(pl.multiple_of(r * cols, cols), cols), :].astype(F32)
            pad_x[lead, y, pl.ds(SUB, cols), :] = jnp.where(kept, block, 0.0)

        loop(images * rows, mask_row)

        def conv(lead):
            for lane in range(0, channels, LANES):
                lanes = pl.ds(lane, LANES)
                for col in range(0, cols, SUB):
                    out = filtered(
                        pad_x,
                        lead,
                        rows,
                        col,
                        lambda dy, dx: small_ref[pl.ds(3 * (dy + 1) + dx + 1, 1), lanes],
                        1,
                        1,
                        lanes,
                    )
                    bias = small_ref[pl.ds(58, 1), lanes]
                    for y in range(rows):
                        own = pad_x[lead, y, pl.ds(SUB + col, SUB), lanes]
                        at = pl.multiple_of(lead * cells + (y * cols + col), SUB)
                        first_ref[pl.ds(at, SUB), lanes] = own + out[y] + bias

        loop(images, conv)

        def normalize(r):
            at = pl.ds(pl.multiple_of(r * cols, cols), cols)
            normed, _ = norm_parts(first_ref[at, :])
            norma_ref[at, :] = (
                normed * small_ref[pl.ds(59, 1), :] + small_ref[pl.ds(60, 1), :]
            ).astype(BF16)

        loop(images * rows, normalize)

    diagonal = head_diagonal()

    def project(lead):
        at = pl.ds(pl.multiple_of(lead * cells, cells), cells)
        proj = dot(norma_ref[at, :], wq_ref[0])
        query = (proj[:, :LANES] + part_ref[0, pl.ds(61, 1), :]).astype(BF16)
        value = (proj[:, 2 * LANES :] + part_ref[0, pl.ds(62, 1), :]).astype(BF16)
        kept = cell_keep(shape_ref, lead, rows, cols, LANES)
        key = jnp.where(kept, proj[:, LANES : 2 * LANES], -1e30)
        expo = jnp.exp(key - jnp.max(key, axis=0, keepdims=True))
        probs = (expo / jnp.sum(expo, axis=0, keepdims=True)).astype(BF16)
        query_ref[0, at, :] = query
        probs_ref[0, at, :] = probs
        value_ref[0, at, :] = value
        kv = jnp.where(diagonal, dot_lt(probs, value), 0.0).astype(BF16)
        kv_ref[0, lead] = kv
        masked = jnp.where(kept, value.astype(F32), 0.0)
        pad_v[lead, :, pl.ds(SUB, cols), :] = masked.reshape(rows, cols, LANES)

    loop(images, project)

    def conv_near(radius):
        def conv(lead):
            for col in range(0, cols, SUB):
                out = filtered(
                    pad_v,
                    lead,
                    rows,
                    col,
                    lambda dy, dx: part_ref[0, pl.ds(9 + 7 * (dy + 3) + dx + 3, 1), :],
                    radius,
                    1,
                )
                bias = part_ref[0, pl.ds(63, 1), :]
                for y in range(rows):
                    at = pl.multiple_of(lead * cells + (y * cols + col), SUB)
                    near_f[pl.ds(at, SUB), :] = out[y] + bias

        loop(images, conv)

    by_radius(step, radii, conv_near)

    def attend(lead):
        at = pl.ds(pl.multiple_of(lead * cells, cells), cells)
        query = query_ref[0, at, :]
        near = near_f[at, :]
        near_ref[0, at, :] = near.astype(BF16)
        factored = dot(query, kv_ref[0, lead]) * HEAD_SCALE
        attended = (factored + query.astype(F32) * near).astype(BF16)
        attended_ref[0, at, :] = attended
        out = dot_rt(attended, wp_ref[0])

        @pl.when(step == 0)
        def _():
            total[at, :] = out

        @pl.when(step > 0)
        def _():
            total[at, :] = total[at, :] + out

    loop(images, attend)

    @pl.when(step == last)
    def _():
        def finish(r):
            at = pl.ds(pl.multiple_of(r * cols, cols), cols)
            second = first_ref[at, :] + total[at, :] + small_ref[pl.ds(64, 1), :]
            second_ref[at, :] = second
            normed, _ = norm_parts(second)
            normb_ref[at, :] = (
                normed * small_ref[pl.ds(65, 1), :] + small_ref[pl.ds(66, 1), :]
            ).astype(BF16)

        loop(images * rows, finish)


def gelu_parts(pre):
    cdf = 0.5 * (1.0 + lax.erf(pre * ROOT_HALF))
    return pre * cdf, cdf + pre * (jnp.exp(-0.5 * pre * pre) * INV_ROOT_TAU)


def hidden_kernel(
    dims,
    shape_ref,
    cot_ref,
    normb_ref,
    second_ref,
    small_ref,
    bias_ref,
    w1_ref,
    w2_ref,
    out_ref,
    dsecond_ref,
    dw_ref,
    dbias_ref,
    sums_ref,
    dout,
    pre,
    act_grad,
    hact,
    dhpre,
    total,
    dnorm,
):
    images, rows, cols, channels = dims
    cells = rows * cols
    step = pl.program_id(0)
    last = pl.num_programs(0) - 1
    hidden = w1_ref.shape[2]

    @pl.when(step == 0)
    def _():
        def mask_row(r):
            lead = r // rows
            y = r % rows
            kept = col_keep(shape_ref, lead, cols, channels) & (y < shape_ref[lead, 0])
            at = pl.ds(pl.multiple_of(r * cols, cols), cols)
            block = cot_ref[at, :].astype(F32)
            dout[at, :] = jnp.where(kept, block, 0.0).astype(BF16)

        loop(images * rows, mask_row)

    dbias_ref[...] = jnp.zeros_like(dbias_ref)

    def tile(lead):
        at = pl.ds(pl.multiple_of(lead * cells, cells), cells)
        pre[...] = dot(normb_ref[at, :], w1_ref[0]) + bias_ref[0]
        act_grad[...] = dot(dout[at, :], w2_ref[0])

        def chunk(r, acc):
            here = pl.ds(pl.multiple_of(r * 16, 16), 16)
            there = pl.ds(pl.multiple_of(lead * cells + r * 16, 16), 16)
            act, slope = gelu_parts(pre[here, :])
            hact[there, :] = act.astype(BF16)
            back = (act_grad[here, :] * slope).astype(BF16)
            dhpre[there, :] = back
            return acc + back.astype(F32)

        acc = lax.fori_loop(0, cells // 16, chunk, jnp.zeros((16, hidden), F32))
        dbias_ref[0] = dbias_ref[0] + jnp.sum(acc, axis=0, keepdims=True)
        out = dot_rt(hact[at, :], w2_ref[0])
        back = dot_rt(dhpre[at, :], w1_ref[0])

        @pl.when(step == 0)
        def _():
            total[at, :] = out
            dnorm[at, :] = back

        @pl.when(step > 0)
        def _():
            total[at, :] = total[at, :] + out
            dnorm[at, :] = dnorm[at, :] + back

    loop(images, tile)
    dw_ref[0, :, :hidden] = dot_lt(normb_ref[...], dhpre[...]).astype(BF16)
    dw_ref[0, :, hidden:] = dot_lt(dout[...], hact[...]).astype(BF16)

    @pl.when(step == last)
    def _():
        gain = small_ref[pl.ds(65, 1), :]

        def finish(r, acc):
            at = pl.ds(pl.multiple_of(r * cols, cols), cols)
            second = second_ref[at, :]
            out_ref[at, :] = (second + total[at, :] + small_ref[pl.ds(67, 1), :]).astype(BF16)
            normed, rstd = norm_parts(second)
            back = dnorm[at, :]
            got = dout[at, :].astype(F32)
            dsecond = got + norm_back(back, normed, rstd, gain)
            dsecond_ref[at, :] = dsecond
            low = dsecond.astype(BF16).astype(F32)
            terms = (low, back * normed, back, got)
            return tuple(
                a + jnp.sum(t.reshape(cols // SUB, SUB, channels), axis=0)
                for a, t in zip(acc, terms)
            )

        zero = jnp.zeros((SUB, channels), F32)
        acc = lax.fori_loop(0, images * rows, finish, (zero,) * 4)
        sums_ref[...] = jnp.zeros_like(sums_ref)
        for k, a in enumerate(acc):
            sums_ref[pl.ds(k, 1), :] = jnp.sum(a, axis=0, keepdims=True)


def attention_back_kernel(
    dims,
    radii,
    shape_ref,
    dsecond_ref,
    norma_ref,
    part_ref,
    wq_ref,
    wp_ref,
    query_ref,
    probs_ref,
    value_ref,
    near_ref,
    attended_ref,
    kv_ref,
    dnorma_ref,
    dw_ref,
    sums_ref,
    low,
    pad_d,
    value_f,
    grads,
    dvalue_f,
):
    images, rows, cols, channels = dims
    cells = rows * cols
    step = pl.program_id(0)

    @pl.when(step == 0)
    def _():
        pad_d[...] = jnp.zeros_like(pad_d)

        def round_row(r):
            at = pl.ds(pl.multiple_of(r * cols, cols), cols)
            low[at, :] = dsecond_ref[at, :].astype(BF16)

        loop(images * rows, round_row)

    sums_ref[...] = jnp.zeros_like(sums_ref)
    diagonal = head_diagonal()

    def first_half(lead):
        at = pl.ds(pl.multiple_of(lead * cells, cells), cells)
        datt = dot(low[at, :], wp_ref[0]).astype(BF16)
        query = query_ref[0, at, :]
        probs = probs_ref[0, at, :]
        value = value_ref[0, at, :]
        kept = cell_keep(shape_ref, lead, rows, cols, LANES)
        dkv = jnp.where(diagonal, dot_lt(query, datt) * HEAD_SCALE, 0.0).astype(BF16)
        datt_f = datt.astype(F32)
        dnear = datt_f * query.astype(F32)
        pad_d[lead, :, pl.ds(SUB, cols), :] = dnear.reshape(rows, cols, LANES)
        dquery = (
            dot_rt(datt, kv_ref[0, lead]) * HEAD_SCALE + datt_f * near_ref[0, at, :].astype(F32)
        ).astype(BF16)
        dprobs = dot_rt(value, dkv)
        probs_f = probs.astype(F32)
        inner = jnp.sum(probs_f * dprobs, axis=0, keepdims=True)
        dkey = (probs_f * (dprobs - inner)).astype(BF16)
        grads[at, :LANES] = dquery
        grads[at, LANES : 2 * LANES] = dkey
        dvalue_f[at, :] = dot(probs, dkv)
        value_f[at, :] = jnp.where(kept, value.astype(F32), 0.0)
        sums_ref[0, pl.ds(61, 1), :] += jnp.sum(dquery.astype(F32), axis=0, keepdims=True)
        sums_ref[0, pl.ds(63, 1), :] += jnp.sum(dnear, axis=0, keepdims=True)

    loop(images, first_half)

    def conv_back(radius):
        def conv(lead):
            x = lax.broadcasted_iota(jnp.int32, (SUB, LANES), 0)
            for col in range(0, cols, SUB):
                out = filtered(
                    pad_d,
                    lead,
                    rows,
                    col,
                    lambda dy, dx: part_ref[0, pl.ds(9 + 7 * (dy + 3) + dx + 3, 1), :],
                    radius,
                    -1,
                )
                inside = (x + col) < shape_ref[lead, 1]
                for y in range(rows):
                    at = pl.ds(pl.multiple_of(lead * cells + (y * cols + col), SUB), SUB)
                    kept = inside & (y < shape_ref[lead, 0])
                    dvalue_f[at, :] = dvalue_f[at, :] + jnp.where(kept, out[y], 0.0)

        loop(images, conv)

        def own(lead, y, col):
            at = pl.multiple_of(lead * cells + (y * cols + col), SUB)
            return value_f[pl.ds(at, SUB), :]

        for dx in range(-radius, radius + 1):
            acc = tap_products(pad_d, own, images, rows, cols, dx, radius)
            for k, dy in enumerate(range(-radius, radius + 1)):
                sums_ref[0, pl.ds(9 + 7 * (dy + 3) + dx + 3, 1), :] = jnp.sum(
                    acc[k], axis=0, keepdims=True
                )

    by_radius(step, radii, conv_back)

    def second_half(lead):
        at = pl.ds(pl.multiple_of(lead * cells, cells), cells)
        dvalue = dvalue_f[at, :].astype(BF16)
        grads[at, 2 * LANES :] = dvalue
        sums_ref[0, pl.ds(62, 1), :] += jnp.sum(dvalue.astype(F32), axis=0, keepdims=True)
        back = dot_rt(grads[at, :], wq_ref[0])

        @pl.when(step == 0)
        def _():
            dnorma_ref[at, :] = back

        @pl.when(step > 0)
        def _():
            dnorma_ref[at, :] = dnorma_ref[at, :] + back

    loop(images, second_half)
    wide = 3 * LANES
    dw_ref[0, :, :wide] = dot_lt(norma_ref[...], grads[...]).astype(BF16)
    dw_ref[0, :, wide:] = dot_lt(low[...], attended_ref[0]).astype(BF16)


def input_back_kernel(
    dims,
    shape_ref,
    x_ref,
    first_ref,
    dnorma_ref,
    dsecond_ref,
    small_ref,
    grad_ref,
    sums_ref,
    pad_d,
    x_f,
):
    images, rows, cols, channels = dims
    cells = rows * cols
    pad_d[...] = jnp.zeros_like(pad_d)
    gain = small_ref[pl.ds(59, 1), :]

    def norm(r, acc):
        lead = r // rows
        y = r % rows
        at = pl.ds(pl.multiple_of(r * cols, cols), cols)
        normed, rstd = norm_parts(first_ref[at, :])
        back = dnorma_ref[at, :]
        dfirst = dsecond_ref[at, :] + norm_back(back, normed, rstd, gain)
        pad_d[lead, y, pl.ds(SUB, cols), :] = dfirst
        kept = col_keep(shape_ref, lead, cols, channels) & (y < shape_ref[lead, 0])
        x_f[at, :] = jnp.where(kept, x_ref[at, :].astype(F32), 0.0)
        terms = (dfirst, back * normed, back)
        return tuple(
            a + jnp.sum(t.reshape(cols // SUB, SUB, channels), axis=0)
            for a, t in zip(acc, terms)
        )

    zero = jnp.zeros((SUB, channels), F32)
    acc = lax.fori_loop(0, images * rows, norm, (zero,) * 3)
    sums_ref[...] = jnp.zeros_like(sums_ref)
    for k, a in enumerate(acc):
        sums_ref[pl.ds(9 + k, 1), :] = jnp.sum(a, axis=0, keepdims=True)

    def conv(lead):
        x = lax.broadcasted_iota(jnp.int32, (SUB, LANES), 0)
        for lane in range(0, channels, LANES):
            lanes = pl.ds(lane, LANES)
            for col in range(0, cols, SUB):
                out = filtered(
                    pad_d,
                    lead,
                    rows,
                    col,
                    lambda dy, dx: small_ref[pl.ds(3 * (dy + 1) + dx + 1, 1), lanes],
                    1,
                    -1,
                    lanes,
                )
                inside = (x + col) < shape_ref[lead, 1]
                for y in range(rows):
                    own = pad_d[lead, y, pl.ds(SUB + col, SUB), lanes]
                    at = pl.multiple_of(lead * cells + (y * cols + col), SUB)
                    kept = inside & (y < shape_ref[lead, 0])
                    grad_ref[pl.ds(at, SUB), lanes] = jnp.where(kept, own + out[y], 0.0)

    loop(images, conv)
    for lane in range(0, channels, LANES):
        lanes = pl.ds(lane, LANES)

        def own(lead, y, col):
            at = pl.multiple_of(lead * cells + (y * cols + col), SUB)
            return x_f[pl.ds(at, SUB), lanes]

        for dx in (-1, 0, 1):
            acc = tap_products(pad_d, own, images, rows, cols, dx, 1, lanes)
            for k, dy in enumerate((-1, 0, 1)):
                sums_ref[pl.ds(3 * (dy + 1) + dx + 1, 1), lanes] = jnp.sum(
                    acc[k], axis=0, keepdims=True
                )


def whole(shape):
    return pl.BlockSpec(shape, lambda *_: (0,) * len(shape))


def part(shape):
    return pl.BlockSpec((1, *shape), lambda j: (j,) + (0,) * len(shape))


SCALARS = pl.BlockSpec(memory_space=pltpu.SMEM)
PARAMS = pltpu.CompilerParams(vmem_limit_bytes=VMEM_LIMIT)


def shape_of(shape, dtype):
    return jax.ShapeDtypeStruct(shape, dtype)


def attention(dims, radii, grids, x, small, parts, wq, wp):
    images, rows, cols, channels = dims
    cells = images * rows * cols
    groups = wq.shape[0]
    kinds = ((cells, LANES),) * 5 + ((images, LANES, LANES),)
    return pl.pallas_call(
        functools.partial(attention_kernel, dims, radii),
        grid=(groups,),
        in_specs=[
            SCALARS,
            whole((cells, channels)),
            whole(small.shape),
            part(parts.shape[1:]),
            part(wq.shape[1:]),
            part(wp.shape[1:]),
        ],
        out_specs=[
            whole((cells, channels)),
            whole((cells, channels)),
            *[part(k) for k in kinds],
            whole((cells, channels)),
            whole((cells, channels)),
        ],
        out_shape=[
            shape_of((cells, channels), F32),
            shape_of((cells, channels), BF16),
            *[shape_of((groups, *k), BF16) for k in kinds],
            shape_of((cells, channels), F32),
            shape_of((cells, channels), BF16),
        ],
        scratch_shapes=[
            pltpu.VMEM((images, rows, cols + 2 * SUB, channels), F32),
            pltpu.VMEM((images, rows, cols + 2 * SUB, LANES), F32),
            pltpu.VMEM((cells, LANES), F32),
            pltpu.VMEM((cells, channels), F32),
        ],
        compiler_params=PARAMS,
        name="attention",
    )(grids, x, small, parts, wq, wp)


def hidden_part(dims, grids, cot, normb, second, small, bias, w1, w2):
    images, rows, cols, channels = dims
    cells = images * rows * cols
    groups, _, hidden = w1.shape
    return pl.pallas_call(
        functools.partial(hidden_kernel, dims),
        grid=(groups,),
        in_specs=[
            SCALARS,
            whole((cells, channels)),
            whole((cells, channels)),
            whole((cells, channels)),
            whole(small.shape),
            part(bias.shape[1:]),
            part(w1.shape[1:]),
            part(w2.shape[1:]),
        ],
        out_specs=[
            whole((cells, channels)),
            whole((cells, channels)),
            part((channels, 2 * hidden)),
            part((1, hidden)),
            whole((SUB, channels)),
        ],
        out_shape=[
            shape_of((cells, channels), BF16),
            shape_of((cells, channels), F32),
            shape_of((groups, channels, 2 * hidden), BF16),
            shape_of((groups, 1, hidden), F32),
            shape_of((SUB, channels), F32),
        ],
        scratch_shapes=[
            pltpu.VMEM((cells, channels), BF16),
            pltpu.VMEM((rows * cols, hidden), F32),
            pltpu.VMEM((rows * cols, hidden), F32),
            pltpu.VMEM((cells, hidden), BF16),
            pltpu.VMEM((cells, hidden), BF16),
            pltpu.VMEM((cells, channels), F32),
            pltpu.VMEM((cells, channels), F32),
        ],
        compiler_params=PARAMS,
        name="hidden",
    )(grids, cot, normb, second, small, bias, w1, w2)


def attention_back(dims, radii, grids, dsecond, norma, parts, wq, wp, saved):
    images, rows, cols, channels = dims
    cells = images * rows * cols
    groups = wq.shape[0]
    return pl.pallas_call(
        functools.partial(attention_back_kernel, dims, radii),
        grid=(groups,),
        in_specs=[
            SCALARS,
            whole((cells, channels)),
            whole((cells, channels)),
            part(parts.shape[1:]),
            part(wq.shape[1:]),
            part(wp.shape[1:]),
            *[part(s.shape[1:]) for s in saved],
        ],
        out_specs=[
            whole((cells, channels)),
            part((channels, 4 * LANES)),
            part((72, LANES)),
        ],
        out_shape=[
            shape_of((cells, channels), F32),
            shape_of((groups, channels, 4 * LANES), BF16),
            shape_of((groups, 72, LANES), F32),
        ],
        scratch_shapes=[
            pltpu.VMEM((cells, channels), BF16),
            pltpu.VMEM((images, rows, cols + 2 * SUB, LANES), F32),
            pltpu.VMEM((cells, LANES), F32),
            pltpu.VMEM((cells, 3 * LANES), BF16),
            pltpu.VMEM((cells, LANES), F32),
        ],
        compiler_params=PARAMS,
        name="attention_back",
    )(grids, dsecond, norma, parts, wq, wp, *saved)


def input_back(dims, grids, x, first, dnorma, dsecond, small):
    images, rows, cols, channels = dims
    cells = images * rows * cols
    return pl.pallas_call(
        functools.partial(input_back_kernel, dims),
        grid=(1,),
        in_specs=[
            SCALARS,
            whole((cells, channels)),
            whole((cells, channels)),
            whole((cells, channels)),
            whole((cells, channels)),
            whole(small.shape),
        ],
        out_specs=[whole((cells, channels)), whole((16, channels))],
        out_shape=[shape_of((cells, channels), F32), shape_of((16, channels), F32)],
        scratch_shapes=[
            pltpu.VMEM((images, rows, cols + 2 * SUB, channels), F32),
            pltpu.VMEM((cells, channels), F32),
        ],
        compiler_params=PARAMS,
        name="input_back",
    )(grids, x, first, dnorma, dsecond, small)


def adamw(weight, mean, square, gradient, factor, rate, decay):
    clipped = gradient * factor
    mean_new = BETA_ONE * mean + (1.0 - BETA_ONE) * clipped
    square_new = BETA_TWO * square + (1.0 - BETA_TWO) * clipped * clipped
    mean_hat = mean_new / (1.0 - BETA_ONE**STEP)
    square_hat = square_new / (1.0 - BETA_TWO**STEP)
    weight_new = weight - rate * (mean_hat / (jnp.sqrt(square_hat) + ADAM_EPS) + decay * weight)
    return (weight_new, mean_new, square_new)


def window_rows(channels):
    radius = jnp.repeat(jnp.array([radius_of(h) for h in range(channels // HD)], jnp.int32), HD)
    tap_list = jnp.arange(49, dtype=jnp.int32)
    tap_row = jnp.abs(tap_list // 7 - 3)
    tap_col = jnp.abs(tap_list % 7 - 3)
    inside = (tap_row[:, None] <= radius[None, :]) & (tap_col[:, None] <= radius[None, :])
    return inside.astype(F32)


def on_device(
    patches,
    cotangent,
    grid_shape,
    qkv_weight,
    qkv_mean,
    qkv_square,
    proj_weight,
    proj_mean,
    proj_square,
    expand_weight,
    expand_mean,
    expand_square,
    contract_weight,
    contract_mean,
    contract_square,
    small_params,
    small_mean,
    small_square,
):
    group = lax.axis_size("mp")
    shards = lax.axis_size("dp")
    place = lax.axis_index("mp")
    local_rows, image_count, cols, channels = patches.shape
    images = image_count // group
    rows = local_rows * group
    dims = (images, rows, cols, channels)
    cells = images * rows * cols
    head_width = qkv_weight.shape[2]
    hidden = expand_weight.shape[1]
    assert head_width == LANES
    per_block = head_width // HD
    radii = [
        max(radius_of(per_block * g + h) for h in range(per_block)) for g in range(group)
    ]
    grids = lax.dynamic_slice_in_dim(grid_shape, place * images, images, 0)

    x = to_images(patches).reshape(cells, channels)

    def whole_weight(weight):
        rows_here = weight.shape[0]
        weight = weight.astype(BF16).reshape(rows_here, -1)
        every = gathered(gathered(weight, "dp").reshape(shards * rows_here, -1), "mp")
        return every

    wq = whole_weight(qkv_weight)
    wp = whole_weight(proj_weight)
    cot = to_images(cotangent.astype(BF16)).reshape(cells, channels)
    w1 = whole_weight(expand_weight)
    w2 = whole_weight(contract_weight)

    window = window_rows(channels)
    masked_small = jnp.concatenate(
        [small_params[:9], small_params[9:58] * window, small_params[58:]], axis=0
    )
    parts = masked_small.reshape(72, group, LANES).transpose(1, 0, 2)
    unit_bias = small_params[68:].reshape(group, 1, hidden)

    first, norma, *saved, second, normb = attention(
        dims, radii, grids, x, small_params, parts, wq, wp
    )
    out, dsecond, dw_hidden, dbias, sums_two = hidden_part(
        dims, grids, cot, normb, second, small_params, unit_bias, w1, w2
    )
    block_out = to_rows(out.reshape(dims))
    dnorma, dw_heads, sums_heads = attention_back(
        dims, radii, grids, dsecond, norma, parts, wq, wp, saved
    )
    grad, sums_one = input_back(dims, grids, x, first, dnorma, dsecond, small_params)
    patch_grad = to_rows(grad.astype(BF16).reshape(dims)).astype(F32)

    def own_share(grads):
        tiles = grads.reshape(group, shards, channels // shards, grads.shape[-1])
        return halved(halved(tiles, "mp", 0), "dp", 0).astype(F32)

    shard_hidden = own_share(dw_hidden)
    shard_heads = own_share(dw_heads)
    shard_expand = shard_hidden[:, :hidden]
    shard_contract = shard_hidden[:, hidden:]
    shard_qkv = shard_heads[:, : 3 * LANES].reshape(-1, 3, LANES)
    shard_proj = shard_heads[:, 3 * LANES :]

    heads_rows = sums_heads.transpose(1, 0, 2).reshape(72, channels)
    small_local = jnp.concatenate(
        [
            sums_one[:9],
            heads_rows[9:58] * window,
            sums_one[9:12],
            heads_rows[61:64],
            sums_two[:4],
            dbias.reshape(-1, channels),
        ],
        axis=0,
    )
    count = group * shards
    both = ("dp", "mp")
    tiles = lax.all_to_all(small_local.reshape(count, -1), both, 0, 0, tiled=True)
    own_small = jnp.sum(tiles, axis=0)
    local_sq = (
        jnp.sum(shard_heads * shard_heads)
        + jnp.sum(shard_hidden * shard_hidden)
        + jnp.sum(own_small * own_small)
    )
    message = jnp.concatenate([own_small, jnp.full((LANES,), local_sq, F32)])
    every = lax.all_to_all(
        jnp.broadcast_to(message, (count, message.shape[0])), both, 0, 0, tiled=True
    )
    grad_small = every[:, : own_small.shape[0]].reshape(small_params.shape)
    grad_norm = jnp.sqrt(jnp.sum(every[:, own_small.shape[0]]))
    factor = jnp.minimum(1.0, CLIP_NORM / (grad_norm + 1e-06))
    rate_model = RATE_FACTOR * D ** (-0.5)
    rate_hidden = RATE_FACTOR * FF ** (-0.5)
    qkv_new = adamw(qkv_weight, qkv_mean, qkv_square, shard_qkv, factor, rate_model, WEIGHT_DECAY)
    proj_new = adamw(
        proj_weight, proj_mean, proj_square, shard_proj, factor, rate_model, WEIGHT_DECAY
    )
    expand_new = adamw(
        expand_weight, expand_mean, expand_square, shard_expand, factor, rate_model, WEIGHT_DECAY
    )
    contract_new = adamw(
        contract_weight,
        contract_mean,
        contract_square,
        shard_contract,
        factor,
        rate_hidden,
        WEIGHT_DECAY,
    )
    small_new = adamw(small_params, small_mean, small_square, grad_small, factor, SMALL_RATE, 0.0)
    return (
        block_out,
        patch_grad,
        grad_norm,
        *qkv_new,
        *proj_new,
        *expand_new,
        *contract_new,
        *small_new,
    )


def solution(mesh):
    cells = P("mp", "dp", None, None)
    heads = P("dp", None, "mp")
    matrix = P("dp", "mp")
    params = [heads] * 3 + [matrix] * 9 + [P()] * 3
    return jax.shard_map(
        on_device,
        mesh=mesh,
        in_specs=(cells, cells, P("dp", None), *params),
        out_specs=(cells, cells, P(), *params),
        check_vma=False,
    )
```

```python
import functools
import math

import jax
import jax.numpy as jnp
from jax import lax
from jax.experimental import pallas as pl
from jax.experimental.pallas import tpu as pltpu
from jax.sharding import PartitionSpec as P

D = 512
HD = 64
FF = 2048
STEP = 10


NORM_EPS = 1e-06
CLIP_NORM = 1.0
BETA_ONE = 0.9
BETA_TWO = 0.999
ADAM_EPS = 1e-08
WEIGHT_DECAY = 0.05
RATE_FACTOR = 2.0
SMALL_RATE = 0.5
ROOT_HALF = 0.7071067811865476
INV_ROOT_TAU = 0.3989422804014327
HEAD_SCALE = HD ** (-0.5)

LANES = 128
SUB = 8
F32 = jnp.float32
BF16 = jnp.bfloat16


def radius_of(head):
    return 1 if head < 2 else 2 if head < 5 else 3


def log2(size):
    bits = size.bit_length() - 1
    assert 1 << bits == size
    return bits


BLOCK = 64
NEAR_LAST = (2, 1, 0)
NEAR_FIRST = (0, 2, 1)
CORE, CHIP = 0, 1


def flip(array, axis, bit):
    size = lax.axis_size(axis)
    return lax.ppermute(array, axis, [(i, i ^ (1 << bit)) for i in range(size)])


def bit_of(axis, bit):
    return (lax.axis_index(axis) >> bit) & 1


def finer_bits(shard_rows):
    return log2(BLOCK // shard_rows) if shard_rows < BLOCK else 0


def after(array, *others):
    return lax.optimization_barrier((array, *others))[0]


def whole_block(shard):
    for bit in range(finer_bits(shard.shape[0])):
        other = flip(shard, "dp", bit)
        upper = bit_of("dp", bit) == 1
        shard = jnp.where(
            upper,
            jnp.concatenate([other, shard], axis=0),
            jnp.concatenate([shard, other], axis=0),
        )
    return shard[None]


def doubled(blocks, bit, low):
    return jnp.concatenate([blocks, flip(blocks, "dp", bit + low)], axis=0)


def dp_masks(order):
    masks = [0]
    for bit in order:
        masks += [m ^ (1 << bit) for m in masks]
    return masks


def added(mine, got):
    return mine.astype(F32) + got.astype(F32)


def halved(blocks, bit, low):
    half = blocks.shape[0] // 2
    return added(blocks[:half], flip(blocks[half:], "dp", bit + low))


def own_rows(total, low):
    for bit in reversed(range(low)):
        pair = total.astype(BF16).reshape(2, -1, total.shape[-1])
        mine = lax.dynamic_index_in_dim(pair, bit_of("dp", bit), 0, keepdims=False)
        theirs = lax.dynamic_index_in_dim(pair, 1 - bit_of("dp", bit), 0, keepdims=False)
        total = added(mine, flip(theirs, "dp", bit))
    return total


def swapped(pieces):
    size = lax.axis_size("mp")
    return [
        piece if k == 0 else lax.ppermute(piece, "mp", [(i, i ^ k) for i in range(size)])
        for k, piece in enumerate(pieces)
    ]


def dot(a, b):
    return lax.dot_general(a, b, (((1,), (0,)), ((), ())), preferred_element_type=F32)


def dot_rt(a, b):
    return lax.dot_general(a, b, (((1,), (1,)), ((), ())), preferred_element_type=F32)


def dot_lt(a, b):
    return lax.dot_general(a, b, (((0,), (0,)), ((), ())), preferred_element_type=F32)


def row_mean(values):
    return jnp.sum(values, axis=-1, keepdims=True) * (1.0 / values.shape[-1])


def norm_parts(values):
    center = values - row_mean(values)
    rstd = lax.rsqrt(row_mean(center * center) + NORM_EPS)
    return center * rstd, rstd


def norm_back(gradient, normed, rstd, gain_row):
    scaled = gradient * gain_row
    return rstd * (scaled - row_mean(scaled) - normed * row_mean(scaled * normed))


def shifted_rows(src, lead, rows, start, lanes=slice(None)):
    return [src[lead, y, pl.ds(start, SUB), lanes] for y in range(rows)]


def filtered(src, lead, rows, col, taps, radius, sign, lanes=slice(None)):
    acc = [None] * rows
    for dx in range(-radius, radius + 1):
        cells = shifted_rows(src, lead, rows, col + SUB + sign * dx, lanes)
        for dy in range(-radius, radius + 1):
            tap = taps(dy, dx)
            for y in range(rows):
                from_row = y + sign * dy
                if 0 <= from_row < rows:
                    term = tap * cells[from_row]
                    acc[y] = term if acc[y] is None else acc[y] + term
    return acc


def tap_products(src, own, images, rows, cols, dx, radius, lanes=slice(None)):
    def image(lead, acc):
        acc = list(acc)
        for col in range(0, cols, SUB):
            cells = shifted_rows(src, lead, rows, col + SUB - dx, lanes)
            mine = [own(lead, y, col) for y in range(rows)]
            for k, dy in enumerate(range(-radius, radius + 1)):
                total = acc[k]
                for y in range(rows):
                    if 0 <= y - dy < rows:
                        total = total + mine[y] * cells[y - dy]
                acc[k] = total
        return tuple(acc)

    zero = jnp.zeros((SUB, LANES), F32)
    return lax.fori_loop(0, images, image, (zero,) * (2 * radius + 1))


def loop(count, body, unroll=1):
    def step(i, carry):
        body(i)
        return carry

    lax.fori_loop(0, count, step, 0, unroll=unroll)


def slot_of(mask, order):
    return sum(((mask >> bit) & 1) << k for k, bit in enumerate(order))


def fetch(blocks, order, target, dp_block):
    for slot, mask in enumerate(dp_masks(order)):
        row = pl.multiple_of((dp_block ^ mask) * BLOCK, BLOCK)
        target[pl.ds(row, BLOCK), :] = blocks[slot]


def hand_out(blocks, order, values, columns, dp_block):
    for block in range(values.shape[0] // BLOCK):
        slot = slot_of(dp_block ^ block, order)
        blocks[slot, :, columns] = values[block * BLOCK : (block + 1) * BLOCK].astype(BF16)


def height(meta_ref, lead):
    return meta_ref[2 + 2 * lead]


def width(meta_ref, lead):
    return meta_ref[3 + 2 * lead]


def col_keep(meta_ref, lead, cols, lanes):
    return lax.broadcasted_iota(jnp.int32, (cols, lanes), 0) < width(meta_ref, lead)


def cell_keep(meta_ref, lead, rows, cols, lanes):
    x = lax.broadcasted_iota(jnp.int32, (rows, cols, lanes), 1)
    y = lax.broadcasted_iota(jnp.int32, (rows, cols, lanes), 0)
    kept = (x < width(meta_ref, lead)) & (y < height(meta_ref, lead))
    return kept.reshape(rows * cols, lanes)


def head_diagonal():
    a = lax.broadcasted_iota(jnp.int32, (LANES, LANES), 0) // HD
    b = lax.broadcasted_iota(jnp.int32, (LANES, LANES), 1) // HD
    return a == b


def by_radius(step, radii, run):
    for radius in sorted(set(radii)):
        steps = [k for k, r in enumerate(radii) if r == radius]
        hit = functools.reduce(lambda a, b: a | b, [step == k for k in steps])
        pl.when(hit)(functools.partial(run, radius))


def enter_kernel(
    dims,
    local_rows,
    meta_ref,
    *refs,
):
    images, rows, cols, channels = dims
    cells = rows * cols
    group = rows // local_rows
    pieces = refs[:group]
    small_ref, x_ref, first_ref, norma_ref, normed_ref, rstd_ref, pad_x = refs[group:]
    place = meta_ref[0]
    zeros = jnp.zeros((images, rows, SUB, channels), F32)
    pad_x[:, :, :SUB, :] = zeros
    pad_x[:, :, SUB + cols :, :] = zeros

    for k, piece in enumerate(pieces):

        def mask_row(r):
            lead = r // local_rows
            y_here = r % local_rows
            y = (place ^ k) * local_rows + y_here
            kept = col_keep(meta_ref, lead, cols, channels) & (y < height(meta_ref, lead))
            block = jnp.where(kept, piece[y_here, lead], 0)
            at = pl.ds(pl.multiple_of((lead * rows + y) * cols, cols), cols)
            x_ref[at, :] = block
            pad_x[lead, y, pl.ds(SUB, cols), :] = block.astype(F32)

        loop(images * local_rows, mask_row, 2)

    def conv(lead):
        for lane in range(0, channels, LANES):
            lanes = pl.ds(lane, LANES)
            for col in range(0, cols, SUB):
                out = filtered(
                    pad_x,
                    lead,
                    rows,
                    col,
                    lambda dy, dx: small_ref[pl.ds(3 * (dy + 1) + dx + 1, 1), lanes],
                    1,
                    1,
                    lanes,
                )
                bias = small_ref[pl.ds(58, 1), lanes]
                for y in range(rows):
                    own = pad_x[lead, y, pl.ds(SUB + col, SUB), lanes]
                    at = pl.multiple_of(lead * cells + (y * cols + col), SUB)
                    first_ref[pl.ds(at, SUB), lanes] = own + out[y] + bias

    loop(images, conv)

    def normalize(r):
        at = pl.ds(pl.multiple_of(r * cols, cols), cols)
        normed, rstd = norm_parts(first_ref[at, :])
        normed_ref[at, :] = normed
        rstd_ref[at, :] = jnp.broadcast_to(rstd, (cols, LANES))
        norma_ref[at, :] = (
            normed * small_ref[pl.ds(59, 1), :] + small_ref[pl.ds(60, 1), :]
        ).astype(BF16)

    loop(images * rows, normalize, 4)


def attention_kernel(
    dims,
    radii,
    base,
    final,
    meta_ref,
    norma_ref,
    part_ref,
    w_0,
    w_1,
    *refs,
):
    images, rows, cols, channels = dims
    cells = rows * cols
    if base:
        before_ref, *refs = refs
    if final:
        first_ref, small_ref, *refs = refs
    query_ref, probs_ref, value_ref, near_ref, attended_ref, kv_ref, *refs = refs
    if final:
        second_ref, normb_ref, normed_ref, rstd_ref, total, *refs = refs
    else:
        total, *refs = refs
    weight, pad_v, near_f = refs

    for k, blocks in enumerate((w_0, w_1)):
        fetch(blocks, NEAR_LAST, weight.at[k], meta_ref[1])
    pad_v[...] = jnp.zeros_like(pad_v)
    diagonal = head_diagonal()

    def head_step(step):
        block = (step + base) ^ meta_ref[0]
        attention_step(step, block)

    def attention_step(step, block):

        def project(lead):
            at = pl.ds(pl.multiple_of(lead * cells, cells), cells)
            proj = dot(norma_ref[at, :], weight[step, :, : 3 * LANES])
            query = (proj[:, :LANES] + part_ref[block, pl.ds(61, 1), :]).astype(BF16)
            value = (proj[:, 2 * LANES :] + part_ref[block, pl.ds(62, 1), :]).astype(BF16)
            kept = cell_keep(meta_ref, lead, rows, cols, LANES)
            key = jnp.where(kept, proj[:, LANES : 2 * LANES], -1e30)
            expo = jnp.exp(key - jnp.max(key, axis=0, keepdims=True))
            probs = (expo / jnp.sum(expo, axis=0, keepdims=True)).astype(BF16)
            query_ref[step, at, :] = query
            probs_ref[step, at, :] = probs
            value_ref[step, at, :] = value
            kv = jnp.where(diagonal, dot_lt(probs, value), 0.0).astype(BF16)
            kv_ref[step, lead] = kv
            masked = jnp.where(kept, value.astype(F32), 0.0)
            pad_v[lead, :, pl.ds(SUB, cols), :] = masked.reshape(rows, cols, LANES)

        loop(images, project)

        def conv_near(radius):
            def conv(lead):
                for col in range(0, cols, SUB):
                    out = filtered(
                        pad_v,
                        lead,
                        rows,
                        col,
                        lambda dy, dx: part_ref[block, pl.ds(9 + 7 * (dy + 3) + dx + 3, 1), :],
                        radius,
                        1,
                    )
                    bias = part_ref[block, pl.ds(63, 1), :]
                    for y in range(rows):
                        at = pl.multiple_of(lead * cells + (y * cols + col), SUB)
                        near_f[pl.ds(at, SUB), :] = out[y] + bias

            loop(images, conv)

        by_radius(block, radii, conv_near)

        def attend(lead):
            at = pl.ds(pl.multiple_of(lead * cells, cells), cells)
            query = query_ref[step, at, :]
            near = near_f[at, :]
            near_ref[step, at, :] = near.astype(BF16)
            factored = dot(query, kv_ref[step, lead]) * HEAD_SCALE
            attended = (factored + query.astype(F32) * near).astype(BF16)
            attended_ref[step, at, :] = attended
            out = dot_rt(attended, weight[step, :, 3 * LANES :])

            @pl.when(step == 0)
            def _():
                total[at, :] = out + before_ref[at, :] if base else out

            @pl.when(step > 0)
            def _():
                total[at, :] = total[at, :] + out

        loop(images, attend)
    loop(2, head_step)
    if not final:
        return

    def finish(r):
        at = pl.ds(pl.multiple_of(r * cols, cols), cols)
        second = first_ref[at, :] + total[at, :] + small_ref[pl.ds(64, 1), :]
        second_ref[at, :] = second
        normed, rstd = norm_parts(second)
        normed_ref[at, :] = normed
        rstd_ref[at, :] = jnp.broadcast_to(rstd, (cols, LANES))
        normb_ref[at, :] = (
            normed * small_ref[pl.ds(65, 1), :] + small_ref[pl.ds(66, 1), :]
        ).astype(BF16)

    loop(images * rows, finish, 4)


def gelu_parts(pre):
    cdf = 0.5 * (1.0 + lax.erf(pre * ROOT_HALF))
    return pre * cdf, cdf + pre * (jnp.exp(-0.5 * pre * pre) * INV_ROOT_TAU)


def hidden_kernel(
    dims,
    local_rows,
    base,
    final,
    meta_ref,
    normb_ref,
    bias_ref,
    w1_0,
    w1_1,
    w2_0,
    w2_1,
    *refs,
):
    images, rows, cols, channels = dims
    cells = rows * cols
    group = rows // local_rows
    if base:
        dout, total_in, dnorm_in, *refs = refs
    else:
        pieces, refs = refs[:group], refs[group:]
    if final:
        second_ref, normed_ref, rstd_ref, small_ref, *refs = refs
    d_0, d_1, dbias_ref, *refs = refs
    if final:
        outs, refs = refs[:group], refs[group:]
        dsecond_ref, low_ref, sums_ref, total, dnorm, *refs = refs
    else:
        dout, total, dnorm, *refs = refs
    w1, w2, pre, act_grad, hact, dhpre = refs
    hidden = w1.shape[2]
    place, dp_block = meta_ref[0], meta_ref[1]

    for k, (one, two) in enumerate(((w1_0, w2_0), (w1_1, w2_1))):
        fetch(one, NEAR_LAST, w1.at[k], dp_block)
        fetch(two, NEAR_FIRST, w2.at[k], dp_block)
    if not base:
        for k, piece in enumerate(pieces):

            def mask_row(r):
                lead = r // local_rows
                y_here = r % local_rows
                y = (place ^ k) * local_rows + y_here
                kept = col_keep(meta_ref, lead, cols, channels) & (y < height(meta_ref, lead))
                at = pl.ds(pl.multiple_of((lead * rows + y) * cols, cols), cols)
                block = piece[y_here, lead].astype(F32)
                dout[at, :] = jnp.where(kept, block, 0.0).astype(BF16)

            loop(images * local_rows, mask_row, 2)

    dbias_ref[...] = jnp.zeros_like(dbias_ref)

    def hidden_step(step):
        def tile(lead):
            at = pl.ds(pl.multiple_of(lead * cells, cells), cells)
            pre[...] = dot(normb_ref[at, :], w1[step]) + bias_ref[(step + base) ^ place]
            act_grad[...] = dot(dout[at, :], w2[step])

            def chunk(r, acc):
                here = pl.ds(pl.multiple_of(r * 16, 16), 16)
                there = pl.ds(pl.multiple_of(lead * cells + r * 16, 16), 16)
                act, slope = gelu_parts(pre[here, :])
                hact[there, :] = act.astype(BF16)
                back = (act_grad[here, :] * slope).astype(BF16)
                dhpre[there, :] = back
                return acc + back.astype(F32)

            acc = lax.fori_loop(0, cells // 16, chunk, jnp.zeros((16, hidden), F32))
            dbias_ref[step] = dbias_ref[step] + jnp.sum(acc, axis=0, keepdims=True)
            out = dot_rt(hact[at, :], w2[step])
            back = dot_rt(dhpre[at, :], w1[step])

            @pl.when(step == 0)
            def _():
                total[at, :] = out + total_in[at, :] if base else out
                dnorm[at, :] = back + dnorm_in[at, :] if base else back

            @pl.when(step > 0)
            def _():
                total[at, :] = total[at, :] + out
                dnorm[at, :] = dnorm[at, :] + back

        loop(images, tile)
        dw1 = dot_lt(normb_ref[...], dhpre[...])
        dw2 = dot_lt(dout[...], hact[...])
        for k, out in enumerate((d_0, d_1)):

            @pl.when(step == k)
            def _(k=k, out=out):
                hand_out(out, NEAR_LAST, dw1, pl.ds(0, hidden), dp_block)
                hand_out(out, NEAR_LAST, dw2, pl.ds(hidden, hidden), dp_block)

    loop(2, hidden_step)
    if final:
        gain = small_ref[pl.ds(65, 1), :]
        zero = jnp.zeros((SUB, channels), F32)
        acc = (zero,) * 4
        for k, out_ref in enumerate(outs):

            def finish(r, acc):
                lead = r // local_rows
                y_here = r % local_rows
                y = (place ^ k) * local_rows + y_here
                at = pl.ds(pl.multiple_of((lead * rows + y) * cols, cols), cols)
                second = second_ref[at, :]
                out = second + total[at, :] + small_ref[pl.ds(67, 1), :]
                out_ref[y_here, lead] = out.astype(BF16)
                normed = normed_ref[at, :]
                rstd = jnp.concatenate([rstd_ref[at, :]] * (channels // LANES), axis=1)
                back = dnorm[at, :]
                got = dout[at, :].astype(F32)
                dsecond = got + norm_back(back, normed, rstd, gain)
                dsecond_ref[at, :] = dsecond
                low = dsecond.astype(BF16)
                low_ref[at, :] = low
                terms = (low.astype(F32), back * normed, back, got)
                return tuple(
                    a + jnp.sum(t.reshape(cols // SUB, SUB, channels), axis=0)
                    for a, t in zip(acc, terms)
                )

            acc = lax.fori_loop(0, images * local_rows, finish, acc, unroll=2)
        sums_ref[...] = jnp.zeros_like(sums_ref)
        for k, a in enumerate(acc):
            sums_ref[pl.ds(k, 1), :] = jnp.sum(a, axis=0, keepdims=True)


def attention_back_kernel(
    dims,
    radii,
    base,
    final,
    meta_ref,
    low,
    norma_ref,
    part_ref,
    w_0,
    w_1,
    query_ref,
    probs_ref,
    value_ref,
    near_ref,
    attended_ref,
    kv_ref,
    *refs,
):
    images, rows, cols, channels = dims
    cells = rows * cols
    if final:
        before_ref, *refs = refs
    dnorma_ref, d_0, d_1, sums_ref, weight, pad_d, value_f, grads, dvalue_f = refs
    dp_block = meta_ref[1]

    for k, blocks in enumerate((w_0, w_1)):
        fetch(blocks, NEAR_LAST, weight.at[k], dp_block)
    pad_d[...] = jnp.zeros_like(pad_d)
    sums_ref[...] = jnp.zeros_like(sums_ref)
    diagonal = head_diagonal()

    def head_step(step):
        attention_back_step(step, (step + base) ^ meta_ref[0])

    def attention_back_step(step, block):
        def first_half(lead):
            at = pl.ds(pl.multiple_of(lead * cells, cells), cells)
            datt = dot(low[at, :], weight[step, :, 3 * LANES :]).astype(BF16)
            query = query_ref[step, at, :]
            probs = probs_ref[step, at, :]
            value = value_ref[step, at, :]
            kept = cell_keep(meta_ref, lead, rows, cols, LANES)
            dkv = jnp.where(diagonal, dot_lt(query, datt) * HEAD_SCALE, 0.0).astype(BF16)
            datt_f = datt.astype(F32)
            dnear = datt_f * query.astype(F32)
            pad_d[lead, :, pl.ds(SUB, cols), :] = dnear.reshape(rows, cols, LANES)
            dquery = (
                dot_rt(datt, kv_ref[step, lead]) * HEAD_SCALE + datt_f * near_ref[step, at, :].astype(F32)
            ).astype(BF16)
            dprobs = dot_rt(value, dkv)
            probs_f = probs.astype(F32)
            inner = jnp.sum(probs_f * dprobs, axis=0, keepdims=True)
            dkey = (probs_f * (dprobs - inner)).astype(BF16)
            grads[at, :LANES] = dquery
            grads[at, LANES : 2 * LANES] = dkey
            dvalue_f[at, :] = dot(probs, dkv)
            value_f[at, :] = jnp.where(kept, value.astype(F32), 0.0)
            sums_ref[step, pl.ds(61, 1), :] += jnp.sum(dquery.astype(F32), axis=0, keepdims=True)
            sums_ref[step, pl.ds(63, 1), :] += jnp.sum(dnear, axis=0, keepdims=True)

        loop(images, first_half)

        def conv_back(radius):
            def conv(lead):
                x = lax.broadcasted_iota(jnp.int32, (SUB, LANES), 0)
                for col in range(0, cols, SUB):
                    out = filtered(
                        pad_d,
                        lead,
                        rows,
                        col,
                        lambda dy, dx: part_ref[block, pl.ds(9 + 7 * (dy + 3) + dx + 3, 1), :],
                        radius,
                        -1,
                    )
                    inside = (x + col) < width(meta_ref, lead)
                    for y in range(rows):
                        at = pl.ds(pl.multiple_of(lead * cells + (y * cols + col), SUB), SUB)
                        kept = inside & (y < height(meta_ref, lead))
                        dvalue_f[at, :] = dvalue_f[at, :] + jnp.where(kept, out[y], 0.0)

            loop(images, conv)

            def own(lead, y, col):
                at = pl.multiple_of(lead * cells + (y * cols + col), SUB)
                return value_f[pl.ds(at, SUB), :]

            for dx in range(-radius, radius + 1):
                acc = tap_products(pad_d, own, images, rows, cols, dx, radius)
                for k, dy in enumerate(range(-radius, radius + 1)):
                    sums_ref[step, pl.ds(9 + 7 * (dy + 3) + dx + 3, 1), :] = jnp.sum(
                        acc[k], axis=0, keepdims=True
                    )

        by_radius(block, radii, conv_back)

        def second_half(lead):
            at = pl.ds(pl.multiple_of(lead * cells, cells), cells)
            dvalue = dvalue_f[at, :].astype(BF16)
            grads[at, 2 * LANES :] = dvalue
            sums_ref[step, pl.ds(62, 1), :] += jnp.sum(dvalue.astype(F32), axis=0, keepdims=True)
            back = dot_rt(grads[at, :], weight[step, :, : 3 * LANES])

            @pl.when(step == 0)
            def _():
                dnorma_ref[at, :] = back + before_ref[at, :] if final else back

            @pl.when(step > 0)
            def _():
                dnorma_ref[at, :] = dnorma_ref[at, :] + back

        loop(images, second_half)
        wide = 3 * LANES
        dwq = dot_lt(norma_ref[...], grads[...])
        dwp = dot_lt(low[...], attended_ref[step])
        for k, out in enumerate((d_0, d_1)):

            @pl.when(step == k)
            def _(k=k, out=out):
                hand_out(out, NEAR_LAST, dwq, pl.ds(0, wide), dp_block)
                hand_out(out, NEAR_LAST, dwp, pl.ds(wide, LANES), dp_block)

    loop(2, head_step)

def input_back_kernel(
    dims,
    local_rows,
    tile_rows,
    meta_ref,
    x_ref,
    normed_ref,
    rstd_ref,
    dnorma_ref,
    dsecond_ref,
    small_ref,
    heads_0,
    heads_1,
    window_ref,
    two_ref,
    dbias_0,
    dbias_1,
    *refs,
):
    images, rows, cols, channels = dims
    cells = rows * cols
    group = rows // local_rows
    outs = refs[:group]
    tiles_ref, pad_d, x_f, sums = refs[group:]
    place = meta_ref[0]
    zeros = jnp.zeros((images, rows, SUB, channels), F32)
    pad_d[:, :, :SUB, :] = zeros
    pad_d[:, :, SUB + cols :, :] = zeros
    gain = small_ref[pl.ds(59, 1), :]

    def norm(r, acc):
        lead = r // rows
        y = r % rows
        at = pl.ds(pl.multiple_of(r * cols, cols), cols)
        normed = normed_ref[at, :]
        rstd = jnp.concatenate([rstd_ref[at, :]] * (channels // LANES), axis=1)
        back = dnorma_ref[at, :]
        dfirst = dsecond_ref[at, :] + norm_back(back, normed, rstd, gain)
        pad_d[lead, y, pl.ds(SUB, cols), :] = dfirst
        x_f[at, :] = x_ref[at, :].astype(F32)
        terms = (dfirst, back * normed, back)
        return tuple(
            a + jnp.sum(t.reshape(cols // SUB, SUB, channels), axis=0)
            for a, t in zip(acc, terms)
        )

    zero = jnp.zeros((SUB, channels), F32)
    acc = lax.fori_loop(0, images * rows, norm, (zero,) * 3, unroll=4)
    for k, a in enumerate(acc):
        sums[pl.ds(58 + k, 1), :] = jnp.sum(a, axis=0, keepdims=True)

    def conv(lead):
        x = lax.broadcasted_iota(jnp.int32, (SUB, LANES), 0)
        for lane in range(0, channels, LANES):
            lanes = pl.ds(lane, LANES)
            for col in range(0, cols, SUB):
                out = filtered(
                    pad_d,
                    lead,
                    rows,
                    col,
                    lambda dy, dx: small_ref[pl.ds(3 * (dy + 1) + dx + 1, 1), lanes],
                    1,
                    -1,
                    lanes,
                )
                inside = (x + col) < width(meta_ref, lead)
                for y in range(rows):
                    own = pad_d[lead, y, pl.ds(SUB + col, SUB), lanes]
                    at = pl.multiple_of(lead * cells + (y * cols + col), SUB)
                    kept = inside & (y < height(meta_ref, lead))
                    x_f[pl.ds(at, SUB), lanes] = jnp.where(kept, own + out[y], 0.0)

    for lane in range(0, channels, LANES):
        lanes = pl.ds(lane, LANES)

        def own(lead, y, col):
            at = pl.multiple_of(lead * cells + (y * cols + col), SUB)
            return x_f[pl.ds(at, SUB), lanes]

        for dx in (-1, 0, 1):
            acc = tap_products(pad_d, own, images, rows, cols, dx, 1, lanes)
            for k, dy in enumerate((-1, 0, 1)):
                sums[pl.ds(3 * (dy + 1) + dx + 1, 1), lanes] = jnp.sum(
                    acc[k], axis=0, keepdims=True
                )
    loop(images, conv)
    for k, out_ref in enumerate(outs):

        def give(r):
            lead = r // local_rows
            y_here = r % local_rows
            y = (place ^ k) * local_rows + y_here
            at = pl.ds(pl.multiple_of((lead * rows + y) * cols, cols), cols)
            out_ref[y_here, lead] = x_f[at, :].astype(BF16)

        loop(images * local_rows, give, 2)

    for mask in range(group):
        heads_ref = (heads_0, heads_1)[mask // 2].at[mask % 2]
        lanes = pl.ds(pl.multiple_of((place ^ mask) * LANES, LANES), LANES)
        sums[pl.ds(9, 49), lanes] = heads_ref[pl.ds(9, 49), :] * window_ref[:, lanes]
        sums[pl.ds(61, 3), lanes] = heads_ref[pl.ds(61, 3), :]
        sums[pl.ds(68 + (place ^ mask), 1), :] = (dbias_0, dbias_1)[mask // 2][mask % 2]
    sums[pl.ds(64, 4), :] = two_ref[pl.ds(0, 4), :]
    tiles_ref[...] = jnp.zeros_like(tiles_ref)
    for d in range(tiles_ref.shape[0]):
        here = min(tile_rows, sums.shape[0] - d * tile_rows)
        for j in range(tiles_ref.shape[1]):
            if here > 0:
                tiles_ref[d, j, pl.ds(0, here), :] = sums[
                    pl.ds(d * tile_rows, here), pl.ds(j * LANES, LANES)
                ]


def join_kernel(meta_ref, *refs):
    *pieces, out_ref = refs
    images = pieces[0].shape[1]
    for k, piece in enumerate(pieces):
        out_ref[:, pl.ds((meta_ref[0] ^ k) * images, images)] = piece[...].astype(out_ref.dtype)


SCALARS = pl.BlockSpec(memory_space=pltpu.SMEM)
CLOSE = pl.BlockSpec(memory_space=pltpu.VMEM)
ENTER_MIB = 24
ATTENTION_MIB = 24
HIDDEN_MIB = 32
BACK_MIB = 24
INPUT_MIB = 24
JOIN_MIB = 16


def shape_of(shape, dtype):
    return jax.ShapeDtypeStruct(shape, dtype)


def call(kernel, name, us, mib, inputs, out_specs, out_shape, scratch):
    return pl.pallas_call(
        kernel,
        in_specs=[spec for _, spec in inputs],
        out_specs=out_specs,
        out_shape=out_shape,
        scratch_shapes=scratch,
        compiler_params=pltpu.CompilerParams(vmem_limit_bytes=mib * 2**20),
        cost_estimate=pl.CostEstimate(flops=us * 10**9, bytes_accessed=us * 2**20, transcendentals=0),
        name=name,
    )(*[array for array, _ in inputs])


def near_by(arrays):
    return [(a, CLOSE) for a in arrays]


def enter(dims, meta, pieces, small):
    images, rows, cols, channels = dims
    flat = (images * rows * cols, channels)
    return call(
        functools.partial(enter_kernel, dims, pieces[0].shape[0]),
        "enter",
        8,
        ENTER_MIB,
        [(meta, SCALARS), *near_by(pieces), (small, CLOSE)],
        [CLOSE] * 5,
        [
            shape_of(flat, BF16),
            shape_of(flat, F32),
            shape_of(flat, BF16),
            shape_of(flat, F32),
            shape_of((flat[0], LANES), F32),
        ],
        [pltpu.VMEM((images, rows, cols + 2 * SUB, channels), F32)],
    )


def attention(dims, radii, base, final, meta, norma, parts, weights, *more):
    images, rows, cols, channels = dims
    cells = images * rows * cols
    flat = (cells, channels)
    kinds = ((cells, LANES),) * 5 + ((images, LANES, LANES),)
    scratch = [
        pltpu.VMEM((2, channels, 4 * LANES), BF16),
        pltpu.VMEM((images, rows, cols + 2 * SUB, LANES), F32),
        pltpu.VMEM((cells, LANES), F32),
    ]
    sums = [shape_of(flat, F32)]
    if final:
        sums += [shape_of(flat, BF16), shape_of(flat, F32), shape_of((cells, LANES), F32)]
    return call(
        functools.partial(attention_kernel, dims, radii, base, final),
        "attention",
        10,
        ATTENTION_MIB,
        [(meta, SCALARS), *near_by([norma, parts]), *near_by(weights), *near_by(more)],
        [CLOSE] * (len(kinds) + len(sums)),
        [*[shape_of((2, *k), BF16) for k in kinds], *sums],
        ([pltpu.VMEM(flat, F32)] if final else []) + scratch,
    )


def hidden_part(dims, base, final, meta, normb, bias, w1, w2, *more):
    images, rows, cols, channels = dims
    cells = images * rows * cols
    groups, _, hidden = bias.shape
    local_rows = rows // groups
    piece = (local_rows, images, cols, channels)
    flat = (cells, channels)
    blocks = w1[0].shape
    if final:
        outs = [
            *[shape_of(piece, BF16) for _ in range(groups)],
            shape_of(flat, F32),
            shape_of(flat, BF16),
            shape_of((SUB, channels), F32),
        ]
    else:
        outs = [shape_of(flat, BF16), shape_of(flat, F32), shape_of(flat, F32)]
    return call(
        functools.partial(hidden_kernel, dims, local_rows, base, final),
        "hidden",
        15,
        HIDDEN_MIB,
        [(meta, SCALARS), *near_by([normb, bias]), *near_by([*w1, *w2]), *near_by(more)],
        [CLOSE] * (3 + len(outs)),
        [
            *[shape_of((*blocks[:2], 2 * hidden), BF16) for _ in range(2)],
            shape_of((2, 1, hidden), F32),
            *outs,
        ],
        ([pltpu.VMEM(flat, F32)] * 2 if final else [])
        + [
            pltpu.VMEM((2, channels, hidden), BF16),
            pltpu.VMEM((2, channels, hidden), BF16),
            pltpu.VMEM((rows * cols, hidden), F32),
            pltpu.VMEM((rows * cols, hidden), F32),
            pltpu.VMEM((cells, hidden), BF16),
            pltpu.VMEM((cells, hidden), BF16),
        ],
    )


def attention_back(dims, radii, base, meta, low, norma, parts, weights, saved, *before):
    images, rows, cols, channels = dims
    cells = images * rows * cols
    flat = (cells, channels)
    blocks = weights[0].shape
    return call(
        functools.partial(attention_back_kernel, dims, radii, base, len(before)),
        "attention_back",
        14,
        BACK_MIB,
        [
            (meta, SCALARS),
            *near_by([low, norma, parts]),
            *near_by(weights),
            *near_by([*saved, *before]),
        ],
        [CLOSE] * 4,
        [
            shape_of(flat, F32),
            *[shape_of(blocks, BF16) for _ in range(2)],
            shape_of((2, 72, LANES), F32),
        ],
        [
            pltpu.VMEM((2, channels, 4 * LANES), BF16),
            pltpu.VMEM((images, rows, cols + 2 * SUB, LANES), F32),
            pltpu.VMEM((cells, LANES), F32),
            pltpu.VMEM((cells, 3 * LANES), BF16),
            pltpu.VMEM((cells, LANES), F32),
        ],
    )


def input_back(dims, groups, shards, meta, *args):
    images, rows, cols, channels = dims
    flat = (images * rows * cols, channels)
    piece = (rows // groups, images, cols, channels)
    tile_rows = -(-72 // shards)
    tiles = (shards, groups, tile_rows, LANES)
    return call(
        functools.partial(input_back_kernel, dims, rows // groups, tile_rows),
        "input_back",
        10,
        INPUT_MIB,
        [(meta, SCALARS), *near_by(args)],
        [CLOSE] * (groups + 1),
        [*[shape_of(piece, BF16) for _ in range(groups)], shape_of(tiles, F32)],
        [
            pltpu.VMEM((images, rows, cols + 2 * SUB, channels), F32),
            pltpu.VMEM(flat, F32),
            pltpu.VMEM((72, channels), F32),
        ],
    )


def join(meta, pieces, dtype):
    local_rows, images, cols, channels = pieces[0].shape
    return call(
        join_kernel,
        "join",
        2,
        JOIN_MIB,
        [(meta, SCALARS), *near_by(pieces)],
        CLOSE,
        shape_of((local_rows, images * len(pieces), cols, channels), dtype),
        [],
    )


def adamw(weight, mean, square, gradient, factor, rate, decay):
    clipped = gradient * factor
    mean_new = BETA_ONE * mean + (1.0 - BETA_ONE) * clipped
    square_new = BETA_TWO * square + (1.0 - BETA_TWO) * clipped * clipped
    mean_hat = mean_new / (1.0 - BETA_ONE**STEP)
    square_hat = square_new / (1.0 - BETA_TWO**STEP)
    weight_new = weight - rate * (mean_hat / (jnp.sqrt(square_hat) + ADAM_EPS) + decay * weight)
    return (weight_new, mean_new, square_new)


def window_rows(channels):
    radius = jnp.repeat(jnp.array([radius_of(h) for h in range(channels // HD)], jnp.int32), HD)
    tap_list = jnp.arange(49, dtype=jnp.int32)
    tap_row = jnp.abs(tap_list // 7 - 3)
    tap_col = jnp.abs(tap_list % 7 - 3)
    inside = (tap_row[:, None] <= radius[None, :]) & (tap_col[:, None] <= radius[None, :])
    return inside.astype(F32)


def on_device(
    patches,
    cotangent,
    grid_shape,
    qkv_weight,
    qkv_mean,
    qkv_square,
    proj_weight,
    proj_mean,
    proj_square,
    expand_weight,
    expand_mean,
    expand_square,
    contract_weight,
    contract_mean,
    contract_square,
    small_params,
    small_mean,
    small_square,
):
    group = lax.axis_size("mp")
    shards = lax.axis_size("dp")
    place = lax.axis_index("mp")
    local_rows, image_count, cols, channels = patches.shape
    images = image_count // group
    rows = local_rows * group
    dims = (images, rows, cols, channels)
    shard_rows = qkv_weight.shape[0]
    head_width = qkv_weight.shape[2]
    hidden = expand_weight.shape[1]
    assert head_width == LANES
    per_block = head_width // HD
    radii = [
        max(radius_of(per_block * g + h) for h in range(per_block)) for g in range(group)
    ]
    grids = lax.dynamic_slice_in_dim(grid_shape, place * images, images, 0)
    dp_block = lax.axis_index("dp") >> finer_bits(shard_rows)
    meta = jnp.concatenate([jnp.stack([place, dp_block]).astype(jnp.int32), grids.reshape(-1)])

    def image_pieces(array):
        pieces = [
            lax.dynamic_slice_in_dim(array, (place ^ k) * images, images, 1).astype(BF16)
            for k in range(group)
        ]
        return swapped(pieces)

    low = finer_bits(shard_rows)

    heads_shard = jnp.concatenate(
        [qkv_weight.astype(BF16).reshape(shard_rows, -1), proj_weight.astype(BF16)], axis=1
    )
    one_shard = expand_weight.astype(BF16)
    two_shard = contract_weight.astype(BF16)

    heads = whole_block(heads_shard)
    heads = doubled(heads, 2, low)
    two = doubled(whole_block(two_shard), 0, low)
    heads = doubled(heads, 1, low)
    one = doubled(after(whole_block(one_shard), heads), 2, low)
    heads = doubled(heads, 0, low)
    heads_all = [heads, flip(heads, "mp", CORE)]
    heads_chip = flip(heads, "mp", CHIP)
    patch_pieces = image_pieces(patches)
    cot_pieces = image_pieces(after(cotangent, patch_pieces[-1]))
    one = doubled(one, 1, low)
    two = doubled(after(two, one), 2, low)

    window = window_rows(channels)
    parts = small_params.at[9:58].multiply(window).reshape(72, group, LANES).transpose(1, 0, 2)
    unit_bias = small_params[68:].reshape(group, 1, hidden)

    x, first, norma, normed_1, rstd_1 = enter(dims, meta, patch_pieces, small_params)
    *saved_0, attn = attention(dims, radii, 0, False, meta, norma, parts, heads_all)
    one = doubled(one, 0, low)
    two = doubled(two, 1, low)
    heads_all += [heads_chip, flip(heads_chip, "mp", CORE)]
    *saved_1, second, normb, normed_2, rstd_2 = attention(
        dims, radii, 2, True, meta, norma, parts, heads_all[2:], attn, first, small_params
    )
    one_all = [one, flip(one, "mp", CORE)]
    two_all = [two, flip(two, "mp", CORE)]
    one_chip, two_chip = flip(one, "mp", CHIP), flip(two, "mp", CHIP)
    dm_0, dm_1, dbias_0, dout, total, dnorm = hidden_part(
        dims, 0, False, meta, normb, unit_bias, one_all, two_all, *cot_pieces
    )
    one_all += [one_chip, flip(one_chip, "mp", CORE)]
    two_all += [two_chip, flip(two_chip, "mp", CORE)]
    dm_2, dm_3, dbias_1, *out_pieces, dsecond, dsecond_low, sums_two = hidden_part(
        dims,
        2,
        True,
        meta,
        normb,
        unit_bias,
        one_all[2:],
        two_all[2:],
        dout,
        total,
        dnorm,
        second,
        normed_2,
        rstd_2,
        small_params,
    )
    out_pieces = swapped(out_pieces)

    def low_added(mine, got):
        return added(mine, got).astype(BF16)

    own = low_added(dm_0, flip(dm_1, "mp", CORE))
    dnorma, da_2, da_3, sums_heads_1 = attention_back(
        dims, radii, 2, meta, after(dsecond_low, own), norma, parts, heads_all[2:], saved_1
    )
    own = halved(own, 0, low).astype(BF16)
    far = low_added(dm_2, flip(dm_3, "mp", CORE))
    heads_far = low_added(da_2, flip(da_3, "mp", CORE))
    dnorma, da_0, da_1, sums_heads_0 = attention_back(
        dims,
        radii,
        0,
        meta,
        after(dsecond_low, own, far, heads_far),
        norma,
        parts,
        heads_all[:2],
        saved_0,
        dnorma,
    )
    heads_own = low_added(da_0, flip(da_1, "mp", CORE))
    heads_own = low_added(heads_own, flip(heads_far, "mp", CHIP))
    own = halved(own, 1, low).astype(BF16)
    far = halved(far, 0, low).astype(BF16)
    *grad_pieces, tiles = input_back(
        dims,
        group,
        shards,
        meta,
        x,
        normed_1,
        rstd_1,
        after(dnorma, heads_own, own, far),
        dsecond,
        small_params,
        sums_heads_0,
        sums_heads_1,
        window,
        sums_two,
        dbias_0,
        dbias_1,
    )
    heads_own = halved(heads_own, 0, low).astype(BF16)
    own = halved(own, 2, low)
    far = halved(far, 1, low).astype(BF16)
    block_out = join(meta, [after(p, tiles) for p in out_pieces], BF16)
    grad_pieces = swapped(grad_pieces)
    heads_own = halved(heads_own, 1, low).astype(BF16)
    far = halved(far, 2, low).astype(BF16)
    heads_own = halved(heads_own, 2, low)
    shard_heads = own_rows(heads_own[0], low)
    shard_hidden = own_rows(added(own, flip(far, "mp", CHIP))[0], low)
    patch_grad = join(meta, grad_pieces, F32)
    shard_expand = shard_hidden[:, :hidden]
    shard_contract = shard_hidden[:, hidden:]
    shard_qkv = shard_heads[:, : 3 * LANES].reshape(-1, 3, LANES)
    shard_proj = shard_heads[:, 3 * LANES :]

    count = group * shards
    both = ("dp", "mp")
    tile_rows = tiles.shape[2]
    tiles = lax.all_to_all(tiles.reshape(count, tile_rows, LANES), both, 0, 0, tiled=True)
    own_small = jnp.sum(tiles, axis=0)
    local_sq = (
        jnp.sum(shard_heads * shard_heads)
        + jnp.sum(shard_hidden * shard_hidden)
        + jnp.sum(own_small * own_small)
    )
    message = jnp.concatenate([own_small, jnp.full((1, LANES), local_sq, F32)], axis=0)
    every = lax.all_to_all(
        jnp.broadcast_to(message, (count, *message.shape)), both, 0, 0, tiled=True
    )
    grad_small = (
        every[:, :tile_rows]
        .reshape(shards, group, tile_rows, LANES)
        .transpose(0, 2, 1, 3)
        .reshape(shards * tile_rows, channels)[:72]
    )
    grad_norm = jnp.sqrt(jnp.sum(every[:, tile_rows, 0]))
    factor = jnp.minimum(1.0, CLIP_NORM / (grad_norm + 1e-06))
    rate_model = RATE_FACTOR * D ** (-0.5)
    rate_hidden = RATE_FACTOR * FF ** (-0.5)
    qkv_new = adamw(qkv_weight, qkv_mean, qkv_square, shard_qkv, factor, rate_model, WEIGHT_DECAY)
    proj_new = adamw(
        proj_weight, proj_mean, proj_square, shard_proj, factor, rate_model, WEIGHT_DECAY
    )
    expand_new = adamw(
        expand_weight, expand_mean, expand_square, shard_expand, factor, rate_model, WEIGHT_DECAY
    )
    contract_new = adamw(
        contract_weight,
        contract_mean,
        contract_square,
        shard_contract,
        factor,
        rate_hidden,
        WEIGHT_DECAY,
    )
    small_new = adamw(small_params, small_mean, small_square, grad_small, factor, SMALL_RATE, 0.0)
    return (
        block_out,
        patch_grad,
        grad_norm,
        *qkv_new,
        *proj_new,
        *expand_new,
        *contract_new,
        *small_new,
    )


def solution(mesh):
    cells = P("mp", "dp", None, None)
    heads = P("dp", None, "mp")
    matrix = P("dp", "mp")
    params = [heads] * 3 + [matrix] * 9 + [P()] * 3
    return jax.shard_map(
        on_device,
        mesh=mesh,
        in_specs=(cells, cells, P("dp", None), *params),
        out_specs=(cells, cells, P(), *params),
        check_vma=False,
    )
```

```python
import functools
import math

import jax
import jax.numpy as jnp
from jax import lax
from jax.experimental import pallas as pl
from jax.experimental.pallas import tpu as pltpu
from jax.sharding import PartitionSpec as P

D = 512
HD = 64
FF = 2048
STEP = 10


NORM_EPS = 1e-06
CLIP_NORM = 1.0
BETA_ONE = 0.9
BETA_TWO = 0.999
ADAM_EPS = 1e-08
WEIGHT_DECAY = 0.05
RATE_FACTOR = 2.0
SMALL_RATE = 0.5
ROOT_HALF = 0.7071067811865476
INV_ROOT_TAU = 0.3989422804014327
HEAD_SCALE = HD ** (-0.5)

LANES = 128
SUB = 8
F32 = jnp.float32
BF16 = jnp.bfloat16


def radius_of(head):
    return 1 if head < 2 else 2 if head < 5 else 3


def log2(size):
    bits = size.bit_length() - 1
    assert 1 << bits == size
    return bits


BLOCK = 64
NEAR_LAST = (2, 1, 0)
CORE, CHIP = 0, 1


def flip(array, axis, bit):
    size = lax.axis_size(axis)
    return lax.ppermute(array, axis, [(i, i ^ (1 << bit)) for i in range(size)])


def bit_of(axis, bit):
    return (lax.axis_index(axis) >> bit) & 1


def finer_bits(shard_rows):
    return log2(BLOCK // shard_rows) if shard_rows < BLOCK else 0


def after(array, *others):
    return lax.optimization_barrier((array, *others))[0]


def tie(*arrays):
    return lax.optimization_barrier(arrays)


def whole_block(shard):
    for bit in range(finer_bits(shard.shape[0])):
        other = flip(shard, "dp", bit)
        upper = bit_of("dp", bit) == 1
        shard = jnp.where(
            upper,
            jnp.concatenate([other, shard], axis=0),
            jnp.concatenate([shard, other], axis=0),
        )
    return shard[None]


def doubled(blocks, bit, low, *before):
    other = flip(blocks, "dp", bit + low)
    return jnp.concatenate([blocks, after(other, *before) if before else other], axis=0)


def dp_masks(order):
    masks = [0]
    for bit in order:
        masks += [m ^ (1 << bit) for m in masks]
    return masks


def added(mine, got):
    return mine.astype(F32) + got.astype(F32)


def low_added(mine, got):
    return added(mine, got).astype(BF16)


def halved(blocks, bit, low, *before):
    half = blocks.shape[0] // 2
    other = flip(blocks[half:], "dp", bit + low)
    return added(blocks[:half], after(other, *before) if before else other)


def own_rows(total, low):
    for bit in reversed(range(low)):
        pair = total.astype(BF16).reshape(2, -1, total.shape[-1])
        mine = lax.dynamic_index_in_dim(pair, bit_of("dp", bit), 0, keepdims=False)
        theirs = lax.dynamic_index_in_dim(pair, 1 - bit_of("dp", bit), 0, keepdims=False)
        total = added(mine, flip(theirs, "dp", bit))
    return total


def dot(a, b):
    return lax.dot_general(a, b, (((1,), (0,)), ((), ())), preferred_element_type=F32)


def dot_rt(a, b):
    return lax.dot_general(a, b, (((1,), (1,)), ((), ())), preferred_element_type=F32)


def dot_lt(a, b):
    return lax.dot_general(a, b, (((0,), (0,)), ((), ())), preferred_element_type=F32)


def row_mean(values):
    return jnp.sum(values, axis=-1, keepdims=True) * (1.0 / values.shape[-1])


def norm_parts(values):
    center = values - row_mean(values)
    rstd = lax.rsqrt(row_mean(center * center) + NORM_EPS)
    return center * rstd, rstd


def norm_back(gradient, normed, rstd, gain_row):
    scaled = gradient * gain_row
    return rstd * (scaled - row_mean(scaled) - normed * row_mean(scaled * normed))


def shifted_rows(src, lead, rows, start, lanes=slice(None)):
    return [src[lead, y, pl.ds(start, SUB), lanes] for y in range(rows)]


def filtered(src, lead, rows, col, taps, radius, sign, lanes=slice(None)):
    acc = [None] * rows
    for dx in range(-radius, radius + 1):
        cells = shifted_rows(src, lead, rows, col + SUB + sign * dx, lanes)
        for dy in range(-radius, radius + 1):
            tap = taps(dy, dx)
            for y in range(rows):
                from_row = y + sign * dy
                if 0 <= from_row < rows:
                    term = tap * cells[from_row]
                    acc[y] = term if acc[y] is None else acc[y] + term
    return acc


def tap_products(src, own, images, rows, cols, dx, radius, lanes=slice(None)):
    def image(lead, acc):
        acc = list(acc)
        for col in range(0, cols, SUB):
            cells = shifted_rows(src, lead, rows, col + SUB - dx, lanes)
            mine = [own(lead, y, col) for y in range(rows)]
            for k, dy in enumerate(range(-radius, radius + 1)):
                total = acc[k]
                for y in range(rows):
                    if 0 <= y - dy < rows:
                        total = total + mine[y] * cells[y - dy]
                acc[k] = total
        return tuple(acc)

    zero = jnp.zeros((SUB, LANES), F32)
    return lax.fori_loop(0, images, image, (zero,) * (2 * radius + 1))


def loop(count, body, unroll=1):
    def step(i, carry):
        body(i)
        return carry

    lax.fori_loop(0, count, step, 0, unroll=unroll)


def slot_of(mask, order):
    return sum(((mask >> bit) & 1) << k for k, bit in enumerate(order))


def fetch(blocks, order, target, dp_block, stride=1, offset=0):
    for slot, mask in enumerate(dp_masks(order)):
        row = pl.multiple_of((dp_block ^ mask) * BLOCK, BLOCK)
        target[pl.ds(row, BLOCK), :] = blocks[slot * stride + offset]


def hand_out(blocks, order, values, columns, dp_block):
    for block in range(values.shape[0] // BLOCK):
        slot = slot_of(dp_block ^ block, order)
        blocks[slot, :, columns] = values[block * BLOCK : (block + 1) * BLOCK].astype(BF16)


def height(meta_ref, lead):
    return meta_ref[2 + 2 * lead]


def width(meta_ref, lead):
    return meta_ref[3 + 2 * lead]


def col_keep(meta_ref, lead, cols, lanes):
    return lax.broadcasted_iota(jnp.int32, (cols, lanes), 0) < width(meta_ref, lead)


def cell_keep(meta_ref, lead, rows, cols, lanes):
    x = lax.broadcasted_iota(jnp.int32, (rows, cols, lanes), 1)
    y = lax.broadcasted_iota(jnp.int32, (rows, cols, lanes), 0)
    kept = (x < width(meta_ref, lead)) & (y < height(meta_ref, lead))
    return kept.reshape(rows * cols, lanes)


def head_diagonal():
    a = lax.broadcasted_iota(jnp.int32, (LANES, LANES), 0) // HD
    b = lax.broadcasted_iota(jnp.int32, (LANES, LANES), 1) // HD
    return a == b


def by_radius(step, radii, run):
    for radius in sorted(set(radii)):
        steps = [k for k, r in enumerate(radii) if r == radius]
        hit = functools.reduce(lambda a, b: a | b, [step == k for k in steps])
        pl.when(hit)(functools.partial(run, radius))


def enter_kernel(
    dims,
    local_rows,
    meta_ref,
    *refs,
):
    images, rows, cols, channels = dims
    cells = rows * cols
    group = rows // local_rows
    pieces = refs[:group]
    small_ref, x_ref, first_ref, norma_ref, normed_ref, rstd_ref, pad_x = refs[group:]
    place = meta_ref[0]
    zeros = jnp.zeros((images, rows, SUB, channels), F32)
    pad_x[:, :, :SUB, :] = zeros
    pad_x[:, :, SUB + cols :, :] = zeros

    for k, piece in enumerate(pieces):

        def mask_row(r):
            lead = r // local_rows
            y_here = r % local_rows
            y = (place ^ k) * local_rows + y_here
            kept = col_keep(meta_ref, lead, cols, channels) & (y < height(meta_ref, lead))
            block = jnp.where(kept, piece[y_here, lead], 0)
            at = pl.ds(pl.multiple_of((lead * rows + y) * cols, cols), cols)
            x_ref[at, :] = block
            pad_x[lead, y, pl.ds(SUB, cols), :] = block.astype(F32)

        loop(images * local_rows, mask_row, 2)

    def conv(lead):
        for lane in range(0, channels, LANES):
            lanes = pl.ds(lane, LANES)
            for col in range(0, cols, SUB):
                out = filtered(
                    pad_x,
                    lead,
                    rows,
                    col,
                    lambda dy, dx: small_ref[pl.ds(3 * (dy + 1) + dx + 1, 1), lanes],
                    1,
                    1,
                    lanes,
                )
                bias = small_ref[pl.ds(58, 1), lanes]
                for y in range(rows):
                    own = pad_x[lead, y, pl.ds(SUB + col, SUB), lanes]
                    at = pl.multiple_of(lead * cells + (y * cols + col), SUB)
                    first_ref[pl.ds(at, SUB), lanes] = own + out[y] + bias

    loop(images, conv)

    def normalize(r):
        at = pl.ds(pl.multiple_of(r * cols, cols), cols)
        normed, rstd = norm_parts(first_ref[at, :])
        normed_ref[at, :] = normed
        rstd_ref[at, :] = jnp.broadcast_to(rstd, (cols, LANES))
        norma_ref[at, :] = (
            normed * small_ref[pl.ds(59, 1), :] + small_ref[pl.ds(60, 1), :]
        ).astype(BF16)

    loop(images * rows, normalize, 4)


def attention_kernel(
    dims,
    radii,
    mask,
    final,
    meta_ref,
    norma_ref,
    part_ref,
    blocks_ref,
    *refs,
):
    images, rows, cols, channels = dims
    cells = rows * cols
    if mask:
        before_ref, *refs = refs
    if final:
        first_ref, small_ref, *refs = refs
    query_ref, probs_ref, value_ref, near_ref, attended_ref, kv_ref, *refs = refs
    if final:
        second_ref, normb_ref, normed_ref, rstd_ref, total, *refs = refs
    else:
        total, *refs = refs
    weight, pad_v, near_f = refs

    fetch(blocks_ref, NEAR_LAST, weight, meta_ref[1])
    pad_v[...] = jnp.zeros_like(pad_v)
    diagonal = head_diagonal()
    block = mask ^ meta_ref[0]

    def project(lead):
        at = pl.ds(pl.multiple_of(lead * cells, cells), cells)
        proj = dot(norma_ref[at, :], weight[:, : 3 * LANES])
        query = (proj[:, :LANES] + part_ref[block, pl.ds(61, 1), :]).astype(BF16)
        value = (proj[:, 2 * LANES :] + part_ref[block, pl.ds(62, 1), :]).astype(BF16)
        kept = cell_keep(meta_ref, lead, rows, cols, LANES)
        key = jnp.where(kept, proj[:, LANES : 2 * LANES], -1e30)
        expo = jnp.exp(key - jnp.max(key, axis=0, keepdims=True))
        probs = (expo / jnp.sum(expo, axis=0, keepdims=True)).astype(BF16)
        query_ref[at, :] = query
        probs_ref[at, :] = probs
        value_ref[at, :] = value
        kv = jnp.where(diagonal, dot_lt(probs, value), 0.0).astype(BF16)
        kv_ref[lead] = kv
        masked = jnp.where(kept, value.astype(F32), 0.0)
        pad_v[lead, :, pl.ds(SUB, cols), :] = masked.reshape(rows, cols, LANES)

    loop(images, project)

    def conv_near(radius):
        def conv(lead):
            for col in range(0, cols, SUB):
                out = filtered(
                    pad_v,
                    lead,
                    rows,
                    col,
                    lambda dy, dx: part_ref[block, pl.ds(9 + 7 * (dy + 3) + dx + 3, 1), :],
                    radius,
                    1,
                )
                bias = part_ref[block, pl.ds(63, 1), :]
                for y in range(rows):
                    at = pl.multiple_of(lead * cells + (y * cols + col), SUB)
                    near_f[pl.ds(at, SUB), :] = out[y] + bias

        loop(images, conv)

    by_radius(block, radii, conv_near)

    def attend(lead):
        at = pl.ds(pl.multiple_of(lead * cells, cells), cells)
        query = query_ref[at, :]
        near = near_f[at, :]
        near_ref[at, :] = near.astype(BF16)
        factored = dot(query, kv_ref[lead]) * HEAD_SCALE
        attended = (factored + query.astype(F32) * near).astype(BF16)
        attended_ref[at, :] = attended
        out = dot_rt(attended, weight[:, 3 * LANES :])

        total[at, :] = out + before_ref[at, :] if mask else out

    loop(images, attend)
    if not final:
        return

    def finish(r):
        at = pl.ds(pl.multiple_of(r * cols, cols), cols)
        second = first_ref[at, :] + total[at, :] + small_ref[pl.ds(64, 1), :]
        second_ref[at, :] = second
        normed, rstd = norm_parts(second)
        normed_ref[at, :] = normed
        rstd_ref[at, :] = jnp.broadcast_to(rstd, (cols, LANES))
        normb_ref[at, :] = (
            normed * small_ref[pl.ds(65, 1), :] + small_ref[pl.ds(66, 1), :]
        ).astype(BF16)

    loop(images * rows, finish, 4)


def gelu_parts(pre):
    cdf = 0.5 * (1.0 + lax.erf(pre * ROOT_HALF))
    return pre * cdf, cdf + pre * (jnp.exp(-0.5 * pre * pre) * INV_ROOT_TAU)


def hidden_kernel(
    dims,
    local_rows,
    mask,
    final,
    meta_ref,
    normb_ref,
    bias_ref,
    blocks_1,
    blocks_2,
    *refs,
):
    images, rows, cols, channels = dims
    cells = rows * cols
    group = rows // local_rows
    if mask:
        dout, total_in, dnorm_in, *refs = refs
    else:
        pieces, refs = refs[:group], refs[group:]
    if final:
        second_ref, normed_ref, rstd_ref, small_ref, *refs = refs
    d_ref, dbias_ref, *refs = refs
    if final:
        outs, refs = refs[:group], refs[group:]
        dsecond_ref, low_ref, sums_ref, total, dnorm, *refs = refs
    else:
        if not mask:
            dout, *refs = refs
        total, dnorm, *refs = refs
    w1, w2, pre, act_grad, hact, dhpre = refs
    hidden = w1.shape[1]
    place, dp_block = meta_ref[0], meta_ref[1]

    fetch(blocks_1, NEAR_LAST, w1, dp_block)
    fetch(blocks_2, NEAR_LAST, w2, dp_block, 2, mask // 2)
    if not mask:
        for k, piece in enumerate(pieces):

            def mask_row(r):
                lead = r // local_rows
                y_here = r % local_rows
                y = (place ^ k) * local_rows + y_here
                kept = col_keep(meta_ref, lead, cols, channels) & (y < height(meta_ref, lead))
                at = pl.ds(pl.multiple_of((lead * rows + y) * cols, cols), cols)
                block = piece[y_here, lead].astype(F32)
                dout[at, :] = jnp.where(kept, block, 0.0).astype(BF16)

            loop(images * local_rows, mask_row, 2)

    dbias_ref[...] = jnp.zeros_like(dbias_ref)

    def tile(lead):
        at = pl.ds(pl.multiple_of(lead * cells, cells), cells)
        pre[...] = dot(normb_ref[at, :], w1[...]) + bias_ref[mask ^ place]
        act_grad[...] = dot(dout[at, :], w2[...])

        def chunk(r, acc):
            here = pl.ds(pl.multiple_of(r * 16, 16), 16)
            there = pl.ds(pl.multiple_of(lead * cells + r * 16, 16), 16)
            act, slope = gelu_parts(pre[here, :])
            hact[there, :] = act.astype(BF16)
            back = (act_grad[here, :] * slope).astype(BF16)
            dhpre[there, :] = back
            return acc + back.astype(F32)

        acc = lax.fori_loop(0, cells // 16, chunk, jnp.zeros((16, hidden), F32))
        dbias_ref[...] = dbias_ref[...] + jnp.sum(acc, axis=0, keepdims=True)
        out = dot_rt(hact[at, :], w2[...])
        back = dot_rt(dhpre[at, :], w1[...])

        total[at, :] = out + total_in[at, :] if mask else out
        dnorm[at, :] = back + dnorm_in[at, :] if mask else back

    loop(images, tile)
    dw1 = dot_lt(normb_ref[...], dhpre[...])
    hand_out(d_ref, NEAR_LAST, dw1, pl.ds(0, hidden), dp_block)
    dw2 = dot_lt(dout[...], hact[...])
    hand_out(d_ref, NEAR_LAST, dw2, pl.ds(hidden, hidden), dp_block)
    if final:
        gain = small_ref[pl.ds(65, 1), :]
        zero = jnp.zeros((SUB, channels), F32)
        acc = (zero,) * 4
        for k, out_ref in enumerate(outs):

            def finish(r, acc):
                lead = r // local_rows
                y_here = r % local_rows
                y = (place ^ k) * local_rows + y_here
                at = pl.ds(pl.multiple_of((lead * rows + y) * cols, cols), cols)
                second = second_ref[at, :]
                out = second + total[at, :] + small_ref[pl.ds(67, 1), :]
                out_ref[y_here, lead] = out.astype(BF16)
                normed = normed_ref[at, :]
                rstd = jnp.concatenate([rstd_ref[at, :]] * (channels // LANES), axis=1)
                back = dnorm[at, :]
                got = dout[at, :].astype(F32)
                dsecond = got + norm_back(back, normed, rstd, gain)
                dsecond_ref[at, :] = dsecond
                low = dsecond.astype(BF16)
                low_ref[at, :] = low
                terms = (low.astype(F32), back * normed, back, got)
                return tuple(
                    a + jnp.sum(t.reshape(cols // SUB, SUB, channels), axis=0)
                    for a, t in zip(acc, terms)
                )

            acc = lax.fori_loop(0, images * local_rows, finish, acc, unroll=2)
        sums_ref[...] = jnp.zeros_like(sums_ref)
        for k, a in enumerate(acc):
            sums_ref[pl.ds(k, 1), :] = jnp.sum(a, axis=0, keepdims=True)


def attention_back_kernel(
    dims,
    radii,
    mask,
    summed,
    meta_ref,
    low,
    norma_ref,
    part_ref,
    blocks_ref,
    query_ref,
    probs_ref,
    value_ref,
    near_ref,
    attended_ref,
    kv_ref,
    *refs,
):
    images, rows, cols, channels = dims
    cells = rows * cols
    if summed:
        before_ref, *refs = refs
    dnorma_ref, d_ref, sums_ref, weight, pad_d, value_f, grads, dvalue_f = refs
    dp_block = meta_ref[1]

    fetch(blocks_ref, NEAR_LAST, weight, dp_block)
    pad_d[...] = jnp.zeros_like(pad_d)
    sums_ref[...] = jnp.zeros_like(sums_ref)
    diagonal = head_diagonal()
    block = mask ^ meta_ref[0]

    def first_half(lead):
        at = pl.ds(pl.multiple_of(lead * cells, cells), cells)
        datt = dot(low[at, :], weight[:, 3 * LANES :]).astype(BF16)
        query = query_ref[at, :]
        probs = probs_ref[at, :]
        value = value_ref[at, :]
        kept = cell_keep(meta_ref, lead, rows, cols, LANES)
        dkv = jnp.where(diagonal, dot_lt(query, datt) * HEAD_SCALE, 0.0).astype(BF16)
        datt_f = datt.astype(F32)
        dnear = datt_f * query.astype(F32)
        pad_d[lead, :, pl.ds(SUB, cols), :] = dnear.reshape(rows, cols, LANES)
        dquery = (
            dot_rt(datt, kv_ref[lead]) * HEAD_SCALE + datt_f * near_ref[at, :].astype(F32)
        ).astype(BF16)
        dprobs = dot_rt(value, dkv)
        probs_f = probs.astype(F32)
        inner = jnp.sum(probs_f * dprobs, axis=0, keepdims=True)
        dkey = (probs_f * (dprobs - inner)).astype(BF16)
        grads[at, :LANES] = dquery
        grads[at, LANES : 2 * LANES] = dkey
        dvalue_f[at, :] = dot(probs, dkv)
        value_f[at, :] = jnp.where(kept, value.astype(F32), 0.0)
        sums_ref[pl.ds(61, 1), :] += jnp.sum(dquery.astype(F32), axis=0, keepdims=True)
        sums_ref[pl.ds(63, 1), :] += jnp.sum(dnear, axis=0, keepdims=True)

    loop(images, first_half)

    def conv_back(radius):
        def conv(lead):
            x = lax.broadcasted_iota(jnp.int32, (SUB, LANES), 0)
            for col in range(0, cols, SUB):
                out = filtered(
                    pad_d,
                    lead,
                    rows,
                    col,
                    lambda dy, dx: part_ref[block, pl.ds(9 + 7 * (dy + 3) + dx + 3, 1), :],
                    radius,
                    -1,
                )
                inside = (x + col) < width(meta_ref, lead)
                for y in range(rows):
                    at = pl.ds(pl.multiple_of(lead * cells + (y * cols + col), SUB), SUB)
                    kept = inside & (y < height(meta_ref, lead))
                    dvalue_f[at, :] = dvalue_f[at, :] + jnp.where(kept, out[y], 0.0)

        loop(images, conv)

        def own(lead, y, col):
            at = pl.multiple_of(lead * cells + (y * cols + col), SUB)
            return value_f[pl.ds(at, SUB), :]

        for dx in range(-radius, radius + 1):
            acc = tap_products(pad_d, own, images, rows, cols, dx, radius)
            for k, dy in enumerate(range(-radius, radius + 1)):
                sums_ref[pl.ds(9 + 7 * (dy + 3) + dx + 3, 1), :] = jnp.sum(
                    acc[k], axis=0, keepdims=True
                )

    by_radius(block, radii, conv_back)

    def second_half(lead):
        at = pl.ds(pl.multiple_of(lead * cells, cells), cells)
        dvalue = dvalue_f[at, :].astype(BF16)
        grads[at, 2 * LANES :] = dvalue
        sums_ref[pl.ds(62, 1), :] += jnp.sum(dvalue.astype(F32), axis=0, keepdims=True)
        back = dot_rt(grads[at, :], weight[:, : 3 * LANES])

        dnorma_ref[at, :] = back + before_ref[at, :] if summed else back

    loop(images, second_half)
    wide = 3 * LANES
    dwq = dot_lt(norma_ref[...], grads[...])
    hand_out(d_ref, NEAR_LAST, dwq, pl.ds(0, wide), dp_block)
    dwp = dot_lt(low[...], attended_ref[...])
    hand_out(d_ref, NEAR_LAST, dwp, pl.ds(wide, LANES), dp_block)


def input_back_kernel(
    dims,
    local_rows,
    tile_rows,
    meta_ref,
    x_ref,
    normed_ref,
    rstd_ref,
    dnorma_ref,
    dsecond_ref,
    small_ref,
    window_ref,
    two_ref,
    *refs,
):
    images, rows, cols, channels = dims
    cells = rows * cols
    group = rows // local_rows
    heads_refs, dbias_refs, refs = refs[:group], refs[group : 2 * group], refs[2 * group :]
    outs, (tiles_ref, pad_d, x_f, sums) = refs[:group], refs[group:]
    place = meta_ref[0]
    zeros = jnp.zeros((images, rows, SUB, channels), F32)
    pad_d[:, :, :SUB, :] = zeros
    pad_d[:, :, SUB + cols :, :] = zeros
    gain = small_ref[pl.ds(59, 1), :]

    def norm(r, acc):
        lead = r // rows
        y = r % rows
        at = pl.ds(pl.multiple_of(r * cols, cols), cols)
        normed = normed_ref[at, :]
        rstd = jnp.concatenate([rstd_ref[at, :]] * (channels // LANES), axis=1)
        back = dnorma_ref[at, :]
        dfirst = dsecond_ref[at, :] + norm_back(back, normed, rstd, gain)
        pad_d[lead, y, pl.ds(SUB, cols), :] = dfirst
        x_f[at, :] = x_ref[at, :].astype(F32)
        terms = (dfirst, back * normed, back)
        return tuple(
            a + jnp.sum(t.reshape(cols // SUB, SUB, channels), axis=0)
            for a, t in zip(acc, terms)
        )

    zero = jnp.zeros((SUB, channels), F32)
    acc = lax.fori_loop(0, images * rows, norm, (zero,) * 3, unroll=4)
    for k, a in enumerate(acc):
        sums[pl.ds(58 + k, 1), :] = jnp.sum(a, axis=0, keepdims=True)

    def conv(lead):
        x = lax.broadcasted_iota(jnp.int32, (SUB, LANES), 0)
        for lane in range(0, channels, LANES):
            lanes = pl.ds(lane, LANES)
            for col in range(0, cols, SUB):
                out = filtered(
                    pad_d,
                    lead,
                    rows,
                    col,
                    lambda dy, dx: small_ref[pl.ds(3 * (dy + 1) + dx + 1, 1), lanes],
                    1,
                    -1,
                    lanes,
                )
                inside = (x + col) < width(meta_ref, lead)
                for y in range(rows):
                    own = pad_d[lead, y, pl.ds(SUB + col, SUB), lanes]
                    at = pl.multiple_of(lead * cells + (y * cols + col), SUB)
                    kept = inside & (y < height(meta_ref, lead))
                    x_f[pl.ds(at, SUB), lanes] = jnp.where(kept, own + out[y], 0.0)

    for lane in range(0, channels, LANES):
        lanes = pl.ds(lane, LANES)

        def own(lead, y, col):
            at = pl.multiple_of(lead * cells + (y * cols + col), SUB)
            return x_f[pl.ds(at, SUB), lanes]

        for dx in (-1, 0, 1):
            acc = tap_products(pad_d, own, images, rows, cols, dx, 1, lanes)
            for k, dy in enumerate((-1, 0, 1)):
                sums[pl.ds(3 * (dy + 1) + dx + 1, 1), lanes] = jnp.sum(
                    acc[k], axis=0, keepdims=True
                )
    loop(images, conv)
    for k, out_ref in enumerate(outs):

        def give(r):
            lead = r // local_rows
            y_here = r % local_rows
            y = (place ^ k) * local_rows + y_here
            at = pl.ds(pl.multiple_of((lead * rows + y) * cols, cols), cols)
            out_ref[y_here, lead] = x_f[at, :].astype(BF16)

        loop(images * local_rows, give, 2)

    for mask in range(group):
        heads_ref = heads_refs[mask]
        lanes = pl.ds(pl.multiple_of((place ^ mask) * LANES, LANES), LANES)
        sums[pl.ds(9, 49), lanes] = heads_ref[pl.ds(9, 49), :] * window_ref[:, lanes]
        sums[pl.ds(61, 3), lanes] = heads_ref[pl.ds(61, 3), :]
        sums[pl.ds(68 + (place ^ mask), 1), :] = dbias_refs[mask][...]
    sums[pl.ds(64, 4), :] = two_ref[pl.ds(0, 4), :]
    tiles_ref[...] = jnp.zeros_like(tiles_ref)
    for d in range(tiles_ref.shape[0]):
        here = min(tile_rows, sums.shape[0] - d * tile_rows)
        for j in range(tiles_ref.shape[1]):
            if here > 0:
                tiles_ref[d, j, pl.ds(0, here), :] = sums[
                    pl.ds(d * tile_rows, here), pl.ds(j * LANES, LANES)
                ]


def join_kernel(meta_ref, *refs):
    *pieces, out_ref = refs
    images = pieces[0].shape[1]
    for k, piece in enumerate(pieces):
        out_ref[:, pl.ds((meta_ref[0] ^ k) * images, images)] = piece[...].astype(out_ref.dtype)


SCALARS = pl.BlockSpec(memory_space=pltpu.SMEM)
CLOSE = pl.BlockSpec(memory_space=pltpu.VMEM)
ENTER_MIB = 8
ATTENTION_MIB = 10
HIDDEN_MIB = 18
BACK_MIB = 10
INPUT_MIB = 10
JOIN_MIB = 4


def shape_of(shape, dtype):
    return jax.ShapeDtypeStruct(shape, dtype)


def call(kernel, name, us, mib, inputs, out_specs, out_shape, scratch):
    return pl.pallas_call(
        kernel,
        in_specs=[spec for _, spec in inputs],
        out_specs=out_specs,
        out_shape=out_shape,
        scratch_shapes=scratch,
        compiler_params=pltpu.CompilerParams(vmem_limit_bytes=mib * 2**20),
        cost_estimate=pl.CostEstimate(flops=us * 10**9, bytes_accessed=us * 2**20, transcendentals=0),
        name=name,
    )(*[array for array, _ in inputs])


def near_by(arrays):
    return [(a, CLOSE) for a in arrays]


def enter(dims, meta, pieces, small):
    images, rows, cols, channels = dims
    flat = (images * rows * cols, channels)
    return call(
        functools.partial(enter_kernel, dims, pieces[0].shape[0]),
        "enter",
        8,
        ENTER_MIB,
        [(meta, SCALARS), *near_by(pieces), (small, CLOSE)],
        [CLOSE] * 5,
        [
            shape_of(flat, BF16),
            shape_of(flat, F32),
            shape_of(flat, BF16),
            shape_of(flat, F32),
            shape_of((flat[0], LANES), F32),
        ],
        [pltpu.VMEM((images, rows, cols + 2 * SUB, channels), F32)],
    )


def attention(dims, radii, mask, meta, norma, parts, blocks, *more):
    images, rows, cols, channels = dims
    cells = images * rows * cols
    flat = (cells, channels)
    final = len(more) > 1
    kinds = ((cells, LANES),) * 5 + ((images, LANES, LANES),)
    sums = [shape_of(flat, F32)]
    if final:
        sums += [shape_of(flat, BF16), shape_of(flat, F32), shape_of((cells, LANES), F32)]
    return call(
        functools.partial(attention_kernel, dims, radii, mask, final),
        "attention",
        5,
        ATTENTION_MIB,
        [(meta, SCALARS), *near_by([norma, parts, blocks, *more])],
        [CLOSE] * (len(kinds) + len(sums)),
        [*[shape_of(k, BF16) for k in kinds], *sums],
        ([pltpu.VMEM(flat, F32)] if final else [])
        + [
            pltpu.VMEM((channels, 4 * LANES), BF16),
            pltpu.VMEM((images, rows, cols + 2 * SUB, LANES), F32),
            pltpu.VMEM((cells, LANES), F32),
        ],
    )


def hidden_part(dims, mask, final, meta, normb, bias, blocks_1, blocks_2, *more):
    images, rows, cols, channels = dims
    cells = images * rows * cols
    groups, _, hidden = bias.shape
    local_rows = rows // groups
    piece = (local_rows, images, cols, channels)
    flat = (cells, channels)
    if final:
        outs = [
            *[shape_of(piece, BF16) for _ in range(groups)],
            shape_of(flat, F32),
            shape_of(flat, BF16),
            shape_of((SUB, channels), F32),
        ]
    else:
        outs = [shape_of(flat, F32), shape_of(flat, F32)]
        outs = outs if mask else [shape_of(flat, BF16), *outs]
    return call(
        functools.partial(hidden_kernel, dims, local_rows, mask, final),
        "hidden",
        8,
        HIDDEN_MIB,
        [(meta, SCALARS), *near_by([normb, bias, blocks_1, blocks_2, *more])],
        [CLOSE] * (2 + len(outs)),
        [
            shape_of((*blocks_1.shape[:2], 2 * hidden), BF16),
            shape_of((1, hidden), F32),
            *outs,
        ],
        ([pltpu.VMEM(flat, F32)] * 2 if final else [])
        + [
            pltpu.VMEM((channels, hidden), BF16),
            pltpu.VMEM((channels, hidden), BF16),
            pltpu.VMEM((rows * cols, hidden), F32),
            pltpu.VMEM((rows * cols, hidden), F32),
            pltpu.VMEM((cells, hidden), BF16),
            pltpu.VMEM((cells, hidden), BF16),
        ],
    )


def attention_back(dims, radii, mask, meta, low, norma, parts, blocks, saved, *before):
    images, rows, cols, channels = dims
    cells = images * rows * cols
    flat = (cells, channels)
    return call(
        functools.partial(attention_back_kernel, dims, radii, mask, len(before)),
        "attention_back",
        7,
        BACK_MIB,
        [(meta, SCALARS), *near_by([low, norma, parts, blocks, *saved, *before])],
        [CLOSE] * 3,
        [
            shape_of(flat, F32),
            shape_of(blocks.shape, BF16),
            shape_of((72, LANES), F32),
        ],
        [
            pltpu.VMEM((channels, 4 * LANES), BF16),
            pltpu.VMEM((images, rows, cols + 2 * SUB, LANES), F32),
            pltpu.VMEM((cells, LANES), F32),
            pltpu.VMEM((cells, 3 * LANES), BF16),
            pltpu.VMEM((cells, LANES), F32),
        ],
    )


def input_back(dims, groups, shards, meta, *args):
    images, rows, cols, channels = dims
    flat = (images * rows * cols, channels)
    piece = (rows // groups, images, cols, channels)
    tile_rows = -(-72 // shards)
    tiles = (shards, groups, tile_rows, LANES)
    return call(
        functools.partial(input_back_kernel, dims, rows // groups, tile_rows),
        "input_back",
        10,
        INPUT_MIB,
        [(meta, SCALARS), *near_by(args)],
        [CLOSE] * (groups + 1),
        [*[shape_of(piece, BF16) for _ in range(groups)], shape_of(tiles, F32)],
        [
            pltpu.VMEM((images, rows, cols + 2 * SUB, channels), F32),
            pltpu.VMEM(flat, F32),
            pltpu.VMEM((72, channels), F32),
        ],
    )


def join(meta, pieces, dtype):
    local_rows, images, cols, channels = pieces[0].shape
    return call(
        join_kernel,
        "join",
        2,
        JOIN_MIB,
        [(meta, SCALARS), *near_by(pieces)],
        CLOSE,
        shape_of((local_rows, images * len(pieces), cols, channels), dtype),
        [],
    )


def adamw(weight, mean, square, gradient, factor, rate, decay):
    clipped = gradient * factor
    mean_new = BETA_ONE * mean + (1.0 - BETA_ONE) * clipped
    square_new = BETA_TWO * square + (1.0 - BETA_TWO) * clipped * clipped
    mean_hat = mean_new / (1.0 - BETA_ONE**STEP)
    square_hat = square_new / (1.0 - BETA_TWO**STEP)
    weight_new = weight - rate * (mean_hat / (jnp.sqrt(square_hat) + ADAM_EPS) + decay * weight)
    return (weight_new, mean_new, square_new)


def window_rows(channels):
    radius = jnp.repeat(jnp.array([radius_of(h) for h in range(channels // HD)], jnp.int32), HD)
    tap_list = jnp.arange(49, dtype=jnp.int32)
    tap_row = jnp.abs(tap_list // 7 - 3)
    tap_col = jnp.abs(tap_list % 7 - 3)
    inside = (tap_row[:, None] <= radius[None, :]) & (tap_col[:, None] <= radius[None, :])
    return inside.astype(F32)


def on_device(
    patches,
    cotangent,
    grid_shape,
    qkv_weight,
    qkv_mean,
    qkv_square,
    proj_weight,
    proj_mean,
    proj_square,
    expand_weight,
    expand_mean,
    expand_square,
    contract_weight,
    contract_mean,
    contract_square,
    small_params,
    small_mean,
    small_square,
):
    group = lax.axis_size("mp")
    shards = lax.axis_size("dp")
    place = lax.axis_index("mp")
    local_rows, image_count, cols, channels = patches.shape
    images = image_count // group
    rows = local_rows * group
    dims = (images, rows, cols, channels)
    shard_rows = qkv_weight.shape[0]
    head_width = qkv_weight.shape[2]
    hidden = expand_weight.shape[1]
    assert head_width == LANES
    per_block = head_width // HD
    radii = [
        max(radius_of(per_block * g + h) for h in range(per_block)) for g in range(group)
    ]
    grids = lax.dynamic_slice_in_dim(grid_shape, place * images, images, 0)
    dp_block = lax.axis_index("dp") >> finer_bits(shard_rows)
    meta = jnp.concatenate([jnp.stack([place, dp_block]).astype(jnp.int32), grids.reshape(-1)])

    def image_pieces(array):
        return [
            lax.dynamic_slice_in_dim(array, (place ^ k) * images, images, 1).astype(BF16)
            for k in range(group)
        ]

    def swapped(near, *far):
        from_far = flip(jnp.stack(far), "mp", CHIP)
        return [flip(near, "mp", CORE), from_far[0], flip(from_far[1], "mp", CORE)]

    low = finer_bits(shard_rows)

    heads_shard = jnp.concatenate(
        [qkv_weight.astype(BF16).reshape(shard_rows, -1), proj_weight.astype(BF16)], axis=1
    )
    one_shard = expand_weight.astype(BF16)
    two_shard = contract_weight.astype(BF16)

    patch_own, *patch_pieces = image_pieces(patches)
    patch_pieces = [patch_own, *swapped(*patch_pieces)]
    heads = doubled(whole_block(heads_shard), 2, low)
    two = whole_block(two_shard)
    two = jnp.concatenate([two, flip(two, "mp", CHIP)], axis=0)
    one = doubled(after(whole_block(one_shard), heads), 2, low)
    heads = doubled(heads, 1, low)
    two = after(two, heads)

    window = window_rows(channels)
    parts = small_params.at[9:58].multiply(window).reshape(72, group, LANES).transpose(1, 0, 2)
    unit_bias = small_params[68:].reshape(group, 1, hidden)

    x, first, norma, normed_1, rstd_1 = enter(dims, meta, patch_pieces, small_params)
    heads = doubled(heads, 0, low, norma)
    one = doubled(one, 1, low, norma)
    two = doubled(two, 2, low, norma)
    saved, weights = [None] * group, [heads] + [None] * (group - 1)

    *saved[0], attn = attention(dims, radii, 0, meta, norma, parts, heads)
    weights[1] = after(flip(heads, "mp", CORE), attn)
    heads_chip = flip(heads, "mp", CHIP)
    cot_own, cot_near, *cot_far = image_pieces(after(cotangent, patch_pieces[2]))
    cot_far = after(flip(jnp.stack(cot_far), "mp", CHIP), attn)
    cot_pieces = [cot_own, flip(cot_near, "mp", CORE), cot_far[0], flip(cot_far[1], "mp", CORE)]
    *saved[1], attn = attention(dims, radii, 1, meta, norma, parts, weights[1], attn)
    weights[2] = after(heads_chip, attn)
    one = doubled(one, 0, low, attn)
    two = doubled(two, 1, low, attn)
    *saved[2], attn = attention(dims, radii, 2, meta, norma, parts, weights[2], attn)
    weights[3] = after(flip(weights[2], "mp", CORE), attn)
    *saved[3], second, normb, normed_2, rstd_2 = attention(
        dims, radii, 3, meta, norma, parts, weights[3], attn, first, small_params
    )
    two = doubled(two, 0, low, normb)

    grads, dbias = [None] * group, [None] * group
    grads[0], dbias[0], dout, total, dnorm = hidden_part(
        dims, 0, False, meta, normb, unit_bias, one, two, *cot_pieces
    )
    one_near, two_near = after(flip(one, "mp", CORE), dnorm), after(flip(two, "mp", CORE), dnorm)
    one_chip = flip(one, "mp", CHIP)
    grads[1], dbias[1], total, dnorm = hidden_part(
        dims, 1, False, meta, normb, unit_bias, one_near, two_near, dout, total, dnorm
    )
    one_chip = after(one_chip, dnorm)
    grads[2], dbias[2], total, dnorm = hidden_part(
        dims, 2, False, meta, normb, unit_bias, one_chip, two, dout, total, dnorm
    )
    one_chip = after(flip(one_chip, "mp", CORE), dnorm)
    own = low_added(grads[0], flip(grads[1], "mp", CORE))
    dnorm, own = tie(dnorm, own)
    grads[3], dbias[3], *outs, dsecond, dsecond_low, sums_two = hidden_part(
        dims,
        3,
        True,
        meta,
        normb,
        unit_bias,
        one_chip,
        two_near,
        dout,
        total,
        dnorm,
        second,
        normed_2,
        rstd_2,
        small_params,
    )

    heads_grads, heads_sums = [None] * group, [None] * group

    def back(mask, low_rows, *before):
        dnorma, heads_grads[mask], heads_sums[mask] = attention_back(
            dims, radii, mask, meta, low_rows, norma, parts, weights[mask], saved[mask], *before
        )
        return dnorma

    def part_way(blocks, bit, first, last):
        half = blocks.shape[0] // 2
        other = flip(blocks[half + first : half + last], "dp", bit + low)
        return low_added(blocks[first:last], other)

    own_1 = part_way(own, 0, 2, 4)
    low_rows, own, own_1, sent, out_3 = tie(dsecond_low, own, own_1, grads[3], outs[3])
    dnorma = back(3, low_rows)

    own_0 = part_way(own, 0, 0, 2)
    far = low_added(grads[2], flip(sent, "mp", CORE))
    out_3 = flip(out_3, "mp", CHIP)
    low_rows, dnorma, own_0, own_1, far, out_3, sent = tie(
        low_rows, dnorma, own_0, own_1, far, out_3, heads_grads[3]
    )
    dnorma = back(2, low_rows, dnorma)

    own = low_added(own_0, flip(own_1, "dp", 1 + low))
    far_1 = part_way(far, 0, 2, 4)
    heads_far = low_added(heads_grads[2], flip(sent, "mp", CORE))
    low_rows, dnorma, own, far, far_1, heads_far, out_3 = tie(
        low_rows, dnorma, own, far, far_1, heads_far, out_3
    )
    dnorma = back(1, low_rows, dnorma)

    own = added(own[:1], flip(own[1:], "dp", 2 + low))
    far_0 = part_way(far, 0, 0, 2)
    half = heads_far.shape[0] // 2
    heads_far_0 = flip(heads_far[:half], "mp", CHIP)
    out_3 = flip(out_3, "mp", CORE)
    low_rows, dnorma, own, far_0, far_1, heads_far, heads_far_0, out_3, sent, out_1 = tie(
        low_rows,
        dnorma,
        own,
        far_0,
        far_1,
        heads_far,
        heads_far_0,
        out_3,
        heads_grads[1],
        outs[1],
    )
    dnorma = back(0, low_rows, dnorma)

    far = low_added(far_0, flip(far_1, "dp", 1 + low))
    heads_far_1 = flip(heads_far[half:], "mp", CHIP)
    heads_near = flip(sent, "mp", CORE)
    out_1 = flip(out_1, "mp", CORE)
    heads_0 = low_added(low_added(heads_grads[0][:half], heads_near[:half]), heads_far_0)
    heads_1 = low_added(low_added(heads_grads[0][half:], heads_near[half:]), heads_far_1)
    dnorma, far, heads_0, heads_1, out_1, out_2 = tie(
        dnorma, far, heads_0, heads_1, out_1, outs[2]
    )
    *grad_pieces, tiles = input_back(
        dims,
        group,
        shards,
        meta,
        x,
        normed_1,
        rstd_1,
        dnorma,
        dsecond,
        small_params,
        window,
        sums_two,
        *heads_sums,
        *dbias,
    )
    far = low_added(far[:1], flip(far[1:], "dp", 2 + low))
    heads_own = low_added(heads_0, flip(heads_1, "dp", 0 + low))
    out_2 = flip(out_2, "mp", CHIP)
    grad_0, grad_1, grad_2, grad_3, tiles, far, heads_own, out_2 = tie(
        *grad_pieces, tiles, far, heads_own, out_2
    )

    heads_own = halved(heads_own, 1, low).astype(BF16)
    far = flip(far, "mp", CHIP)
    grad_pieces = [grad_0, *swapped(grad_1, grad_2, grad_3)]
    heads_own = halved(heads_own, 2, low)
    block_out = join(meta, [outs[0], out_1, out_2, out_3], BF16)
    shard_heads = own_rows(heads_own[0], low)
    shard_hidden = own_rows(added(own, far)[0], low)
    patch_grad = join(meta, grad_pieces, F32)
    shard_expand = shard_hidden[:, :hidden]
    shard_contract = shard_hidden[:, hidden:]
    shard_qkv = shard_heads[:, : 3 * LANES].reshape(-1, 3, LANES)
    shard_proj = shard_heads[:, 3 * LANES :]

    count = group * shards
    both = ("dp", "mp")
    tile_rows = tiles.shape[2]
    tiles = lax.all_to_all(tiles.reshape(count, tile_rows, LANES), both, 0, 0, tiled=True)
    own_small = jnp.sum(tiles, axis=0)
    local_sq = (
        jnp.sum(shard_heads * shard_heads)
        + jnp.sum(shard_hidden * shard_hidden)
        + jnp.sum(own_small * own_small)
    )
    message = jnp.concatenate([own_small, jnp.full((1, LANES), local_sq, F32)], axis=0)
    every = lax.all_to_all(
        jnp.broadcast_to(message, (count, *message.shape)), both, 0, 0, tiled=True
    )
    grad_small = (
        every[:, :tile_rows]
        .reshape(shards, group, tile_rows, LANES)
        .transpose(0, 2, 1, 3)
        .reshape(shards * tile_rows, channels)[:72]
    )
    grad_norm = jnp.sqrt(jnp.sum(every[:, tile_rows, 0]))
    factor = jnp.minimum(1.0, CLIP_NORM / (grad_norm + 1e-06))
    rate_model = RATE_FACTOR * D ** (-0.5)
    rate_hidden = RATE_FACTOR * FF ** (-0.5)
    qkv_new = adamw(qkv_weight, qkv_mean, qkv_square, shard_qkv, factor, rate_model, WEIGHT_DECAY)
    proj_new = adamw(
        proj_weight, proj_mean, proj_square, shard_proj, factor, rate_model, WEIGHT_DECAY
    )
    expand_new = adamw(
        expand_weight, expand_mean, expand_square, shard_expand, factor, rate_model, WEIGHT_DECAY
    )
    contract_new = adamw(
        contract_weight,
        contract_mean,
        contract_square,
        shard_contract,
        factor,
        rate_hidden,
        WEIGHT_DECAY,
    )
    small_new = adamw(small_params, small_mean, small_square, grad_small, factor, SMALL_RATE, 0.0)
    return (
        block_out,
        patch_grad,
        grad_norm,
        *qkv_new,
        *proj_new,
        *expand_new,
        *contract_new,
        *small_new,
    )


def solution(mesh):
    cells = P("mp", "dp", None, None)
    heads = P("dp", None, "mp")
    matrix = P("dp", "mp")
    params = [heads] * 3 + [matrix] * 9 + [P()] * 3
    return jax.shard_map(
        on_device,
        mesh=mesh,
        in_specs=(cells, cells, P("dp", None), *params),
        out_specs=(cells, cells, P(), *params),
        check_vma=False,
    )
```

```python
import functools
import math

import jax
import jax.numpy as jnp
from jax import lax
from jax.experimental import pallas as pl
from jax.experimental.pallas import tpu as pltpu
from jax.sharding import PartitionSpec as P

D = 512
HD = 64
FF = 2048
STEP = 10


NORM_EPS = 1e-06
CLIP_NORM = 1.0
BETA_ONE = 0.9
BETA_TWO = 0.999
ADAM_EPS = 1e-08
WEIGHT_DECAY = 0.05
RATE_FACTOR = 2.0
SMALL_RATE = 0.5
ROOT_HALF = 0.7071067811865476
INV_ROOT_TAU = 0.3989422804014327
HEAD_SCALE = HD ** (-0.5)

LANES = 128
SUB = 8
F32 = jnp.float32
BF16 = jnp.bfloat16


def radius_of(head):
    return 1 if head < 2 else 2 if head < 5 else 3


def log2(size):
    bits = size.bit_length() - 1
    assert 1 << bits == size
    return bits


BLOCK = 64
NEAR_LAST = (2, 1, 0)
CORE, CHIP = 0, 1


def flip(array, axis, bit):
    size = lax.axis_size(axis)
    return lax.ppermute(array, axis, [(i, i ^ (1 << bit)) for i in range(size)])


def bit_of(axis, bit):
    return (lax.axis_index(axis) >> bit) & 1


def finer_bits(shard_rows):
    return log2(BLOCK // shard_rows) if shard_rows < BLOCK else 0


def after(array, *others):
    return lax.optimization_barrier((array, *others))[0]


def tie(*arrays):
    return lax.optimization_barrier(arrays)


def whole_block(shard):
    for bit in range(finer_bits(shard.shape[0])):
        other = flip(shard, "dp", bit)
        upper = bit_of("dp", bit) == 1
        shard = jnp.where(
            upper,
            jnp.concatenate([other, shard], axis=0),
            jnp.concatenate([shard, other], axis=0),
        )
    return shard[None]


def doubled(blocks, bit, low, *before):
    other = flip(blocks, "dp", bit + low)
    return jnp.concatenate([blocks, after(other, *before) if before else other], axis=0)


def dp_masks(order):
    masks = [0]
    for bit in order:
        masks += [m ^ (1 << bit) for m in masks]
    return masks


def added(mine, got):
    return mine.astype(F32) + got.astype(F32)


def low_added(mine, got):
    return added(mine, got).astype(BF16)


def halved(blocks, bit, low, *before):
    half = blocks.shape[0] // 2
    other = flip(blocks[half:], "dp", bit + low)
    return added(blocks[:half], after(other, *before) if before else other)


def own_rows(total, low):
    for bit in reversed(range(low)):
        pair = total.astype(BF16).reshape(2, -1, total.shape[-1])
        mine = lax.dynamic_index_in_dim(pair, bit_of("dp", bit), 0, keepdims=False)
        theirs = lax.dynamic_index_in_dim(pair, 1 - bit_of("dp", bit), 0, keepdims=False)
        total = added(mine, flip(theirs, "dp", bit))
    return total


def dot(a, b):
    return lax.dot_general(a, b, (((1,), (0,)), ((), ())), preferred_element_type=F32)


def dot_rt(a, b):
    return lax.dot_general(a, b, (((1,), (1,)), ((), ())), preferred_element_type=F32)


def dot_lt(a, b):
    return lax.dot_general(a, b, (((0,), (0,)), ((), ())), preferred_element_type=F32)


def row_mean(values):
    return jnp.sum(values, axis=-1, keepdims=True) * (1.0 / values.shape[-1])


def norm_parts(values):
    center = values - row_mean(values)
    rstd = lax.rsqrt(row_mean(center * center) + NORM_EPS)
    return center * rstd, rstd


def norm_back(gradient, normed, rstd, gain_row):
    scaled = gradient * gain_row
    return rstd * (scaled - row_mean(scaled) - normed * row_mean(scaled * normed))


def shifted_rows(src, lead, rows, start, lanes=slice(None)):
    return [src[lead, y, pl.ds(start, SUB), lanes] for y in range(rows)]


def filtered(src, lead, rows, col, taps, radius, sign, lanes=slice(None)):
    acc = [None] * rows
    for dx in range(-radius, radius + 1):
        cells = shifted_rows(src, lead, rows, col + SUB + sign * dx, lanes)
        for dy in range(-radius, radius + 1):
            tap = taps(dy, dx)
            for y in range(rows):
                from_row = y + sign * dy
                if 0 <= from_row < rows:
                    term = tap * cells[from_row]
                    acc[y] = term if acc[y] is None else acc[y] + term
    return acc


def tap_products(src, own, images, rows, cols, dx, radius, lanes=slice(None)):
    def image(lead, acc):
        acc = list(acc)
        for col in range(0, cols, SUB):
            cells = shifted_rows(src, lead, rows, col + SUB - dx, lanes)
            mine = [own(lead, y, col) for y in range(rows)]
            for k, dy in enumerate(range(-radius, radius + 1)):
                total = acc[k]
                for y in range(rows):
                    if 0 <= y - dy < rows:
                        total = total + mine[y] * cells[y - dy]
                acc[k] = total
        return tuple(acc)

    zero = jnp.zeros((SUB, LANES), F32)
    return lax.fori_loop(0, images, image, (zero,) * (2 * radius + 1))


def each(count, body):
    for i in range(count):
        body(i)


def loop(count, body, unroll=1):
    def step(i, carry):
        body(i)
        return carry

    lax.fori_loop(0, count, step, 0, unroll=unroll)


def slot_of(mask, order):
    return sum(((mask >> bit) & 1) << k for k, bit in enumerate(order))


def fetch(blocks, order, target, dp_block, stride=1, offset=0):
    for slot, mask in enumerate(dp_masks(order)):
        row = pl.multiple_of((dp_block ^ mask) * BLOCK, BLOCK)
        target[pl.ds(row, BLOCK), :] = blocks[slot * stride + offset]


def hand_out(blocks, order, values, columns, dp_block):
    for block in range(values.shape[0] // BLOCK):
        slot = slot_of(dp_block ^ block, order)
        blocks[slot, :, columns] = values[block * BLOCK : (block + 1) * BLOCK].astype(BF16)


def place_of(meta_ref):
    return meta_ref[0]


def height(meta_ref, lead):
    return meta_ref[2 + 2 * lead]


def width(meta_ref, lead):
    return meta_ref[3 + 2 * lead]


def col_keep(meta_ref, lead, cols, lanes):
    return lax.broadcasted_iota(jnp.int32, (cols, lanes), 0) < width(meta_ref, lead)


def cell_keep(meta_ref, lead, rows, cols, lanes):
    x = lax.broadcasted_iota(jnp.int32, (rows, cols, lanes), 1)
    y = lax.broadcasted_iota(jnp.int32, (rows, cols, lanes), 0)
    kept = (x < width(meta_ref, lead)) & (y < height(meta_ref, lead))
    return kept.reshape(rows * cols, lanes)


def head_diagonal():
    a = lax.broadcasted_iota(jnp.int32, (LANES, LANES), 0) // HD
    b = lax.broadcasted_iota(jnp.int32, (LANES, LANES), 1) // HD
    return a == b


def by_radius(step, radii, run):
    for radius in sorted(set(radii)):
        steps = [k for k, r in enumerate(radii) if r == radius]
        hit = functools.reduce(lambda a, b: a | b, [step == k for k in steps])
        pl.when(hit)(functools.partial(run, radius))


def enter_kernel(
    dims,
    local_rows,
    meta_ref,
    *refs,
):
    images, rows, cols, channels = dims
    cells = rows * cols
    group = rows // local_rows
    core = place_of(meta_ref) & 1
    firsts = (place_of(meta_ref) * images, 0, core * images, 0)
    pieces = refs[:group]
    small_ref, x_ref, first_ref, norma_ref, normed_ref, rstd_ref, pad_x = refs[group:]
    place = meta_ref[0]
    zeros = jnp.zeros((images, rows, SUB, channels), F32)
    pad_x[:, :, :SUB, :] = zeros
    pad_x[:, :, SUB + cols :, :] = zeros

    for k, (piece, first_image) in enumerate(zip(pieces, firsts)):

        def mask_row(r, k=k, piece=piece, first_image=first_image):
            lead = r // local_rows
            y_here = r % local_rows
            y = (place ^ k) * local_rows + y_here
            kept = col_keep(meta_ref, lead, cols, channels) & (y < height(meta_ref, lead))
            block = jnp.where(kept, piece[y_here, first_image + lead], 0)
            at = pl.ds(pl.multiple_of((lead * rows + y) * cols, cols), cols)
            x_ref[at, :] = block
            pad_x[lead, y, pl.ds(SUB, cols), :] = block.astype(F32)

        loop(images * local_rows, mask_row, 2)

    def conv(lead):
        for lane in range(0, channels, LANES):
            lanes = pl.ds(lane, LANES)
            for col in range(0, cols, SUB):
                out = filtered(
                    pad_x,
                    lead,
                    rows,
                    col,
                    lambda dy, dx: small_ref[pl.ds(3 * (dy + 1) + dx + 1, 1), lanes],
                    1,
                    1,
                    lanes,
                )
                bias = small_ref[pl.ds(58, 1), lanes]
                for y in range(rows):
                    own = pad_x[lead, y, pl.ds(SUB + col, SUB), lanes]
                    at = pl.multiple_of(lead * cells + (y * cols + col), SUB)
                    first_ref[pl.ds(at, SUB), lanes] = own + out[y] + bias

    loop(images, conv)

    def normalize(r):
        at = pl.ds(pl.multiple_of(r * cols, cols), cols)
        normed, rstd = norm_parts(first_ref[at, :])
        normed_ref[at, :] = normed
        rstd_ref[at, :] = jnp.broadcast_to(rstd, (cols, LANES))
        norma_ref[at, :] = (
            normed * small_ref[pl.ds(59, 1), :] + small_ref[pl.ds(60, 1), :]
        ).astype(BF16)

    loop(images * rows, normalize, 8)


def attention_kernel(
    dims,
    radii,
    mask,
    final,
    meta_ref,
    norma_ref,
    part_ref,
    blocks_ref,
    *refs,
):
    images, rows, cols, channels = dims
    cells = rows * cols
    if mask:
        before_ref, *refs = refs
    if final:
        first_ref, small_ref, *refs = refs
    query_ref, probs_ref, value_ref, near_ref, attended_ref, kv_ref, *refs = refs
    if final:
        second_ref, normb_ref, normed_ref, rstd_ref, total, *refs = refs
    else:
        total, *refs = refs
    weight, pad_v, near_f = refs

    fetch(blocks_ref, NEAR_LAST, weight, meta_ref[1])
    pad_v[...] = jnp.zeros_like(pad_v)
    diagonal = head_diagonal()
    block = mask ^ meta_ref[0]

    def project(lead):
        at = pl.ds(lead * cells, cells)
        proj = dot(norma_ref[at, :], weight[:, : 3 * LANES])
        query = (proj[:, :LANES] + part_ref[block, pl.ds(61, 1), :]).astype(BF16)
        value = (proj[:, 2 * LANES :] + part_ref[block, pl.ds(62, 1), :]).astype(BF16)
        kept = cell_keep(meta_ref, lead, rows, cols, LANES)
        key = jnp.where(kept, proj[:, LANES : 2 * LANES], -1e30)
        expo = jnp.exp(key - jnp.max(key, axis=0, keepdims=True))
        probs = (expo / jnp.sum(expo, axis=0, keepdims=True)).astype(BF16)
        query_ref[at, :] = query
        probs_ref[at, :] = probs
        value_ref[at, :] = value
        kv = jnp.where(diagonal, dot_lt(probs, value), 0.0).astype(BF16)
        kv_ref[lead] = kv
        masked = jnp.where(kept, value.astype(F32), 0.0)
        pad_v[lead, :, pl.ds(SUB, cols), :] = masked.reshape(rows, cols, LANES)

    each(images, project)

    def conv_near(radius):
        def conv(lead):
            for col in range(0, cols, SUB):
                out = filtered(
                    pad_v,
                    lead,
                    rows,
                    col,
                    lambda dy, dx: part_ref[block, pl.ds(9 + 7 * (dy + 3) + dx + 3, 1), :],
                    radius,
                    1,
                )
                bias = part_ref[block, pl.ds(63, 1), :]
                for y in range(rows):
                    at = pl.multiple_of(lead * cells + (y * cols + col), SUB)
                    near_f[pl.ds(at, SUB), :] = out[y] + bias

        loop(images, conv)

    by_radius(block, radii, conv_near)

    def attend(lead):
        at = pl.ds(lead * cells, cells)
        query = query_ref[at, :]
        near = near_f[at, :]
        near_ref[at, :] = near.astype(BF16)
        factored = dot(query, kv_ref[lead]) * HEAD_SCALE
        attended = (factored + query.astype(F32) * near).astype(BF16)
        attended_ref[at, :] = attended
        out = dot_rt(attended, weight[:, 3 * LANES :])

        total[at, :] = out + before_ref[at, :] if mask else out

    each(images, attend)
    if not final:
        return

    def finish(r):
        at = pl.ds(pl.multiple_of(r * cols, cols), cols)
        second = first_ref[at, :] + total[at, :] + small_ref[pl.ds(64, 1), :]
        second_ref[at, :] = second
        normed, rstd = norm_parts(second)
        normed_ref[at, :] = normed
        rstd_ref[at, :] = jnp.broadcast_to(rstd, (cols, LANES))
        normb_ref[at, :] = (
            normed * small_ref[pl.ds(65, 1), :] + small_ref[pl.ds(66, 1), :]
        ).astype(BF16)

    loop(images * rows, finish, 8)


def gelu_parts(pre):
    cdf = 0.5 * (1.0 + lax.erf(pre * ROOT_HALF))
    return pre * cdf, cdf + pre * (jnp.exp(-0.5 * pre * pre) * INV_ROOT_TAU)


def hidden_kernel(
    dims,
    local_rows,
    mask,
    final,
    meta_ref,
    normb_ref,
    bias_ref,
    blocks_1,
    blocks_2,
    *refs,
):
    images, rows, cols, channels = dims
    cells = rows * cols
    group = rows // local_rows
    if mask:
        dout, total_in, dnorm_in, *refs = refs
    else:
        pieces, refs = refs[:group], refs[group:]
    if final:
        second_ref, normed_ref, rstd_ref, small_ref, *refs = refs
    d_ref, dbias_ref, *refs = refs
    if final:
        outs, refs = refs[:group], refs[group:]
        dsecond_ref, low_ref, sums_ref, total, dnorm, *refs = refs
    else:
        if not mask:
            dout, *refs = refs
        total, dnorm, *refs = refs
    w1, w2, pre, act_grad, hact, dhpre = refs
    hidden = w1.shape[1]
    place, dp_block = meta_ref[0], meta_ref[1]

    fetch(blocks_1, NEAR_LAST, w1, dp_block)
    fetch(blocks_2, NEAR_LAST, w2, dp_block, 2, mask // 2)
    if not mask:
        firsts = (0, 0, (place & 1) * images, 0)
        for k, (piece, first_image) in enumerate(zip(pieces, firsts)):

            def mask_row(r, k=k, piece=piece, first_image=first_image):
                lead = r // local_rows
                y_here = r % local_rows
                y = (place ^ k) * local_rows + y_here
                kept = col_keep(meta_ref, lead, cols, channels) & (y < height(meta_ref, lead))
                at = pl.ds(pl.multiple_of((lead * rows + y) * cols, cols), cols)
                block = piece[y_here, first_image + lead].astype(F32)
                dout[at, :] = jnp.where(kept, block, 0.0).astype(BF16)

            loop(images * local_rows, mask_row, 2)

    dbias_ref[...] = jnp.zeros_like(dbias_ref)

    size = 256
    bias_acc = jnp.zeros((SUB, hidden), F32)
    for t in range(images * cells // size):
        at = pl.ds(t * size, size)
        pre_t = dot(normb_ref[at, :], w1[...]) + bias_ref[mask ^ place]
        act_t = dot(dout[at, :], w2[...])
        act, slope = gelu_parts(pre_t)
        hact_t = act.astype(BF16)
        back_t = (act_t * slope).astype(BF16)
        hact[at, :] = hact_t
        dhpre[at, :] = back_t
        bias_acc += jnp.sum(back_t.astype(F32).reshape(size // SUB, SUB, hidden), axis=0)
        out = dot_rt(hact_t, w2[...])
        back = dot_rt(back_t, w1[...])
        total[at, :] = out + total_in[at, :] if mask else out
        dnorm[at, :] = back + dnorm_in[at, :] if mask else back
    dbias_ref[...] = jnp.sum(bias_acc, axis=0, keepdims=True)
    dw1 = dot_lt(normb_ref[...], dhpre[...])
    hand_out(d_ref, NEAR_LAST, dw1, pl.ds(0, hidden), dp_block)
    dw2 = dot_lt(dout[...], hact[...])
    hand_out(d_ref, NEAR_LAST, dw2, pl.ds(hidden, hidden), dp_block)
    if final:
        gain = small_ref[pl.ds(65, 1), :]
        zero = jnp.zeros((SUB, channels), F32)
        acc = (zero,) * 4
        for k, out_ref in enumerate(outs):

            def finish(r, acc):
                lead = r // local_rows
                y_here = r % local_rows
                y = (place ^ k) * local_rows + y_here
                at = pl.ds(pl.multiple_of((lead * rows + y) * cols, cols), cols)
                second = second_ref[at, :]
                out = second + total[at, :] + small_ref[pl.ds(67, 1), :]
                out_ref[y_here, lead] = out.astype(BF16)
                normed = normed_ref[at, :]
                rstd = jnp.concatenate([rstd_ref[at, :]] * (channels // LANES), axis=1)
                back = dnorm[at, :]
                got = dout[at, :].astype(F32)
                dsecond = got + norm_back(back, normed, rstd, gain)
                dsecond_ref[at, :] = dsecond
                low = dsecond.astype(BF16)
                low_ref[at, :] = low
                terms = (low.astype(F32), back * normed, back, got)
                return tuple(
                    a + jnp.sum(t.reshape(cols // SUB, SUB, channels), axis=0)
                    for a, t in zip(acc, terms)
                )

            acc = lax.fori_loop(0, images * local_rows, finish, acc, unroll=4)
        sums_ref[...] = jnp.zeros_like(sums_ref)
        for k, a in enumerate(acc):
            sums_ref[pl.ds(k, 1), :] = jnp.sum(a, axis=0, keepdims=True)


def attention_back_kernel(
    dims,
    radii,
    mask,
    summed,
    meta_ref,
    low,
    norma_ref,
    part_ref,
    blocks_ref,
    query_ref,
    probs_ref,
    value_ref,
    near_ref,
    attended_ref,
    kv_ref,
    *refs,
):
    images, rows, cols, channels = dims
    cells = rows * cols
    if summed:
        before_ref, *refs = refs
    dnorma_ref, d_ref, sums_ref, weight, pad_d, value_f, grads, dvalue_f = refs
    dp_block = meta_ref[1]

    fetch(blocks_ref, NEAR_LAST, weight, dp_block)
    pad_d[...] = jnp.zeros_like(pad_d)
    sums_ref[...] = jnp.zeros_like(sums_ref)
    diagonal = head_diagonal()
    block = mask ^ meta_ref[0]

    def first_half(lead):
        at = pl.ds(lead * cells, cells)
        datt = dot(low[at, :], weight[:, 3 * LANES :]).astype(BF16)
        query = query_ref[at, :]
        probs = probs_ref[at, :]
        value = value_ref[at, :]
        kept = cell_keep(meta_ref, lead, rows, cols, LANES)
        dkv = jnp.where(diagonal, dot_lt(query, datt) * HEAD_SCALE, 0.0).astype(BF16)
        datt_f = datt.astype(F32)
        dnear = datt_f * query.astype(F32)
        pad_d[lead, :, pl.ds(SUB, cols), :] = dnear.reshape(rows, cols, LANES)
        dquery = (
            dot_rt(datt, kv_ref[lead]) * HEAD_SCALE + datt_f * near_ref[at, :].astype(F32)
        ).astype(BF16)
        dprobs = dot_rt(value, dkv)
        probs_f = probs.astype(F32)
        inner = jnp.sum(probs_f * dprobs, axis=0, keepdims=True)
        dkey = (probs_f * (dprobs - inner)).astype(BF16)
        grads[at, :LANES] = dquery
        grads[at, LANES : 2 * LANES] = dkey
        dvalue_f[at, :] = dot(probs, dkv)
        value_f[at, :] = jnp.where(kept, value.astype(F32), 0.0)
        sums_ref[pl.ds(61, 1), :] += jnp.sum(dquery.astype(F32), axis=0, keepdims=True)
        sums_ref[pl.ds(63, 1), :] += jnp.sum(dnear, axis=0, keepdims=True)

    each(images, first_half)

    def conv_back(radius):
        def conv(lead):
            x = lax.broadcasted_iota(jnp.int32, (SUB, LANES), 0)
            for col in range(0, cols, SUB):
                out = filtered(
                    pad_d,
                    lead,
                    rows,
                    col,
                    lambda dy, dx: part_ref[block, pl.ds(9 + 7 * (dy + 3) + dx + 3, 1), :],
                    radius,
                    -1,
                )
                inside = (x + col) < width(meta_ref, lead)
                for y in range(rows):
                    at = pl.ds(pl.multiple_of(lead * cells + (y * cols + col), SUB), SUB)
                    kept = inside & (y < height(meta_ref, lead))
                    dvalue_f[at, :] = dvalue_f[at, :] + jnp.where(kept, out[y], 0.0)

        loop(images, conv)

        def own(lead, y, col):
            at = pl.multiple_of(lead * cells + (y * cols + col), SUB)
            return value_f[pl.ds(at, SUB), :]

        for dx in range(-radius, radius + 1):
            acc = tap_products(pad_d, own, images, rows, cols, dx, radius)
            for k, dy in enumerate(range(-radius, radius + 1)):
                sums_ref[pl.ds(9 + 7 * (dy + 3) + dx + 3, 1), :] = jnp.sum(
                    acc[k], axis=0, keepdims=True
                )

    by_radius(block, radii, conv_back)

    def second_half(lead):
        at = pl.ds(lead * cells, cells)
        dvalue = dvalue_f[at, :].astype(BF16)
        grads[at, 2 * LANES :] = dvalue
        sums_ref[pl.ds(62, 1), :] += jnp.sum(dvalue.astype(F32), axis=0, keepdims=True)
        back = dot_rt(grads[at, :], weight[:, : 3 * LANES])

        dnorma_ref[at, :] = back + before_ref[at, :] if summed else back

    each(images, second_half)
    wide = 3 * LANES
    dwq = dot_lt(norma_ref[...], grads[...])
    hand_out(d_ref, NEAR_LAST, dwq, pl.ds(0, wide), dp_block)
    dwp = dot_lt(low[...], attended_ref[...])
    hand_out(d_ref, NEAR_LAST, dwp, pl.ds(wide, LANES), dp_block)


def input_back_kernel(
    dims,
    local_rows,
    tile_rows,
    meta_ref,
    x_ref,
    normed_ref,
    rstd_ref,
    dnorma_ref,
    dsecond_ref,
    small_ref,
    window_ref,
    two_ref,
    *refs,
):
    images, rows, cols, channels = dims
    cells = rows * cols
    group = rows // local_rows
    heads_refs, dbias_refs, refs = refs[:group], refs[group : 2 * group], refs[2 * group :]
    *outs, far_ref = refs[: group - 1]
    outs = (*outs, far_ref.at[0], far_ref.at[1])
    tiles_ref, pad_d, x_f, sums = refs[group - 1 :]
    place = meta_ref[0]
    zeros = jnp.zeros((images, rows, SUB, channels), F32)
    pad_d[:, :, :SUB, :] = zeros
    pad_d[:, :, SUB + cols :, :] = zeros
    gain = small_ref[pl.ds(59, 1), :]

    def norm(r, acc):
        lead = r // rows
        y = r % rows
        at = pl.ds(pl.multiple_of(r * cols, cols), cols)
        normed = normed_ref[at, :]
        rstd = jnp.concatenate([rstd_ref[at, :]] * (channels // LANES), axis=1)
        back = dnorma_ref[at, :]
        dfirst = dsecond_ref[at, :] + norm_back(back, normed, rstd, gain)
        pad_d[lead, y, pl.ds(SUB, cols), :] = dfirst
        x_f[at, :] = x_ref[at, :].astype(F32)
        terms = (dfirst, back * normed, back)
        return tuple(
            a + jnp.sum(t.reshape(cols // SUB, SUB, channels), axis=0)
            for a, t in zip(acc, terms)
        )

    zero = jnp.zeros((SUB, channels), F32)
    acc = lax.fori_loop(0, images * rows, norm, (zero,) * 3, unroll=8)
    for k, a in enumerate(acc):
        sums[pl.ds(58 + k, 1), :] = jnp.sum(a, axis=0, keepdims=True)

    def conv(lead):
        x = lax.broadcasted_iota(jnp.int32, (SUB, LANES), 0)
        for lane in range(0, channels, LANES):
            lanes = pl.ds(lane, LANES)
            for col in range(0, cols, SUB):
                out = filtered(
                    pad_d,
                    lead,
                    rows,
                    col,
                    lambda dy, dx: small_ref[pl.ds(3 * (dy + 1) + dx + 1, 1), lanes],
                    1,
                    -1,
                    lanes,
                )
                inside = (x + col) < width(meta_ref, lead)
                for y in range(rows):
                    own = pad_d[lead, y, pl.ds(SUB + col, SUB), lanes]
                    at = pl.multiple_of(lead * cells + (y * cols + col), SUB)
                    kept = inside & (y < height(meta_ref, lead))
                    x_f[pl.ds(at, SUB), lanes] = jnp.where(kept, own + out[y], 0.0)

    for lane in range(0, channels, LANES):
        lanes = pl.ds(lane, LANES)

        def own(lead, y, col):
            at = pl.multiple_of(lead * cells + (y * cols + col), SUB)
            return x_f[pl.ds(at, SUB), lanes]

        for dx in (-1, 0, 1):
            acc = tap_products(pad_d, own, images, rows, cols, dx, 1, lanes)
            for k, dy in enumerate((-1, 0, 1)):
                sums[pl.ds(3 * (dy + 1) + dx + 1, 1), lanes] = jnp.sum(
                    acc[k], axis=0, keepdims=True
                )
    loop(images, conv)
    for k, out_ref in enumerate(outs):

        def give(r):
            lead = r // local_rows
            y_here = r % local_rows
            y = (place ^ k) * local_rows + y_here
            at = pl.ds(pl.multiple_of((lead * rows + y) * cols, cols), cols)
            out_ref[y_here, lead] = x_f[at, :].astype(BF16)

        loop(images * local_rows, give, 2)

    for mask in range(group):
        heads_ref = heads_refs[mask]
        lanes = pl.ds(pl.multiple_of((place ^ mask) * LANES, LANES), LANES)
        sums[pl.ds(9, 49), lanes] = heads_ref[pl.ds(9, 49), :] * window_ref[:, lanes]
        sums[pl.ds(61, 3), lanes] = heads_ref[pl.ds(61, 3), :]
        sums[pl.ds(68 + (place ^ mask), 1), :] = dbias_refs[mask][...]
    sums[pl.ds(64, 4), :] = two_ref[pl.ds(0, 4), :]
    tiles_ref[...] = jnp.zeros_like(tiles_ref)
    for d in range(tiles_ref.shape[0]):
        here = min(tile_rows, sums.shape[0] - d * tile_rows)
        for j in range(tiles_ref.shape[1]):
            if here > 0:
                tiles_ref[d, j, pl.ds(0, here), :] = sums[
                    pl.ds(d * tile_rows, here), pl.ds(j * LANES, LANES)
                ]


def join_kernel(meta_ref, *refs):
    *pieces, out_ref = refs
    images = pieces[0].shape[1]
    for k, piece in enumerate(pieces):
        values = piece[0] if len(piece.shape) == 5 else piece[...]
        out_ref[:, pl.ds((meta_ref[0] ^ k) * images, images)] = values.astype(out_ref.dtype)


SCALARS = pl.BlockSpec(memory_space=pltpu.SMEM)
CLOSE = pl.BlockSpec(memory_space=pltpu.VMEM)
ENTER_MIB = 8
ATTENTION_MIB = 10
HIDDEN_MIB = 18
BACK_MIB = 10
INPUT_MIB = 10
JOIN_MIB = 4
FINAL_MIB = 8


def shape_of(shape, dtype):
    return jax.ShapeDtypeStruct(shape, dtype)


def call(kernel, name, us, mib, inputs, out_specs, out_shape, scratch):
    return pl.pallas_call(
        kernel,
        in_specs=[spec for _, spec in inputs],
        out_specs=out_specs,
        out_shape=out_shape,
        scratch_shapes=scratch,
        compiler_params=pltpu.CompilerParams(vmem_limit_bytes=mib * 2**20),
        cost_estimate=pl.CostEstimate(flops=us * 10**9, bytes_accessed=us * 2**20, transcendentals=0),
        name=name,
    )(*[array for array, _ in inputs])


def near_by(arrays):
    return [(a, CLOSE) for a in arrays]


def enter(dims, local_rows, meta, pieces, small):
    images, rows, cols, channels = dims
    flat = (images * rows * cols, channels)
    return call(
        functools.partial(enter_kernel, dims, local_rows),
        "enter",
        8,
        ENTER_MIB,
        [(meta, SCALARS), *near_by(pieces), (small, CLOSE)],
        [CLOSE] * 5,
        [
            shape_of(flat, BF16),
            shape_of(flat, F32),
            shape_of(flat, BF16),
            shape_of(flat, F32),
            shape_of((flat[0], LANES), F32),
        ],
        [pltpu.VMEM((images, rows, cols + 2 * SUB, channels), F32)],
    )


def attention(dims, radii, mask, meta, norma, parts, blocks, *more):
    images, rows, cols, channels = dims
    cells = images * rows * cols
    flat = (cells, channels)
    final = len(more) > 1
    kinds = ((cells, LANES),) * 5 + ((images, LANES, LANES),)
    sums = [shape_of(flat, F32)]
    if final:
        sums += [shape_of(flat, BF16), shape_of(flat, F32), shape_of((cells, LANES), F32)]
    return call(
        functools.partial(attention_kernel, dims, radii, mask, final),
        "attention",
        5,
        ATTENTION_MIB,
        [(meta, SCALARS), *near_by([norma, parts, blocks, *more])],
        [CLOSE] * (len(kinds) + len(sums)),
        [*[shape_of(k, BF16) for k in kinds], *sums],
        ([pltpu.VMEM(flat, F32)] if final else [])
        + [
            pltpu.VMEM((channels, 4 * LANES), BF16),
            pltpu.VMEM((images, rows, cols + 2 * SUB, LANES), F32),
            pltpu.VMEM((cells, LANES), F32),
        ],
    )


def hidden_part(dims, mask, final, meta, normb, bias, blocks_1, blocks_2, *more):
    images, rows, cols, channels = dims
    cells = images * rows * cols
    groups, _, hidden = bias.shape
    local_rows = rows // groups
    piece = (local_rows, images, cols, channels)
    flat = (cells, channels)
    if final:
        outs = [
            *[shape_of(piece, BF16) for _ in range(groups)],
            shape_of(flat, F32),
            shape_of(flat, BF16),
            shape_of((SUB, channels), F32),
        ]
    else:
        outs = [shape_of(flat, F32), shape_of(flat, F32)]
        outs = outs if mask else [shape_of(flat, BF16), *outs]
    return call(
        functools.partial(hidden_kernel, dims, local_rows, mask, final),
        "hidden",
        8,
        HIDDEN_MIB,
        [(meta, SCALARS), *near_by([normb, bias, blocks_1, blocks_2, *more])],
        [CLOSE] * (2 + len(outs)),
        [
            shape_of((*blocks_1.shape[:2], 2 * hidden), BF16),
            shape_of((1, hidden), F32),
            *outs,
        ],
        ([pltpu.VMEM(flat, F32)] * 2 if final else [])
        + [
            pltpu.VMEM((channels, hidden), BF16),
            pltpu.VMEM((channels, hidden), BF16),
            pltpu.VMEM((rows * cols, hidden), F32),
            pltpu.VMEM((rows * cols, hidden), F32),
            pltpu.VMEM((cells, hidden), BF16),
            pltpu.VMEM((cells, hidden), BF16),
        ],
    )


def attention_back(dims, radii, mask, meta, low, norma, parts, blocks, saved, *before):
    images, rows, cols, channels = dims
    cells = images * rows * cols
    flat = (cells, channels)
    return call(
        functools.partial(attention_back_kernel, dims, radii, mask, len(before)),
        "attention_back",
        7,
        BACK_MIB,
        [(meta, SCALARS), *near_by([low, norma, parts, blocks, *saved, *before])],
        [CLOSE] * 3,
        [
            shape_of(flat, F32),
            shape_of(blocks.shape, BF16),
            shape_of((72, LANES), F32),
        ],
        [
            pltpu.VMEM((channels, 4 * LANES), BF16),
            pltpu.VMEM((images, rows, cols + 2 * SUB, LANES), F32),
            pltpu.VMEM((cells, LANES), F32),
            pltpu.VMEM((cells, 3 * LANES), BF16),
            pltpu.VMEM((cells, LANES), F32),
        ],
    )


def input_back(dims, groups, shards, meta, *args):
    images, rows, cols, channels = dims
    flat = (images * rows * cols, channels)
    piece = (rows // groups, images, cols, channels)
    tile_rows = -(-72 // shards)
    tiles = (shards, groups, tile_rows, LANES)
    return call(
        functools.partial(input_back_kernel, dims, rows // groups, tile_rows),
        "input_back",
        10,
        INPUT_MIB,
        [(meta, SCALARS), *near_by(args)],
        [CLOSE] * 4,
        [
            *[shape_of(piece, BF16) for _ in range(2)],
            shape_of((2, *piece), BF16),
            shape_of(tiles, F32),
        ],
        [
            pltpu.VMEM((images, rows, cols + 2 * SUB, channels), F32),
            pltpu.VMEM(flat, F32),
            pltpu.VMEM((72, channels), F32),
        ],
    )


def join(meta, pieces, dtype):
    local_rows, images, cols, channels = pieces[0].shape
    return call(
        join_kernel,
        "join",
        2,
        JOIN_MIB,
        [(meta, SCALARS), *near_by(pieces)],
        CLOSE,
        shape_of((local_rows, images * len(pieces), cols, channels), dtype),
        [],
    )


def sums_kernel(counts, *refs):
    heads, hidden = refs[: counts[0]], refs[counts[0] : sum(counts)]
    tiles_ref, heads_ref, hidden_ref, message_ref = refs[sum(counts) :]
    squares = jnp.zeros((1, LANES), F32)
    for terms, out_ref in ((heads, heads_ref), (hidden, hidden_ref)):
        total = sum(term[...].astype(F32).reshape(out_ref.shape) for term in terms)
        out_ref[...] = total
        columns = jnp.sum(total * total, axis=0, keepdims=True)
        for lane in range(0, columns.shape[1], LANES):
            squares += columns[:, lane : lane + LANES]
    small = jnp.sum(tiles_ref[...], axis=0)
    squares += jnp.sum(small * small, axis=0, keepdims=True)
    rows = small.shape[0]
    for k in range(message_ref.shape[0]):
        message_ref[k, pl.ds(0, rows), :] = small
        message_ref[k, pl.ds(rows, 1), :] = squares


def sums_of(heads, hidden, tiles):
    shard_rows = heads[0].shape[-2]
    count, rows, _ = tiles.shape
    return call(
        functools.partial(sums_kernel, (len(heads), len(hidden))),
        "sums",
        2,
        FINAL_MIB,
        near_by([*heads, *hidden, tiles]),
        [CLOSE] * 3,
        [
            shape_of((shard_rows, heads[0].shape[-1]), F32),
            shape_of((shard_rows, hidden[0].shape[-1]), F32),
            shape_of((count, rows + 1, LANES), F32),
        ],
        [],
    )


RATE_MODEL = RATE_FACTOR * D ** (-0.5)
RATE_HIDDEN = RATE_FACTOR * FF ** (-0.5)


def adamw(weight, mean, square, gradient, factor, rate, decay):
    clipped = gradient * factor
    mean_new = BETA_ONE * mean + (1.0 - BETA_ONE) * clipped
    square_new = BETA_TWO * square + (1.0 - BETA_TWO) * clipped * clipped
    mean_hat = mean_new / (1.0 - BETA_ONE**STEP)
    square_hat = square_new / (1.0 - BETA_TWO**STEP)
    weight_new = weight - rate * (mean_hat / (jnp.sqrt(square_hat) + ADAM_EPS) + decay * weight)
    return (weight_new, mean_new, square_new)


def update_kernel(groups, every_ref, heads_ref, hidden_ref, *refs):
    ins, outs, (grads,) = refs[:15], refs[15:31], refs[31:]
    count, rows, _ = every_ref.shape
    rows -= 1
    squares = jnp.sum(every_ref[:, pl.ds(rows, 1), :], axis=0)
    norm = jnp.sqrt(jnp.sum(squares, axis=1, keepdims=True))
    factor = jnp.minimum(1.0, CLIP_NORM / (norm + 1e-06))
    outs[0][...] = norm
    for k in range(count):
        first, lane = k // groups * rows, k % groups * LANES
        here = min(rows, grads.shape[0] - first)
        if here > 0:
            grads[pl.ds(first, here), pl.ds(lane, LANES)] = every_ref[k, pl.ds(0, here), :]
    hidden = hidden_ref.shape[1] // 2
    for k in range(3):
        gradient = heads_ref[:, k * LANES : (k + 1) * LANES]
        new = adamw(
            ins[0][k], ins[1][k], ins[2][k], gradient, factor, RATE_MODEL, WEIGHT_DECAY
        )
        for out, value in zip(outs[1:4], new):
            out[k] = value
    for n, gradient, rate, decay in (
        (1, heads_ref[:, 3 * LANES :], RATE_MODEL, WEIGHT_DECAY),
        (2, hidden_ref[:, :hidden], RATE_MODEL, WEIGHT_DECAY),
        (3, hidden_ref[:, hidden:], RATE_HIDDEN, WEIGHT_DECAY),
        (4, grads[...], SMALL_RATE, 0.0),
    ):
        weight, mean, square = (r[...] for r in ins[3 * n : 3 * n + 3])
        new = adamw(weight, mean, square, gradient, factor, rate, decay)
        for out, value in zip(outs[1 + 3 * n : 4 + 3 * n], new):
            out[...] = value


def updated(groups, every, heads, hidden, state):
    return call(
        functools.partial(update_kernel, groups),
        "update",
        3,
        FINAL_MIB,
        near_by([every, heads, hidden, *state]),
        [CLOSE] * 16,
        [shape_of((1, 1), F32), *[shape_of(a.shape, F32) for a in state]],
        [pltpu.VMEM(state[-1].shape, F32)],
    )


def window_rows(channels):
    radius = jnp.repeat(jnp.array([radius_of(h) for h in range(channels // HD)], jnp.int32), HD)
    tap_list = jnp.arange(49, dtype=jnp.int32)
    tap_row = jnp.abs(tap_list // 7 - 3)
    tap_col = jnp.abs(tap_list % 7 - 3)
    inside = (tap_row[:, None] <= radius[None, :]) & (tap_col[:, None] <= radius[None, :])
    return inside.astype(F32)


def on_device(
    patches,
    cotangent,
    grid_shape,
    qkv_weight,
    qkv_mean,
    qkv_square,
    proj_weight,
    proj_mean,
    proj_square,
    expand_weight,
    expand_mean,
    expand_square,
    contract_weight,
    contract_mean,
    contract_square,
    small_params,
    small_mean,
    small_square,
):
    group = lax.axis_size("mp")
    shards = lax.axis_size("dp")
    place = lax.axis_index("mp")
    local_rows, image_count, cols, channels = patches.shape
    images = image_count // group
    rows = local_rows * group
    dims = (images, rows, cols, channels)
    shard_rows = qkv_weight.shape[0]
    head_width = qkv_weight.shape[2]
    hidden = expand_weight.shape[1]
    assert head_width == LANES
    per_block = head_width // HD
    radii = [
        max(radius_of(per_block * g + h) for h in range(per_block)) for g in range(group)
    ]
    grids = lax.dynamic_slice_in_dim(grid_shape, place * images, images, 0)
    dp_block = lax.axis_index("dp") >> finer_bits(shard_rows)
    meta = jnp.concatenate([jnp.stack([place, dp_block]).astype(jnp.int32), grids.reshape(-1)])

    def core(array):
        return flip(array, "mp", CORE)

    def chip(array):
        return flip(array, "mp", CHIP)

    def over_dp(array, bit):
        return flip(array, "dp", bit + low)

    def joined(*arrays):
        return jnp.concatenate(arrays, axis=0)

    def some_images(array, first, count):
        return lax.dynamic_slice_in_dim(array, first, count, 1).astype(BF16)

    def image_parts(array):
        near = some_images(array, (place ^ 1) * images, images)
        far = some_images(array, ((place ^ 2) & ~1) * images, 2 * images)
        return near, far

    def for_other_core(far):
        return some_images(far, ((place & 1) ^ 1) * images, images)

    low = finer_bits(shard_rows)

    heads_shard = jnp.concatenate(
        [qkv_weight.astype(BF16).reshape(shard_rows, -1), proj_weight.astype(BF16)], axis=1
    )
    one_shard = expand_weight.astype(BF16)
    two_shard = contract_weight.astype(BF16)

    heads, one, two = whole_block(heads_shard), whole_block(one_shard), whole_block(two_shard)
    patch_near, patch_far = image_parts(patches)
    two = joined(two, chip(two))
    heads = joined(heads, over_dp(heads, 2))
    two, patch_far, patch_near = tie(two, patch_far, patch_near)
    patch_far = chip(patch_far)
    patch_near = core(patch_near)

    heads, one = tie(heads, one)
    heads = joined(heads, over_dp(heads, 1))
    one_got = over_dp(one, 2)

    patch_far, cotangent = tie(patch_far, cotangent)
    patch_relayed = core(for_other_core(patch_far))
    cot_near, cot_far = image_parts(cotangent)
    cot_own = some_images(cotangent, place * images, images)

    window = window_rows(channels)
    parts = small_params.at[9:58].multiply(window).reshape(72, group, LANES).transpose(1, 0, 2)
    unit_bias = small_params[68:].reshape(group, 1, hidden)

    patch_pieces = [patches, patch_near, patch_far, patch_relayed]
    x, first, norma, normed_1, rstd_1 = enter(dims, local_rows, meta, patch_pieces, small_params)
    heads_got, two_got = over_dp(heads, 0), over_dp(two, 2)
    norma, heads_got, one_got, two_got = tie(norma, heads_got, one_got, two_got)
    heads = joined(heads, heads_got)
    one = joined(one, one_got)
    two = joined(two, two_got)
    saved, weights = [None] * group, [heads] + [None] * (group - 1)

    *saved[0], attn = attention(dims, radii, 0, meta, norma, parts, heads)
    weights[1] = after(core(heads), attn)
    one = joined(one, after(over_dp(one, 1), attn))
    heads_chip = chip(heads)
    cot_far = after(chip(cot_far), attn)
    cot_pieces = [cot_own, core(cot_near), cot_far, core(for_other_core(cot_far))]
    *saved[1], attn = attention(dims, radii, 1, meta, norma, parts, weights[1], attn)
    weights[2] = after(heads_chip, attn)
    one = joined(one, after(over_dp(one, 0), attn))
    two = doubled(two, 1, low, attn)
    *saved[2], attn = attention(dims, radii, 2, meta, norma, parts, weights[2], attn)
    weights[3] = after(flip(weights[2], "mp", CORE), attn)
    *saved[3], second, normb, normed_2, rstd_2 = attention(
        dims, radii, 3, meta, norma, parts, weights[3], attn, first, small_params
    )
    two = doubled(two, 0, low, normb)

    grads, dbias = [None] * group, [None] * group
    grads[0], dbias[0], dout, total, dnorm = hidden_part(
        dims, 0, False, meta, normb, unit_bias, one, two, *cot_pieces
    )
    one_near, two_near = after(flip(one, "mp", CORE), dnorm), after(flip(two, "mp", CORE), dnorm)
    one_chip = flip(one, "mp", CHIP)
    grads[1], dbias[1], total, dnorm = hidden_part(
        dims, 1, False, meta, normb, unit_bias, one_near, two_near, dout, total, dnorm
    )
    one_chip = after(one_chip, dnorm)
    grads[2], dbias[2], total, dnorm = hidden_part(
        dims, 2, False, meta, normb, unit_bias, one_chip, two, dout, total, dnorm
    )
    one_chip = after(flip(one_chip, "mp", CORE), dnorm)
    own = low_added(grads[0], flip(grads[1], "mp", CORE))
    dnorm, own = tie(dnorm, own)
    grads[3], dbias[3], *outs, dsecond, dsecond_low, sums_two = hidden_part(
        dims,
        3,
        True,
        meta,
        normb,
        unit_bias,
        one_chip,
        two_near,
        dout,
        total,
        dnorm,
        second,
        normed_2,
        rstd_2,
        small_params,
    )

    heads_grads, heads_sums = [None] * group, [None] * group

    def back(mask, low_rows, *before):
        dnorma, heads_grads[mask], heads_sums[mask] = attention_back(
            dims, radii, mask, meta, low_rows, norma, parts, weights[mask], saved[mask], *before
        )
        return dnorma

    def part_way(blocks, bit, first, last):
        half = blocks.shape[0] // 2
        other = flip(blocks[half + first : half + last], "dp", bit + low)
        return low_added(blocks[first:last], other)

    own_1 = part_way(own, 0, 2, 4)
    low_rows, own, own_1, sent, out_3 = tie(dsecond_low, own, own_1, grads[3], outs[3])
    dnorma = back(3, low_rows)

    own_0 = part_way(own, 0, 0, 2)
    far = low_added(grads[2], flip(sent, "mp", CORE))
    out_3 = flip(out_3, "mp", CHIP)
    low_rows, dnorma, own_0, own_1, far, out_3, sent = tie(
        low_rows, dnorma, own_0, own_1, far, out_3, heads_grads[3]
    )
    dnorma = back(2, low_rows, dnorma)

    own = low_added(own_0, over_dp(own_1, 1))
    far_1 = part_way(far, 0, 2, 4)
    heads_far = low_added(heads_grads[2], core(sent))
    out_3 = core(out_3)
    low_rows, dnorma, own, far, far_1, heads_far, out_3 = tie(
        low_rows, dnorma, own, far, far_1, heads_far, out_3
    )
    dnorma = back(1, low_rows, dnorma)

    own = added(own[:1], over_dp(own[1:], 2))
    far_0 = part_way(far, 0, 0, 2)
    low_rows, dnorma, own, far_0, far_1, heads_far, sent, out_1 = tie(
        low_rows, dnorma, own, far_0, far_1, heads_far, heads_grads[1], outs[1]
    )
    dnorma = back(0, low_rows, dnorma)

    far = low_added(far_0, over_dp(far_1, 1))
    heads_far = halved(heads_far, 0, low).astype(BF16)
    heads_own = low_added(heads_grads[0], core(sent))
    out_1 = core(out_1)
    dnorma, far, heads_far, heads_own, out_1, out_2 = tie(
        dnorma, far, heads_far, heads_own, out_1, outs[2]
    )
    grad_0, grad_near, grad_far, tiles = input_back(
        dims,
        group,
        shards,
        meta,
        x,
        normed_1,
        rstd_1,
        dnorma,
        dsecond,
        small_params,
        window,
        sums_two,
        *heads_sums,
        *dbias,
    )
    far = low_added(far[:1], over_dp(far[1:], 2))
    heads_far = halved(heads_far, 1, low).astype(BF16)
    heads_own = halved(heads_own, 0, low).astype(BF16)
    out_2 = chip(out_2)
    grad_near, grad_far, tiles, far, heads_far, heads_own, out_2 = tie(
        grad_near, grad_far, tiles, far, heads_far, heads_own, out_2
    )

    heads_own = halved(heads_own, 1, low).astype(BF16)
    heads_far = halved(heads_far, 2, low).astype(BF16)
    far, grad_far = tie(chip(far), grad_far)
    grad_far = chip(grad_far)
    heads_got = over_dp(heads_own[1:], 2)
    heads_terms, hidden_terms = [heads_own[:1], heads_got, chip(heads_far)], [own, far]
    if low:
        heads_terms = [own_rows(sum(t[0].astype(F32) for t in heads_terms), low)]
        hidden_terms = [own_rows(sum(t[0].astype(F32) for t in hidden_terms), low)]
    count = group * shards
    both = ("dp", "mp")
    tiles = tiles.reshape(count, -1, LANES)
    tiles = lax.all_to_all(tiles, both, 0, 0, tiled=True)
    shard_heads, shard_hidden, message = sums_of(heads_terms, hidden_terms, tiles)
    out_0, message = tie(outs[0], message)
    block_out = join(meta, [out_0, out_1, out_2, out_3], BF16)
    grad_far = after(grad_far, block_out)
    every = lax.all_to_all(message, both, 0, 0, tiled=True)
    grad_pieces = [grad_0, core(grad_near), grad_far, core(grad_far[1])]
    patch_grad = join(meta, grad_pieces, F32)
    every, patch_grad = tie(every, patch_grad)
    qkv = [a.transpose(1, 0, 2) for a in (qkv_weight, qkv_mean, qkv_square)]
    grad_norm, *new = updated(
        group,
        every,
        shard_heads,
        shard_hidden,
        [
            *qkv,
            proj_weight,
            proj_mean,
            proj_square,
            expand_weight,
            expand_mean,
            expand_square,
            contract_weight,
            contract_mean,
            contract_square,
            small_params,
            small_mean,
            small_square,
        ],
    )
    return (
        block_out,
        patch_grad,
        grad_norm[0, 0],
        *[a.transpose(1, 0, 2) for a in new[:3]],
        *new[3:],
    )


def solution(mesh):
    cells = P("mp", "dp", None, None)
    heads = P("dp", None, "mp")
    matrix = P("dp", "mp")
    params = [heads] * 3 + [matrix] * 9 + [P()] * 3
    return jax.shard_map(
        on_device,
        mesh=mesh,
        in_specs=(cells, cells, P("dp", None), *params),
        out_specs=(cells, cells, P(), *params),
        check_vma=False,
    )
```

```python
import functools
import math

import jax
import jax.numpy as jnp
from jax import lax
from jax.experimental import pallas as pl
from jax.experimental.pallas import tpu as pltpu
from jax.sharding import PartitionSpec as P

D = 512
HD = 64
FF = 2048
STEP = 10


NORM_EPS = 1e-06
CLIP_NORM = 1.0
BETA_ONE = 0.9
BETA_TWO = 0.999
ADAM_EPS = 1e-08
WEIGHT_DECAY = 0.05
RATE_FACTOR = 2.0
SMALL_RATE = 0.5
ROOT_HALF = 0.7071067811865476
INV_ROOT_TAU = 0.3989422804014327
HEAD_SCALE = HD ** (-0.5)

LANES = 128
SUB = 8
F32 = jnp.float32
BF16 = jnp.bfloat16


def radius_of(head):
    return 1 if head < 2 else 2 if head < 5 else 3


def log2(size):
    bits = size.bit_length() - 1
    assert 1 << bits == size
    return bits


BLOCK = 64
NEAR_LAST = (2, 1, 0)
CORE, CHIP = 0, 1


def flip(array, axis, bit):
    size = lax.axis_size(axis)
    return lax.ppermute(array, axis, [(i, i ^ (1 << bit)) for i in range(size)])


def bit_of(axis, bit):
    return (lax.axis_index(axis) >> bit) & 1


def finer_bits(shard_rows):
    return log2(BLOCK // shard_rows) if shard_rows < BLOCK else 0


def after(array, *others):
    return lax.optimization_barrier((array, *others))[0]


def tie(*arrays):
    return lax.optimization_barrier(arrays)


def whole_block(shard):
    for bit in range(finer_bits(shard.shape[0])):
        other = flip(shard, "dp", bit)
        upper = bit_of("dp", bit) == 1
        shard = jnp.where(
            upper,
            jnp.concatenate([other, shard], axis=0),
            jnp.concatenate([shard, other], axis=0),
        )
    return shard[None]


def doubled(blocks, bit, low, *before):
    other = flip(blocks, "dp", bit + low)
    return jnp.concatenate([blocks, after(other, *before) if before else other], axis=0)


def dp_masks(order):
    masks = [0]
    for bit in order:
        masks += [m ^ (1 << bit) for m in masks]
    return masks


def added(mine, got):
    return mine.astype(F32) + got.astype(F32)


def low_added(mine, got):
    return added(mine, got).astype(BF16)


def halved(blocks, bit, low, *before):
    half = blocks.shape[0] // 2
    other = flip(blocks[half:], "dp", bit + low)
    return added(blocks[:half], after(other, *before) if before else other)


def own_rows(total, low):
    for bit in reversed(range(low)):
        pair = total.astype(BF16).reshape(2, -1, total.shape[-1])
        mine = lax.dynamic_index_in_dim(pair, bit_of("dp", bit), 0, keepdims=False)
        theirs = lax.dynamic_index_in_dim(pair, 1 - bit_of("dp", bit), 0, keepdims=False)
        total = added(mine, flip(theirs, "dp", bit))
    return total


def dot(a, b):
    return lax.dot_general(a, b, (((1,), (0,)), ((), ())), preferred_element_type=F32)


def dot_rt(a, b):
    return lax.dot_general(a, b, (((1,), (1,)), ((), ())), preferred_element_type=F32)


def dot_lt(a, b):
    return lax.dot_general(a, b, (((0,), (0,)), ((), ())), preferred_element_type=F32)


def row_mean(values):
    return jnp.sum(values, axis=-1, keepdims=True) * (1.0 / values.shape[-1])


def norm_parts(values):
    center = values - row_mean(values)
    rstd = lax.rsqrt(row_mean(center * center) + NORM_EPS)
    return center * rstd, rstd


def norm_back(gradient, normed, rstd, gain_row):
    scaled = gradient * gain_row
    return rstd * (scaled - row_mean(scaled) - normed * row_mean(scaled * normed))


def shifted_rows(src, lead, rows, start, lanes=slice(None)):
    return [src[lead, y, pl.ds(start, SUB), lanes] for y in range(rows)]


def filtered(src, lead, rows, col, taps, radius, sign, lanes=slice(None)):
    acc = [None] * rows
    for dx in range(-radius, radius + 1):
        cells = shifted_rows(src, lead, rows, col + SUB + sign * dx, lanes)
        for dy in range(-radius, radius + 1):
            tap = taps(dy, dx)
            for y in range(rows):
                from_row = y + sign * dy
                if 0 <= from_row < rows:
                    term = tap * cells[from_row]
                    acc[y] = term if acc[y] is None else acc[y] + term
    return acc


def tap_products(src, own, images, rows, cols, dx, radius, lanes=slice(None)):
    def image(lead, acc):
        acc = list(acc)
        for col in range(0, cols, SUB):
            cells = shifted_rows(src, lead, rows, col + SUB - dx, lanes)
            mine = [own(lead, y, col) for y in range(rows)]
            for k, dy in enumerate(range(-radius, radius + 1)):
                total = acc[k]
                for y in range(rows):
                    if 0 <= y - dy < rows:
                        total = total + mine[y] * cells[y - dy]
                acc[k] = total
        return tuple(acc)

    zero = jnp.zeros((SUB, LANES), F32)
    return lax.fori_loop(0, images, image, (zero,) * (2 * radius + 1))


def each(count, body):
    for i in range(count):
        body(i)


def loop(count, body, unroll=1):
    def step(i, carry):
        body(i)
        return carry

    lax.fori_loop(0, count, step, 0, unroll=unroll)


def slot_of(mask, order):
    return sum(((mask >> bit) & 1) << k for k, bit in enumerate(order))


def fetch(blocks, order, target, dp_block, stride=1, offset=0):
    for slot, mask in enumerate(dp_masks(order)):
        row = pl.multiple_of((dp_block ^ mask) * BLOCK, BLOCK)
        target[pl.ds(row, BLOCK), :] = blocks[slot * stride + offset]


def hand_out(blocks, order, values, columns, dp_block):
    for block in range(values.shape[0] // BLOCK):
        slot = slot_of(dp_block ^ block, order)
        blocks[slot, :, columns] = values[block * BLOCK : (block + 1) * BLOCK].astype(BF16)


def place_of(meta_ref):
    return meta_ref[0]


def height(meta_ref, lead):
    return meta_ref[2 + 2 * lead]


def width(meta_ref, lead):
    return meta_ref[3 + 2 * lead]


def col_keep(meta_ref, lead, cols, lanes):
    return lax.broadcasted_iota(jnp.int32, (cols, lanes), 0) < width(meta_ref, lead)


def cell_keep(meta_ref, lead, rows, cols, lanes):
    x = lax.broadcasted_iota(jnp.int32, (rows, cols, lanes), 1)
    y = lax.broadcasted_iota(jnp.int32, (rows, cols, lanes), 0)
    kept = (x < width(meta_ref, lead)) & (y < height(meta_ref, lead))
    return kept.reshape(rows * cols, lanes)


def head_diagonal():
    a = lax.broadcasted_iota(jnp.int32, (LANES, LANES), 0) // HD
    b = lax.broadcasted_iota(jnp.int32, (LANES, LANES), 1) // HD
    return a == b


def by_radius(step, radii, run):
    for radius in sorted(set(radii)):
        steps = [k for k, r in enumerate(radii) if r == radius]
        hit = functools.reduce(lambda a, b: a | b, [step == k for k in steps])
        pl.when(hit)(functools.partial(run, radius))


def enter_kernel(
    dims,
    local_rows,
    meta_ref,
    *refs,
):
    images, rows, cols, channels = dims
    cells = rows * cols
    group = rows // local_rows
    core = place_of(meta_ref) & 1
    firsts = (place_of(meta_ref) * images, 0, core * images, 0)
    pieces = refs[:group]
    small_ref, x_ref, first_ref, norma_ref, normed_ref, rstd_ref, pad_x = refs[group:]
    place = meta_ref[0]
    zeros = jnp.zeros((images, rows, SUB, channels), F32)
    pad_x[:, :, :SUB, :] = zeros
    pad_x[:, :, SUB + cols :, :] = zeros

    for k, (piece, first_image) in enumerate(zip(pieces, firsts)):

        def mask_row(r, k=k, piece=piece, first_image=first_image):
            lead = r // local_rows
            y_here = r % local_rows
            y = (place ^ k) * local_rows + y_here
            kept = col_keep(meta_ref, lead, cols, channels) & (y < height(meta_ref, lead))
            block = jnp.where(kept, piece[y_here, first_image + lead], 0)
            at = pl.ds(pl.multiple_of((lead * rows + y) * cols, cols), cols)
            x_ref[at, :] = block
            pad_x[lead, y, pl.ds(SUB, cols), :] = block.astype(F32)

        loop(images * local_rows, mask_row, 2)

    def conv(lead):
        for lane in range(0, channels, LANES):
            lanes = pl.ds(lane, LANES)
            for col in range(0, cols, SUB):
                out = filtered(
                    pad_x,
                    lead,
                    rows,
                    col,
                    lambda dy, dx: small_ref[pl.ds(3 * (dy + 1) + dx + 1, 1), lanes],
                    1,
                    1,
                    lanes,
                )
                bias = small_ref[pl.ds(58, 1), lanes]
                for y in range(rows):
                    own = pad_x[lead, y, pl.ds(SUB + col, SUB), lanes]
                    at = pl.multiple_of(lead * cells + (y * cols + col), SUB)
                    first_ref[pl.ds(at, SUB), lanes] = own + out[y] + bias

    loop(images, conv)

    def normalize(r):
        at = pl.ds(pl.multiple_of(r * cols, cols), cols)
        normed, rstd = norm_parts(first_ref[at, :])
        normed_ref[at, :] = normed
        rstd_ref[at, :] = jnp.broadcast_to(rstd, (cols, LANES))
        norma_ref[at, :] = (
            normed * small_ref[pl.ds(59, 1), :] + small_ref[pl.ds(60, 1), :]
        ).astype(BF16)

    loop(images * rows, normalize, 8)


def attention_kernel(
    dims,
    radii,
    mask,
    final,
    meta_ref,
    norma_ref,
    part_ref,
    blocks_ref,
    *refs,
):
    images, rows, cols, channels = dims
    cells = rows * cols
    if mask:
        before_ref, *refs = refs
    if final:
        first_ref, small_ref, *refs = refs
    query_ref, probs_ref, value_ref, near_ref, attended_ref, kv_ref, *refs = refs
    if final:
        second_ref, normb_ref, normed_ref, rstd_ref, total, *refs = refs
    else:
        total, *refs = refs
    weight, pad_v, near_f = refs

    fetch(blocks_ref, NEAR_LAST, weight, meta_ref[1])
    pad_v[...] = jnp.zeros_like(pad_v)
    diagonal = head_diagonal()
    block = mask ^ meta_ref[0]

    def project(lead):
        at = pl.ds(lead * cells, cells)
        proj = dot(norma_ref[at, :], weight[:, : 3 * LANES])
        query = (proj[:, :LANES] + part_ref[block, pl.ds(61, 1), :]).astype(BF16)
        value = (proj[:, 2 * LANES :] + part_ref[block, pl.ds(62, 1), :]).astype(BF16)
        kept = cell_keep(meta_ref, lead, rows, cols, LANES)
        key = jnp.where(kept, proj[:, LANES : 2 * LANES], -1e30)
        expo = jnp.exp(key - jnp.max(key, axis=0, keepdims=True))
        probs = (expo / jnp.sum(expo, axis=0, keepdims=True)).astype(BF16)
        query_ref[at, :] = query
        probs_ref[at, :] = probs
        value_ref[at, :] = value
        kv = jnp.where(diagonal, dot_lt(probs, value), 0.0).astype(BF16)
        kv_ref[lead] = kv
        masked = jnp.where(kept, value.astype(F32), 0.0)
        pad_v[lead, :, pl.ds(SUB, cols), :] = masked.reshape(rows, cols, LANES)

    each(images, project)

    def conv_near(radius):
        def conv(lead):
            for col in range(0, cols, SUB):
                out = filtered(
                    pad_v,
                    lead,
                    rows,
                    col,
                    lambda dy, dx: part_ref[block, pl.ds(9 + 7 * (dy + 3) + dx + 3, 1), :],
                    radius,
                    1,
                )
                bias = part_ref[block, pl.ds(63, 1), :]
                for y in range(rows):
                    at = pl.multiple_of(lead * cells + (y * cols + col), SUB)
                    near_f[pl.ds(at, SUB), :] = out[y] + bias

        loop(images, conv)

    by_radius(block, radii, conv_near)

    def attend(lead):
        at = pl.ds(lead * cells, cells)
        query = query_ref[at, :]
        near = near_f[at, :]
        near_ref[at, :] = near.astype(BF16)
        factored = dot(query, kv_ref[lead]) * HEAD_SCALE
        attended = (factored + query.astype(F32) * near).astype(BF16)
        attended_ref[at, :] = attended
        out = dot_rt(attended, weight[:, 3 * LANES :])

        total[at, :] = out + before_ref[at, :] if mask else out

    each(images, attend)
    if not final:
        return

    def finish(r):
        at = pl.ds(pl.multiple_of(r * cols, cols), cols)
        second = first_ref[at, :] + total[at, :] + small_ref[pl.ds(64, 1), :]
        second_ref[at, :] = second
        normed, rstd = norm_parts(second)
        normed_ref[at, :] = normed
        rstd_ref[at, :] = jnp.broadcast_to(rstd, (cols, LANES))
        normb_ref[at, :] = (
            normed * small_ref[pl.ds(65, 1), :] + small_ref[pl.ds(66, 1), :]
        ).astype(BF16)

    loop(images * rows, finish, 8)


def gelu_parts(pre):
    cdf = 0.5 * (1.0 + lax.erf(pre * ROOT_HALF))
    return pre * cdf, cdf + pre * (jnp.exp(-0.5 * pre * pre) * INV_ROOT_TAU)


def hidden_kernel(
    dims,
    local_rows,
    mask,
    final,
    meta_ref,
    normb_ref,
    bias_ref,
    blocks_1,
    blocks_2,
    *refs,
):
    images, rows, cols, channels = dims
    cells = rows * cols
    group = rows // local_rows
    if mask:
        dout, total_in, dnorm_in, *refs = refs
    else:
        pieces, refs = refs[:group], refs[group:]
    if final:
        second_ref, normed_ref, rstd_ref, small_ref, *refs = refs
    d_ref, dbias_ref, *refs = refs
    if final:
        outs, refs = refs[:group], refs[group:]
        dsecond_ref, low_ref, sums_ref, total, dnorm, *refs = refs
    else:
        if not mask:
            dout, *refs = refs
        total, dnorm, *refs = refs
    w1, w2, pre, act_grad, hact, dhpre = refs
    hidden = w1.shape[1]
    place, dp_block = meta_ref[0], meta_ref[1]

    fetch(blocks_1, NEAR_LAST, w1, dp_block)
    fetch(blocks_2, NEAR_LAST, w2, dp_block, 2, mask // 2)
    if not mask:
        firsts = (0, 0, (place & 1) * images, 0)
        for k, (piece, first_image) in enumerate(zip(pieces, firsts)):

            def mask_row(r, k=k, piece=piece, first_image=first_image):
                lead = r // local_rows
                y_here = r % local_rows
                y = (place ^ k) * local_rows + y_here
                kept = col_keep(meta_ref, lead, cols, channels) & (y < height(meta_ref, lead))
                at = pl.ds(pl.multiple_of((lead * rows + y) * cols, cols), cols)
                block = piece[y_here, first_image + lead].astype(F32)
                dout[at, :] = jnp.where(kept, block, 0.0).astype(BF16)

            loop(images * local_rows, mask_row, 2)

    dbias_ref[...] = jnp.zeros_like(dbias_ref)

    size = 256
    bias_acc = jnp.zeros((SUB, hidden), F32)
    for t in range(images * cells // size):
        at = pl.ds(t * size, size)
        pre_t = dot(normb_ref[at, :], w1[...]) + bias_ref[mask ^ place]
        act_t = dot(dout[at, :], w2[...])
        act, slope = gelu_parts(pre_t)
        hact_t = act.astype(BF16)
        back_t = (act_t * slope).astype(BF16)
        hact[at, :] = hact_t
        dhpre[at, :] = back_t
        bias_acc += jnp.sum(back_t.astype(F32).reshape(size // SUB, SUB, hidden), axis=0)
        out = dot_rt(hact_t, w2[...])
        back = dot_rt(back_t, w1[...])
        total[at, :] = out + total_in[at, :] if mask else out
        dnorm[at, :] = back + dnorm_in[at, :] if mask else back
    dbias_ref[...] = jnp.sum(bias_acc, axis=0, keepdims=True)
    dw1 = dot_lt(normb_ref[...], dhpre[...])
    hand_out(d_ref, NEAR_LAST, dw1, pl.ds(0, hidden), dp_block)
    dw2 = dot_lt(dout[...], hact[...])
    hand_out(d_ref, NEAR_LAST, dw2, pl.ds(hidden, hidden), dp_block)
    if final:
        gain = small_ref[pl.ds(65, 1), :]
        zero = jnp.zeros((SUB, channels), F32)
        acc = (zero,) * 4
        for k, out_ref in enumerate(outs):

            def finish(r, acc):
                lead = r // local_rows
                y_here = r % local_rows
                y = (place ^ k) * local_rows + y_here
                at = pl.ds(pl.multiple_of((lead * rows + y) * cols, cols), cols)
                second = second_ref[at, :]
                out = second + total[at, :] + small_ref[pl.ds(67, 1), :]
                out_ref[y_here, lead] = out.astype(BF16)
                normed = normed_ref[at, :]
                rstd = jnp.concatenate([rstd_ref[at, :]] * (channels // LANES), axis=1)
                back = dnorm[at, :]
                got = dout[at, :].astype(F32)
                dsecond = got + norm_back(back, normed, rstd, gain)
                dsecond_ref[at, :] = dsecond
                low = dsecond.astype(BF16)
                low_ref[at, :] = low
                terms = (low.astype(F32), back * normed, back, got)
                return tuple(
                    a + jnp.sum(t.reshape(cols // SUB, SUB, channels), axis=0)
                    for a, t in zip(acc, terms)
                )

            acc = lax.fori_loop(0, images * local_rows, finish, acc, unroll=4)
        sums_ref[...] = jnp.zeros_like(sums_ref)
        for k, a in enumerate(acc):
            sums_ref[pl.ds(k, 1), :] = jnp.sum(a, axis=0, keepdims=True)


def attention_back_kernel(
    dims,
    radii,
    mask,
    summed,
    meta_ref,
    low,
    norma_ref,
    part_ref,
    blocks_ref,
    query_ref,
    probs_ref,
    value_ref,
    near_ref,
    attended_ref,
    kv_ref,
    *refs,
):
    images, rows, cols, channels = dims
    cells = rows * cols
    if summed:
        before_ref, *refs = refs
    dnorma_ref, d_ref, sums_ref, weight, pad_d, value_f, grads, dvalue_f = refs
    dp_block = meta_ref[1]

    fetch(blocks_ref, NEAR_LAST, weight, dp_block)
    pad_d[...] = jnp.zeros_like(pad_d)
    sums_ref[...] = jnp.zeros_like(sums_ref)
    diagonal = head_diagonal()
    block = mask ^ meta_ref[0]

    def first_half(lead):
        at = pl.ds(lead * cells, cells)
        datt = dot(low[at, :], weight[:, 3 * LANES :]).astype(BF16)
        query = query_ref[at, :]
        probs = probs_ref[at, :]
        value = value_ref[at, :]
        kept = cell_keep(meta_ref, lead, rows, cols, LANES)
        dkv = jnp.where(diagonal, dot_lt(query, datt) * HEAD_SCALE, 0.0).astype(BF16)
        datt_f = datt.astype(F32)
        dnear = datt_f * query.astype(F32)
        pad_d[lead, :, pl.ds(SUB, cols), :] = dnear.reshape(rows, cols, LANES)
        dquery = (
            dot_rt(datt, kv_ref[lead]) * HEAD_SCALE + datt_f * near_ref[at, :].astype(F32)
        ).astype(BF16)
        dprobs = dot_rt(value, dkv)
        probs_f = probs.astype(F32)
        inner = jnp.sum(probs_f * dprobs, axis=0, keepdims=True)
        dkey = (probs_f * (dprobs - inner)).astype(BF16)
        grads[at, :LANES] = dquery
        grads[at, LANES : 2 * LANES] = dkey
        dvalue_f[at, :] = dot(probs, dkv)
        value_f[at, :] = jnp.where(kept, value.astype(F32), 0.0)
        sums_ref[pl.ds(61, 1), :] += jnp.sum(dquery.astype(F32), axis=0, keepdims=True)
        sums_ref[pl.ds(63, 1), :] += jnp.sum(dnear, axis=0, keepdims=True)

    each(images, first_half)

    def conv_back(radius):
        def conv(lead):
            x = lax.broadcasted_iota(jnp.int32, (SUB, LANES), 0)
            for col in range(0, cols, SUB):
                out = filtered(
                    pad_d,
                    lead,
                    rows,
                    col,
                    lambda dy, dx: part_ref[block, pl.ds(9 + 7 * (dy + 3) + dx + 3, 1), :],
                    radius,
                    -1,
                )
                inside = (x + col) < width(meta_ref, lead)
                for y in range(rows):
                    at = pl.ds(pl.multiple_of(lead * cells + (y * cols + col), SUB), SUB)
                    kept = inside & (y < height(meta_ref, lead))
                    dvalue_f[at, :] = dvalue_f[at, :] + jnp.where(kept, out[y], 0.0)

        loop(images, conv)

        def own(lead, y, col):
            at = pl.multiple_of(lead * cells + (y * cols + col), SUB)
            return value_f[pl.ds(at, SUB), :]

        for dx in range(-radius, radius + 1):
            acc = tap_products(pad_d, own, images, rows, cols, dx, radius)
            for k, dy in enumerate(range(-radius, radius + 1)):
                sums_ref[pl.ds(9 + 7 * (dy + 3) + dx + 3, 1), :] = jnp.sum(
                    acc[k], axis=0, keepdims=True
                )

    by_radius(block, radii, conv_back)

    def second_half(lead):
        at = pl.ds(lead * cells, cells)
        dvalue = dvalue_f[at, :].astype(BF16)
        grads[at, 2 * LANES :] = dvalue
        sums_ref[pl.ds(62, 1), :] += jnp.sum(dvalue.astype(F32), axis=0, keepdims=True)
        back = dot_rt(grads[at, :], weight[:, : 3 * LANES])

        dnorma_ref[at, :] = back + before_ref[at, :] if summed else back

    each(images, second_half)
    wide = 3 * LANES
    dwq = dot_lt(norma_ref[...], grads[...])
    hand_out(d_ref, NEAR_LAST, dwq, pl.ds(0, wide), dp_block)
    dwp = dot_lt(low[...], attended_ref[...])
    hand_out(d_ref, NEAR_LAST, dwp, pl.ds(wide, LANES), dp_block)


def input_back_kernel(
    dims,
    local_rows,
    tile_rows,
    meta_ref,
    x_ref,
    normed_ref,
    rstd_ref,
    dnorma_ref,
    dsecond_ref,
    small_ref,
    window_ref,
    two_ref,
    *refs,
):
    images, rows, cols, channels = dims
    cells = rows * cols
    group = rows // local_rows
    heads_refs, dbias_refs, refs = refs[:group], refs[group : 2 * group], refs[2 * group :]
    outs, (tiles_ref, pad_d, x_f, sums) = refs[:group], refs[group:]
    place = meta_ref[0]
    zeros = jnp.zeros((images, rows, SUB, channels), F32)
    pad_d[:, :, :SUB, :] = zeros
    pad_d[:, :, SUB + cols :, :] = zeros
    gain = small_ref[pl.ds(59, 1), :]

    def norm(r, acc):
        lead = r // rows
        y = r % rows
        at = pl.ds(pl.multiple_of(r * cols, cols), cols)
        normed = normed_ref[at, :]
        rstd = jnp.concatenate([rstd_ref[at, :]] * (channels // LANES), axis=1)
        back = dnorma_ref[at, :]
        dfirst = dsecond_ref[at, :] + norm_back(back, normed, rstd, gain)
        pad_d[lead, y, pl.ds(SUB, cols), :] = dfirst
        x_f[at, :] = x_ref[at, :].astype(F32)
        terms = (dfirst, back * normed, back)
        return tuple(
            a + jnp.sum(t.reshape(cols // SUB, SUB, channels), axis=0)
            for a, t in zip(acc, terms)
        )

    zero = jnp.zeros((SUB, channels), F32)
    acc = lax.fori_loop(0, images * rows, norm, (zero,) * 3, unroll=8)
    for k, a in enumerate(acc):
        sums[pl.ds(58 + k, 1), :] = jnp.sum(a, axis=0, keepdims=True)

    def conv(lead):
        x = lax.broadcasted_iota(jnp.int32, (SUB, LANES), 0)
        for lane in range(0, channels, LANES):
            lanes = pl.ds(lane, LANES)
            for col in range(0, cols, SUB):
                out = filtered(
                    pad_d,
                    lead,
                    rows,
                    col,
                    lambda dy, dx: small_ref[pl.ds(3 * (dy + 1) + dx + 1, 1), lanes],
                    1,
                    -1,
                    lanes,
                )
                inside = (x + col) < width(meta_ref, lead)
                for y in range(rows):
                    own = pad_d[lead, y, pl.ds(SUB + col, SUB), lanes]
                    at = pl.multiple_of(lead * cells + (y * cols + col), SUB)
                    kept = inside & (y < height(meta_ref, lead))
                    x_f[pl.ds(at, SUB), lanes] = jnp.where(kept, own + out[y], 0.0)

    for lane in range(0, channels, LANES):
        lanes = pl.ds(lane, LANES)

        def own(lead, y, col):
            at = pl.multiple_of(lead * cells + (y * cols + col), SUB)
            return x_f[pl.ds(at, SUB), lanes]

        for dx in (-1, 0, 1):
            acc = tap_products(pad_d, own, images, rows, cols, dx, 1, lanes)
            for k, dy in enumerate((-1, 0, 1)):
                sums[pl.ds(3 * (dy + 1) + dx + 1, 1), lanes] = jnp.sum(
                    acc[k], axis=0, keepdims=True
                )
    loop(images, conv)
    for k, out_ref in enumerate(outs):

        def give(r):
            lead = r // local_rows
            y_here = r % local_rows
            y = (place ^ k) * local_rows + y_here
            at = pl.ds(pl.multiple_of((lead * rows + y) * cols, cols), cols)
            out_ref[y_here, lead] = x_f[at, :].astype(BF16)

        loop(images * local_rows, give, 2)

    for mask in range(group):
        heads_ref = heads_refs[mask]
        lanes = pl.ds(pl.multiple_of((place ^ mask) * LANES, LANES), LANES)
        sums[pl.ds(9, 49), lanes] = heads_ref[pl.ds(9, 49), :] * window_ref[:, lanes]
        sums[pl.ds(61, 3), lanes] = heads_ref[pl.ds(61, 3), :]
        sums[pl.ds(68 + (place ^ mask), 1), :] = dbias_refs[mask][...]
    sums[pl.ds(64, 4), :] = two_ref[pl.ds(0, 4), :]
    tiles_ref[...] = jnp.zeros_like(tiles_ref)
    for d in range(tiles_ref.shape[0]):
        here = min(tile_rows, sums.shape[0] - d * tile_rows)
        for j in range(tiles_ref.shape[1]):
            if here > 0:
                tiles_ref[d, j, pl.ds(0, here), :] = sums[
                    pl.ds(d * tile_rows, here), pl.ds(j * LANES, LANES)
                ]


def join_kernel(meta_ref, *refs):
    *pieces, out_ref = refs
    images = pieces[0].shape[1]
    for k, piece in enumerate(pieces):
        values = piece[0] if len(piece.shape) == 5 else piece[...]
        out_ref[:, pl.ds((meta_ref[0] ^ k) * images, images)] = values.astype(out_ref.dtype)


SCALARS = pl.BlockSpec(memory_space=pltpu.SMEM)
CLOSE = pl.BlockSpec(memory_space=pltpu.VMEM)
ENTER_MIB = 8
ATTENTION_MIB = 10
HIDDEN_MIB = 18
BACK_MIB = 10
INPUT_MIB = 10
JOIN_MIB = 4
FINAL_MIB = 8


def shape_of(shape, dtype):
    return jax.ShapeDtypeStruct(shape, dtype)


def call(kernel, name, us, mib, inputs, out_specs, out_shape, scratch):
    return pl.pallas_call(
        kernel,
        in_specs=[spec for _, spec in inputs],
        out_specs=out_specs,
        out_shape=out_shape,
        scratch_shapes=scratch,
        compiler_params=pltpu.CompilerParams(vmem_limit_bytes=mib * 2**20),
        cost_estimate=pl.CostEstimate(flops=us * 10**9, bytes_accessed=us * 2**20, transcendentals=0),
        name=name,
    )(*[array for array, _ in inputs])


def near_by(arrays):
    return [(a, CLOSE) for a in arrays]


def enter(dims, local_rows, meta, pieces, small):
    images, rows, cols, channels = dims
    flat = (images * rows * cols, channels)
    return call(
        functools.partial(enter_kernel, dims, local_rows),
        "enter",
        8,
        ENTER_MIB,
        [(meta, SCALARS), *near_by(pieces), (small, CLOSE)],
        [CLOSE] * 5,
        [
            shape_of(flat, BF16),
            shape_of(flat, F32),
            shape_of(flat, BF16),
            shape_of(flat, F32),
            shape_of((flat[0], LANES), F32),
        ],
        [pltpu.VMEM((images, rows, cols + 2 * SUB, channels), F32)],
    )


def attention(dims, radii, mask, meta, norma, parts, blocks, *more):
    images, rows, cols, channels = dims
    cells = images * rows * cols
    flat = (cells, channels)
    final = len(more) > 1
    kinds = ((cells, LANES),) * 5 + ((images, LANES, LANES),)
    sums = [shape_of(flat, F32)]
    if final:
        sums += [shape_of(flat, BF16), shape_of(flat, F32), shape_of((cells, LANES), F32)]
    return call(
        functools.partial(attention_kernel, dims, radii, mask, final),
        "attention",
        5,
        ATTENTION_MIB,
        [(meta, SCALARS), *near_by([norma, parts, blocks, *more])],
        [CLOSE] * (len(kinds) + len(sums)),
        [*[shape_of(k, BF16) for k in kinds], *sums],
        ([pltpu.VMEM(flat, F32)] if final else [])
        + [
            pltpu.VMEM((channels, 4 * LANES), BF16),
            pltpu.VMEM((images, rows, cols + 2 * SUB, LANES), F32),
            pltpu.VMEM((cells, LANES), F32),
        ],
    )


def hidden_part(dims, mask, final, meta, normb, bias, blocks_1, blocks_2, *more):
    images, rows, cols, channels = dims
    cells = images * rows * cols
    groups, _, hidden = bias.shape
    local_rows = rows // groups
    piece = (local_rows, images, cols, channels)
    flat = (cells, channels)
    if final:
        outs = [
            *[shape_of(piece, BF16) for _ in range(groups)],
            shape_of(flat, F32),
            shape_of(flat, BF16),
            shape_of((SUB, channels), F32),
        ]
    else:
        outs = [shape_of(flat, F32), shape_of(flat, F32)]
        outs = outs if mask else [shape_of(flat, BF16), *outs]
    return call(
        functools.partial(hidden_kernel, dims, local_rows, mask, final),
        "hidden",
        8,
        HIDDEN_MIB,
        [(meta, SCALARS), *near_by([normb, bias, blocks_1, blocks_2, *more])],
        [CLOSE] * (2 + len(outs)),
        [
            shape_of((*blocks_1.shape[:2], 2 * hidden), BF16),
            shape_of((1, hidden), F32),
            *outs,
        ],
        ([pltpu.VMEM(flat, F32)] * 2 if final else [])
        + [
            pltpu.VMEM((channels, hidden), BF16),
            pltpu.VMEM((channels, hidden), BF16),
            pltpu.VMEM((rows * cols, hidden), F32),
            pltpu.VMEM((rows * cols, hidden), F32),
            pltpu.VMEM((cells, hidden), BF16),
            pltpu.VMEM((cells, hidden), BF16),
        ],
    )


def attention_back(dims, radii, mask, meta, low, norma, parts, blocks, saved, *before):
    images, rows, cols, channels = dims
    cells = images * rows * cols
    flat = (cells, channels)
    return call(
        functools.partial(attention_back_kernel, dims, radii, mask, len(before)),
        "attention_back",
        7,
        BACK_MIB,
        [(meta, SCALARS), *near_by([low, norma, parts, blocks, *saved, *before])],
        [CLOSE] * 3,
        [
            shape_of(flat, F32),
            shape_of(blocks.shape, BF16),
            shape_of((72, LANES), F32),
        ],
        [
            pltpu.VMEM((channels, 4 * LANES), BF16),
            pltpu.VMEM((images, rows, cols + 2 * SUB, LANES), F32),
            pltpu.VMEM((cells, LANES), F32),
            pltpu.VMEM((cells, 3 * LANES), BF16),
            pltpu.VMEM((cells, LANES), F32),
        ],
    )


def input_back(dims, groups, shards, meta, *args):
    images, rows, cols, channels = dims
    flat = (images * rows * cols, channels)
    piece = (rows // groups, images, cols, channels)
    tile_rows = -(-72 // shards)
    tiles = (shards, groups, tile_rows, LANES)
    return call(
        functools.partial(input_back_kernel, dims, rows // groups, tile_rows),
        "input_back",
        10,
        INPUT_MIB,
        [(meta, SCALARS), *near_by(args)],
        [CLOSE] * (groups + 1),
        [*[shape_of(piece, BF16) for _ in range(groups)], shape_of(tiles, F32)],
        [
            pltpu.VMEM((images, rows, cols + 2 * SUB, channels), F32),
            pltpu.VMEM(flat, F32),
            pltpu.VMEM((72, channels), F32),
        ],
    )


def join(meta, pieces, dtype):
    local_rows, images, cols, channels = pieces[0].shape
    return call(
        join_kernel,
        "join",
        2,
        JOIN_MIB,
        [(meta, SCALARS), *near_by(pieces)],
        CLOSE,
        shape_of((local_rows, images * len(pieces), cols, channels), dtype),
        [],
    )


def sums_kernel(counts, *refs):
    heads, hidden = refs[: counts[0]], refs[counts[0] : sum(counts)]
    tiles_ref, heads_ref, hidden_ref, message_ref = refs[sum(counts) :]
    squares = jnp.zeros((1, LANES), F32)
    for terms, out_ref in ((heads, heads_ref), (hidden, hidden_ref)):
        total = sum(term[...].astype(F32).reshape(out_ref.shape) for term in terms)
        out_ref[...] = total
        columns = jnp.sum(total * total, axis=0, keepdims=True)
        for lane in range(0, columns.shape[1], LANES):
            squares += columns[:, lane : lane + LANES]
    small = jnp.sum(tiles_ref[...], axis=0)
    squares += jnp.sum(small * small, axis=0, keepdims=True)
    rows = small.shape[0]
    for k in range(message_ref.shape[0]):
        message_ref[k, pl.ds(0, rows), :] = small
        message_ref[k, pl.ds(rows, 1), :] = squares


def sums_of(heads, hidden, tiles):
    shard_rows = heads[0].shape[-2]
    count, rows, _ = tiles.shape
    return call(
        functools.partial(sums_kernel, (len(heads), len(hidden))),
        "sums",
        2,
        FINAL_MIB,
        near_by([*heads, *hidden, tiles]),
        [CLOSE] * 3,
        [
            shape_of((shard_rows, heads[0].shape[-1]), F32),
            shape_of((shard_rows, hidden[0].shape[-1]), F32),
            shape_of((count, rows + 1, LANES), F32),
        ],
        [],
    )


RATE_MODEL = RATE_FACTOR * D ** (-0.5)
RATE_HIDDEN = RATE_FACTOR * FF ** (-0.5)


def adamw(weight, mean, square, gradient, factor, rate, decay):
    clipped = gradient * factor
    mean_new = BETA_ONE * mean + (1.0 - BETA_ONE) * clipped
    square_new = BETA_TWO * square + (1.0 - BETA_TWO) * clipped * clipped
    mean_hat = mean_new / (1.0 - BETA_ONE**STEP)
    square_hat = square_new / (1.0 - BETA_TWO**STEP)
    weight_new = weight - rate * (mean_hat / (jnp.sqrt(square_hat) + ADAM_EPS) + decay * weight)
    return (weight_new, mean_new, square_new)


def update_kernel(groups, every_ref, heads_ref, hidden_ref, *refs):
    ins, outs, (grads,) = refs[:15], refs[15:31], refs[31:]
    count, rows, _ = every_ref.shape
    rows -= 1
    squares = jnp.sum(every_ref[:, pl.ds(rows, 1), :], axis=0)
    norm = jnp.sqrt(jnp.sum(squares, axis=1, keepdims=True))
    factor = jnp.minimum(1.0, CLIP_NORM / (norm + 1e-06))
    outs[0][...] = norm
    for k in range(count):
        first, lane = k // groups * rows, k % groups * LANES
        here = min(rows, grads.shape[0] - first)
        if here > 0:
            grads[pl.ds(first, here), pl.ds(lane, LANES)] = every_ref[k, pl.ds(0, here), :]
    hidden = hidden_ref.shape[1] // 2
    for k in range(3):
        gradient = heads_ref[:, k * LANES : (k + 1) * LANES]
        new = adamw(
            ins[0][k], ins[1][k], ins[2][k], gradient, factor, RATE_MODEL, WEIGHT_DECAY
        )
        for out, value in zip(outs[1:4], new):
            out[k] = value
    for n, gradient, rate, decay in (
        (1, heads_ref[:, 3 * LANES :], RATE_MODEL, WEIGHT_DECAY),
        (2, hidden_ref[:, :hidden], RATE_MODEL, WEIGHT_DECAY),
        (3, hidden_ref[:, hidden:], RATE_HIDDEN, WEIGHT_DECAY),
        (4, grads[...], SMALL_RATE, 0.0),
    ):
        weight, mean, square = (r[...] for r in ins[3 * n : 3 * n + 3])
        new = adamw(weight, mean, square, gradient, factor, rate, decay)
        for out, value in zip(outs[1 + 3 * n : 4 + 3 * n], new):
            out[...] = value


def updated(groups, every, heads, hidden, state):
    return call(
        functools.partial(update_kernel, groups),
        "update",
        3,
        FINAL_MIB,
        near_by([every, heads, hidden, *state]),
        [CLOSE] * 16,
        [shape_of((1, 1), F32), *[shape_of(a.shape, F32) for a in state]],
        [pltpu.VMEM(state[-1].shape, F32)],
    )


def window_rows(channels):
    radius = jnp.repeat(jnp.array([radius_of(h) for h in range(channels // HD)], jnp.int32), HD)
    tap_list = jnp.arange(49, dtype=jnp.int32)
    tap_row = jnp.abs(tap_list // 7 - 3)
    tap_col = jnp.abs(tap_list % 7 - 3)
    inside = (tap_row[:, None] <= radius[None, :]) & (tap_col[:, None] <= radius[None, :])
    return inside.astype(F32)


def on_device(
    patches,
    cotangent,
    grid_shape,
    qkv_weight,
    qkv_mean,
    qkv_square,
    proj_weight,
    proj_mean,
    proj_square,
    expand_weight,
    expand_mean,
    expand_square,
    contract_weight,
    contract_mean,
    contract_square,
    small_params,
    small_mean,
    small_square,
):
    group = lax.axis_size("mp")
    shards = lax.axis_size("dp")
    place = lax.axis_index("mp")
    local_rows, image_count, cols, channels = patches.shape
    images = image_count // group
    rows = local_rows * group
    dims = (images, rows, cols, channels)
    shard_rows = qkv_weight.shape[0]
    head_width = qkv_weight.shape[2]
    hidden = expand_weight.shape[1]
    assert head_width == LANES
    per_block = head_width // HD
    radii = [
        max(radius_of(per_block * g + h) for h in range(per_block)) for g in range(group)
    ]
    grids = lax.dynamic_slice_in_dim(grid_shape, place * images, images, 0)
    dp_block = lax.axis_index("dp") >> finer_bits(shard_rows)
    meta = jnp.concatenate([jnp.stack([place, dp_block]).astype(jnp.int32), grids.reshape(-1)])

    def core(array):
        return flip(array, "mp", CORE)

    def chip(array):
        return flip(array, "mp", CHIP)

    def over_dp(array, bit):
        return flip(array, "dp", bit + low)

    def diagonal(array):
        return lax.ppermute(array, "mp", [(i, i ^ 3) for i in range(group)])

    def joined(*arrays):
        return jnp.concatenate(arrays, axis=0)

    def some_images(array, first, count):
        return lax.dynamic_slice_in_dim(array, first, count, 1).astype(BF16)

    def image_parts(array):
        near = some_images(array, (place ^ 1) * images, images)
        far = some_images(array, ((place ^ 2) & ~1) * images, 2 * images)
        return near, far

    def for_other_core(far):
        return some_images(far, ((place & 1) ^ 1) * images, images)

    low = finer_bits(shard_rows)

    heads_shard = jnp.concatenate(
        [qkv_weight.astype(BF16).reshape(shard_rows, -1), proj_weight.astype(BF16)], axis=1
    )
    one_shard = expand_weight.astype(BF16)
    two_shard = contract_weight.astype(BF16)

    heads, one, two = whole_block(heads_shard), whole_block(one_shard), whole_block(two_shard)
    patch_near, patch_far = image_parts(patches)
    two = joined(two, chip(two))
    heads = joined(heads, over_dp(heads, 2))
    two, patch_far, patch_near = tie(two, patch_far, patch_near)
    patch_far = chip(patch_far)
    patch_near = core(patch_near)

    heads, one = tie(heads, one)
    heads = joined(heads, over_dp(heads, 1))
    one_got = over_dp(one, 2)

    patch_far, cotangent = tie(patch_far, cotangent)
    patch_relayed = core(for_other_core(patch_far))
    cot_near, cot_far = image_parts(cotangent)
    cot_own = some_images(cotangent, place * images, images)

    window = window_rows(channels)
    parts = small_params.at[9:58].multiply(window).reshape(72, group, LANES).transpose(1, 0, 2)
    unit_bias = small_params[68:].reshape(group, 1, hidden)

    patch_pieces = [patches, patch_near, patch_far, patch_relayed]
    x, first, norma, normed_1, rstd_1 = enter(dims, local_rows, meta, patch_pieces, small_params)
    heads_got, two_got = over_dp(heads, 0), over_dp(two, 2)
    norma, heads_got, one_got, two_got = tie(norma, heads_got, one_got, two_got)
    heads = joined(heads, heads_got)
    one = joined(one, one_got)
    two = joined(two, two_got)
    saved, weights = [None] * group, [heads] + [None] * (group - 1)

    *saved[0], attn = attention(dims, radii, 0, meta, norma, parts, heads)
    weights[1] = after(core(heads), attn)
    one = joined(one, after(over_dp(one, 1), attn))
    heads_chip = chip(heads)
    cot_far = after(chip(cot_far), attn)
    cot_pieces = [cot_own, core(cot_near), cot_far, core(for_other_core(cot_far))]
    *saved[1], attn = attention(dims, radii, 1, meta, norma, parts, weights[1], attn)
    weights[2] = after(heads_chip, attn)
    one = joined(one, after(over_dp(one, 0), attn))
    two = doubled(two, 1, low, attn)
    *saved[2], attn = attention(dims, radii, 2, meta, norma, parts, weights[2], attn)
    weights[3] = after(flip(weights[2], "mp", CORE), attn)
    *saved[3], second, normb, normed_2, rstd_2 = attention(
        dims, radii, 3, meta, norma, parts, weights[3], attn, first, small_params
    )
    two = doubled(two, 0, low, normb)

    grads, dbias = [None] * group, [None] * group
    grads[0], dbias[0], dout, total, dnorm = hidden_part(
        dims, 0, False, meta, normb, unit_bias, one, two, *cot_pieces
    )
    one_near, two_near = after(flip(one, "mp", CORE), dnorm), after(flip(two, "mp", CORE), dnorm)
    one_chip = flip(one, "mp", CHIP)
    grads[1], dbias[1], total, dnorm = hidden_part(
        dims, 1, False, meta, normb, unit_bias, one_near, two_near, dout, total, dnorm
    )
    one_chip = after(one_chip, dnorm)
    grads[2], dbias[2], total, dnorm = hidden_part(
        dims, 2, False, meta, normb, unit_bias, one_chip, two, dout, total, dnorm
    )
    one_chip = after(flip(one_chip, "mp", CORE), dnorm)
    own = low_added(grads[0], flip(grads[1], "mp", CORE))
    dnorm, own = tie(dnorm, own)
    grads[3], dbias[3], *outs, dsecond, dsecond_low, sums_two = hidden_part(
        dims,
        3,
        True,
        meta,
        normb,
        unit_bias,
        one_chip,
        two_near,
        dout,
        total,
        dnorm,
        second,
        normed_2,
        rstd_2,
        small_params,
    )

    heads_grads, heads_sums = [None] * group, [None] * group

    def back(mask, low_rows, *before):
        dnorma, heads_grads[mask], heads_sums[mask] = attention_back(
            dims, radii, mask, meta, low_rows, norma, parts, weights[mask], saved[mask], *before
        )
        return dnorma

    def part_way(blocks, bit, first, last):
        half = blocks.shape[0] // 2
        other = flip(blocks[half + first : half + last], "dp", bit + low)
        return low_added(blocks[first:last], other)

    own_1 = part_way(own, 0, 2, 4)
    low_rows, own, own_1, sent, out_3 = tie(dsecond_low, own, own_1, grads[3], outs[3])
    dnorma = back(3, low_rows)

    own_0 = part_way(own, 0, 0, 2)
    far = low_added(grads[2], flip(sent, "mp", CORE))
    out_3 = diagonal(out_3)
    low_rows, dnorma, own_0, own_1, far, out_3, sent = tie(
        low_rows, dnorma, own_0, own_1, far, out_3, heads_grads[3]
    )
    dnorma = back(2, low_rows, dnorma)

    own = low_added(own_0, over_dp(own_1, 1))
    far_1 = part_way(far, 0, 2, 4)
    heads_far = low_added(heads_grads[2], core(sent))
    low_rows, dnorma, own, far, far_1, heads_far, out_3 = tie(
        low_rows, dnorma, own, far, far_1, heads_far, out_3
    )
    dnorma = back(1, low_rows, dnorma)

    own = added(own[:1], over_dp(own[1:], 2))
    far_0 = part_way(far, 0, 0, 2)
    low_rows, dnorma, own, far_0, far_1, heads_far, sent, out_1 = tie(
        low_rows, dnorma, own, far_0, far_1, heads_far, heads_grads[1], outs[1]
    )
    dnorma = back(0, low_rows, dnorma)

    far = low_added(far_0, over_dp(far_1, 1))
    heads_far = halved(heads_far, 0, low).astype(BF16)
    heads_own = low_added(heads_grads[0], core(sent))
    out_1 = core(out_1)
    dnorma, far, heads_far, heads_own, out_1, out_2 = tie(
        dnorma, far, heads_far, heads_own, out_1, outs[2]
    )
    grad_0, grad_1, grad_2, grad_3, tiles = input_back(
        dims,
        group,
        shards,
        meta,
        x,
        normed_1,
        rstd_1,
        dnorma,
        dsecond,
        small_params,
        window,
        sums_two,
        *heads_sums,
        *dbias,
    )
    far = low_added(far[:1], over_dp(far[1:], 2))
    heads_far = halved(heads_far, 1, low).astype(BF16)
    heads_own = halved(heads_own, 0, low).astype(BF16)
    out_2 = chip(out_2)
    grad_1, grad_2, grad_3, tiles, far, heads_far, heads_own, out_2 = tie(
        grad_1, grad_2, grad_3, tiles, far, heads_far, heads_own, out_2
    )

    heads_own = halved(heads_own, 1, low).astype(BF16)
    heads_far = halved(heads_far, 2, low).astype(BF16)
    far, grad_2, grad_3 = tie(chip(far), grad_2, grad_3)
    grad_2, grad_3 = chip(grad_2), diagonal(grad_3)
    block_out = join(meta, [outs[0], out_1, out_2, out_3], BF16)
    heads_got = over_dp(heads_own[1:], 2)
    heads_terms, hidden_terms = [heads_own[:1], heads_got, chip(heads_far)], [own, far]
    if low:
        heads_terms = [own_rows(sum(t[0].astype(F32) for t in heads_terms), low)]
        hidden_terms = [own_rows(sum(t[0].astype(F32) for t in hidden_terms), low)]
    count = group * shards
    both = ("dp", "mp")
    tiles = tiles.reshape(count, -1, LANES)
    tiles = lax.all_to_all(tiles, both, 0, 0, tiled=True)
    shard_heads, shard_hidden, message = sums_of(heads_terms, hidden_terms, tiles)
    every = lax.all_to_all(message, both, 0, 0, tiled=True)
    patch_grad = join(meta, [grad_0, core(grad_1), grad_2, grad_3], F32)
    every, patch_grad = tie(every, patch_grad)
    qkv = [a.transpose(1, 0, 2) for a in (qkv_weight, qkv_mean, qkv_square)]
    grad_norm, *new = updated(
        group,
        every,
        shard_heads,
        shard_hidden,
        [
            *qkv,
            proj_weight,
            proj_mean,
            proj_square,
            expand_weight,
            expand_mean,
            expand_square,
            contract_weight,
            contract_mean,
            contract_square,
            small_params,
            small_mean,
            small_square,
        ],
    )
    return (
        block_out,
        patch_grad,
        grad_norm[0, 0],
        *[a.transpose(1, 0, 2) for a in new[:3]],
        *new[3:],
    )


def solution(mesh):
    cells = P("mp", "dp", None, None)
    heads = P("dp", None, "mp")
    matrix = P("dp", "mp")
    params = [heads] * 3 + [matrix] * 9 + [P()] * 3
    return jax.shard_map(
        on_device,
        mesh=mesh,
        in_specs=(cells, cells, P("dp", None), *params),
        out_specs=(cells, cells, P(), *params),
        check_vma=False,
    )
```
